32 devices in a mesh: genome: 8 (over z, y), tower: 4 (over x, core).
Axes of the slice: x: 2, y: 2, z: 4, core: 2. Of those that a mesh axis runs over, the one named last changes fastest.
Arguments:
- genome_bases: int32 [1048576], P('genome'), may hold values from 0 to 3
- stitch_weight: int32 [256], replicated, may hold values from 1 to 8
- stem_weight: bfloat16 [96, 8192], replicated, may hold values from -0.125 to 0.125
- trunk_in: bfloat16 [6, 48, 288], replicated, may hold values from -0.375 to 0.375
- trunk_out: bfloat16 [6, 96, 48], replicated, may hold values from -0.875 to 0.875
- pair_weight: bfloat16 [96, 96], replicated, may hold values from -0.625 to 0.625
- distance_rate: float32 [48], replicated, may hold values from 0.05 to 0.3
- tower_conv: bfloat16 [2, 3, 48, 144], replicated, may hold values from -0.3125 to 0.3125
- tower_mix: bfloat16 [2, 48, 48], replicated, may hold values from -0.875 to 0.875
- head_weight: bfloat16 [5, 48], replicated, may hold values from -0.875 to 0.875
Outputs:
- stitched: float32 [5, 512, 256], P(None, ('genome', 'tower'))
- scores: float32 [2, 5, 512], P(None, None, ('genome', 'tower'))
The draws below stay inside these ranges and needn't reach their ends.
All inputs are finite; a program needn't handle non-finite values.
Results may differ from the reference program's by a relative error of at most 0.019.
Values may be sent and summed in bfloat16 or wider, within the bound.
No kernel may reach another device: no remote copies, remote signals or barrier semaphores. Data moves between devices by JAX's collectives and lax.ppermute only.
A program may use at most 64 MiB of HBM per device.

```python
import jax
import jax.numpy as jnp
from jax import lax

C1 = 96
MID = 48
C2 = 48
TARGETS = 5
BP = 2048
TRUNK = 6
TOWER = 2
STRIDE = 64
BINS = 256
BASES = 1048576
N_GENOME = 8


def touch_ends(array, own_key, least, largest):
    dims = array.shape
    place = [jax.random.randint(jax.random.fold_in(own_key, axis), (), 0, dims[axis]) for axis in range(len(dims))]
    array = array.at[tuple(place)].set(least)
    longest = dims.index(max(dims))
    place[longest] = (place[longest] + 1) % dims[longest]
    return array.at[tuple(place)].set(largest)


def centred(own_key, shape, spread, most, held_as=jnp.bfloat16):
    drawn = jax.random.normal(own_key, shape, jnp.float32) * spread
    return jnp.minimum(jnp.maximum(drawn, -most), most).astype(held_as)


def setup_inputs(seed: int = 0) -> dict:
    key_of = jax.random.split(jax.random.key(seed), 11)
    return {
        "genome_bases": touch_ends(jax.random.randint(key_of[0], (BASES,), 0, 4), jax.random.fold_in(key_of[0], 1), 0, 3).astype(jnp.int32),
        "stitch_weight": touch_ends(jax.random.randint(key_of[1], (BINS,), 1, 9), jax.random.fold_in(key_of[1], 1), 1, 8).astype(jnp.int32),
        "stem_weight": centred(key_of[2], (C1, 4 * BP), BP ** -0.5, 0.125),
        "trunk_in": centred(key_of[3], (TRUNK, MID, 3 * C1), (3 * C1) ** -0.5, 0.375),
        "trunk_out": centred(key_of[4], (TRUNK, C1, MID), MID ** -0.5, 0.875),
        "pair_weight": centred(key_of[5], (2 * C2, C1), C1 ** -0.5, 0.625),
        "distance_rate": jnp.clip(jax.random.uniform(key_of[6], (C2,), jnp.float32, 0.05, 0.3), 0.05, 0.3),
        "tower_conv": centred(key_of[7], (TOWER, 3, C2, 3 * C2), (9 * C2) ** -0.5, 0.3125),
        "tower_mix": centred(key_of[8], (TOWER, C2, C2), C2 ** -0.5, 0.875),
        "head_weight": centred(key_of[9], (TARGETS, C2), C2 ** -0.5, 0.875),
    }


def shift_cols(values, offset):
    extent = values.shape[-1]
    margins = [(0, 0)] * (values.ndim - 1)
    if offset >= 0:
        padded = jnp.pad(values, margins + [(0, offset)])
        return padded[..., offset:offset + extent]
    padded = jnp.pad(values, margins + [(-offset, 0)])
    return padded[..., :extent]


def stem_features(genome_bases, stem_weight):
    letters = genome_bases.reshape(-1, BP)
    onehot = (letters[:, :, None] == jnp.arange(4, dtype=jnp.int32)[None, None, :]).astype(jnp.bfloat16)
    onehot = onehot.reshape(letters.shape[0], 4 * BP)
    summed = lax.dot_general(stem_weight, onehot, (((1,), (1,)), ((), ())), preferred_element_type=jnp.float32)
    return summed.astype(jnp.bfloat16)


def trunk_stream(window, trunk_in, trunk_out):
    stream = window.astype(jnp.float32)
    layers = trunk_in.shape[0]
    extent = window.shape[-1]
    for layer_index in range(layers):
        dilation = max(1, extent // 2 ** (layers - layer_index))
        active = jax.nn.relu(stream).astype(jnp.bfloat16)
        stacked = jnp.concatenate([shift_cols(active, -dilation), active, shift_cols(active, dilation)], axis=0)
        inner = jnp.dot(trunk_in[layer_index], stacked, preferred_element_type=jnp.float32)
        squeezed = jax.nn.relu(inner).astype(jnp.bfloat16)
        stream = stream + jnp.dot(trunk_out[layer_index], squeezed, preferred_element_type=jnp.float32)
    return stream


def conv_square(active, kernel):
    channels = active.shape[0]
    extent = active.shape[1]
    padded = jnp.pad(active, ((0, 0), (1, 1), (1, 1)))
    summed = jnp.zeros((kernel.shape[1], extent * extent), jnp.float32)
    for row_tap in range(3):
        stacked = jnp.concatenate([padded[:, row_tap:row_tap + extent, col_tap:col_tap + extent] for col_tap in range(3)], axis=0)
        summed = summed + jnp.dot(kernel[row_tap], stacked.reshape(3 * channels, extent * extent), preferred_element_type=jnp.float32)
    return summed.reshape(kernel.shape[1], extent, extent)


def skew_square(contact_maps):
    targets = contact_maps.shape[0]
    extent = contact_maps.shape[1]
    padded = jnp.pad(contact_maps, ((0, 0), (0, 0), (0, extent)))
    flattened = padded.reshape(targets, extent * 2 * extent)
    flattened = jnp.pad(flattened, ((0, 0), (0, extent)))
    sliced = flattened[:, :extent * (2 * extent + 1)]
    return sliced.reshape(targets, extent, 2 * extent + 1)[:, :, :extent]


def reference(genome_bases, stitch_weight, stem_weight, trunk_in, trunk_out, pair_weight, distance_rate, tower_conv, tower_mix, head_weight):
    features = stem_features(genome_bases, stem_weight)
    padded_features = jnp.pad(features, ((0, 0), (0, BINS - STRIDE)))
    row_weight = stitch_weight.astype(jnp.float32)
    channels = distance_rate.shape[0]
    positions = jnp.arange(BINS)
    separation = jnp.abs(positions[:, None] - positions[None, :]).astype(jnp.float32)
    decay_term = jnp.log1p(separation)

    def one_window(window_index):
        window = lax.dynamic_slice_in_dim(padded_features, window_index * STRIDE, BINS, axis=1)
        stream = trunk_stream(window, trunk_in, trunk_out)
        projected = jnp.dot(pair_weight, jax.nn.relu(stream).astype(jnp.bfloat16), preferred_element_type=jnp.float32)
        mixed = projected[:channels][:, :, None] + projected[channels:][:, None, :] - distance_rate[:, None, None] * decay_term[None]
        pair_map = jax.nn.relu(mixed).astype(jnp.bfloat16)
        grid = pair_map.astype(jnp.float32)
        for layer_index in range(TOWER):
            active = jax.nn.relu(grid).astype(jnp.bfloat16)
            convolved = conv_square(active, tower_conv[layer_index])
            squeezed = jax.nn.relu(convolved).astype(jnp.bfloat16)
            update = jnp.dot(tower_mix[layer_index], squeezed.reshape(channels, BINS * BINS), preferred_element_type=jnp.float32)
            grid = grid + update.reshape(channels, BINS, BINS)
        final_act = jax.nn.relu(grid).astype(jnp.bfloat16)
        contact_maps = jnp.dot(head_weight, final_act.reshape(channels, BINS * BINS), preferred_element_type=jnp.float32)
        skewed = skew_square(contact_maps.reshape(TARGETS, BINS, BINS))
        return skewed * row_weight[None, :, None]

    weighted = lax.map(one_window, jnp.arange(N_GENOME, dtype=jnp.int32))
    blocks = BINS // STRIDE
    stacked_blocks = weighted.reshape(N_GENOME, TARGETS, blocks, STRIDE, BINS)
    numerator = jnp.zeros((N_GENOME, TARGETS, STRIDE, BINS), jnp.float32)
    weight_sum = jnp.zeros((N_GENOME, STRIDE, BINS), jnp.float32)
    owner = jnp.arange(N_GENOME)
    offsets = jnp.arange(BINS)
    local_rows = jnp.arange(STRIDE)
    for block_index in range(blocks):
        moved = jnp.pad(stacked_blocks[:, :, block_index], ((block_index, 0), (0, 0), (0, 0), (0, 0)))[:N_GENOME]
        numerator = numerator + moved
        window_rows = STRIDE * block_index + local_rows
        covered = (owner[:, None, None] >= block_index) & (window_rows[None, :, None] + offsets[None, None, :] < BINS)
        weight_sum = weight_sum + jnp.where(covered, row_weight[window_rows][None, :, None], 0.0)
    stitched = numerator / jnp.maximum(weight_sum, 1.0)[:, None]
    total_rows = N_GENOME * STRIDE
    stitched = jnp.transpose(stitched, (1, 0, 2, 3)).reshape(TARGETS, total_rows, BINS)

    extended = jnp.pad(stitched, ((0, 0), (STRIDE, 0), (0, 0)))
    prefix = jnp.concatenate([jnp.zeros((TARGETS, total_rows + STRIDE, 1), jnp.float32), jnp.cumsum(extended, axis=2)], axis=2)
    square = prefix[:, :, STRIDE + 1:2 * STRIDE + 1] - prefix[:, :, 1:STRIDE + 1]
    contact = jnp.exp(extended[:, :, 1:STRIDE + 1])
    insulation = jnp.zeros((TARGETS, total_rows), jnp.float32)
    upstream = jnp.zeros((TARGETS, total_rows), jnp.float32)
    for column in range(STRIDE):
        insulation = insulation + square[:, STRIDE - column:STRIDE - column + total_rows, column]
        upstream = upstream + contact[:, STRIDE - column - 1:STRIDE - column - 1 + total_rows, column]
    insulation = insulation / (STRIDE * STRIDE)
    downstream = jnp.sum(contact[:, STRIDE:], axis=2)
    direction = (downstream - upstream) / (downstream + upstream)
    return stitched, jnp.stack([insulation, direction])
```

```python
import functools

import jax
import jax.numpy as jnp
from jax import lax
from jax.experimental import pallas as pl
from jax.experimental.pallas import tpu as pltpu
from jax.sharding import PartitionSpec as P

BP = 2048
STRIDE = 64
BINS = 256
BLOCKS = BINS // STRIDE
LANES = 128
F32 = jnp.float32
BF16 = jnp.bfloat16
VMEM_BYTES = 48 * 1024 * 1024


def from_behind(block, axis, distance):
    devices = range(lax.axis_size(axis))
    route = [(i - distance, i) for i in devices if i - distance in devices]
    return lax.ppermute(block, axis, route)


def dot(a, b):
    return jnp.dot(a, b, preferred_element_type=F32)


def stem_kernel(bins, bases_hbm, weight_hbm, out_ref, bases, weight, base_sem, weight_sem):
    groups = BP // LANES
    chunks = weight.shape[0]
    span = weight.shape[2]
    base_copy = pltpu.make_async_copy(bases_hbm, bases, base_sem)
    base_copy.start()
    copies = []
    for k in range(chunks):
        copy = pltpu.make_async_copy(
            weight_hbm.at[:, pl.ds(k * span, span)], weight.at[k], weight_sem.at[k]
        )
        copy.start()
        copies.append(copy)
    row = lax.broadcasted_iota(jnp.int32, (LANES, 4 * LANES), 0)
    col = lax.broadcasted_iota(jnp.int32, (LANES, 4 * LANES), 1)
    repeat = (row == col // 4).astype(F32).astype(BF16)
    letter = (lax.broadcasted_iota(jnp.int32, (bins, 4 * LANES), 1) % 4).astype(F32)
    base_copy.wait()
    total = None
    per_chunk = groups // chunks
    for k in range(chunks):
        hot = []
        for q in range(per_chunk):
            rows = bases[pl.ds(k * per_chunk + q, bins, stride=groups), :]
            spread = dot(rows.astype(F32).astype(BF16), repeat)
            hot.append(jnp.where(spread == letter, 1.0, 0.0).astype(BF16))
        hot = jnp.concatenate(hot, axis=1)
        copies[k].wait()
        part = lax.dot_general(
            weight[k], hot, (((1,), (1,)), ((), ())), preferred_element_type=F32
        )
        total = part if total is None else total + part
    out_ref[...] = total.astype(BF16)


def stem(genome_bases, stem_weight):
    bins = genome_bases.shape[0] // BP
    channels, depth = stem_weight.shape
    chunks = 4
    return pl.pallas_call(
        functools.partial(stem_kernel, bins),
        out_shape=jax.ShapeDtypeStruct((channels, bins), BF16),
        in_specs=[pl.BlockSpec(memory_space=pl.ANY)] * 2,
        out_specs=pl.BlockSpec(memory_space=pltpu.VMEM),
        scratch_shapes=[
            pltpu.VMEM((genome_bases.shape[0] // LANES, LANES), jnp.int32),
            pltpu.VMEM((chunks, channels, depth // chunks), BF16),
            pltpu.SemaphoreType.DMA,
            pltpu.SemaphoreType.DMA((chunks,)),
        ],
        compiler_params=pltpu.CompilerParams(vmem_limit_bytes=VMEM_BYTES),
        name="stem",
    )(genome_bases.reshape(-1, LANES), stem_weight)


def banded(kernel, rows):
    taps, out_channels, depth = kernel.shape
    flat = jnp.concatenate([kernel[u] for u in range(taps)], axis=1)
    bands = []
    for r in range(rows):
        parts = [flat]
        if r:
            parts.insert(0, jnp.zeros((out_channels, r * depth), BF16))
        if rows - 1 - r:
            parts.append(jnp.zeros((out_channels, (rows - 1 - r) * depth), BF16))
        bands.append(jnp.concatenate(parts, axis=1) if len(parts) > 1 else flat)
    return jnp.concatenate(bands, axis=0)


def block_diagonal(matrix, count):
    height, width = matrix.shape
    tiled = jnp.concatenate([jnp.concatenate([matrix] * count, axis=1)] * count, axis=0)
    row = lax.broadcasted_iota(jnp.int32, tiled.shape, 0) // height
    col = lax.broadcasted_iota(jnp.int32, tiled.shape, 1) // width
    return jnp.where(row == col, tiled, jnp.zeros((), BF16))


def head_by_row(head, count):
    targets, width = head.shape
    wide = jnp.concatenate([head] * count, axis=1)
    tall = jnp.broadcast_to(wide[:, None, :], (targets, count, count * width))
    row = lax.broadcasted_iota(jnp.int32, tall.shape, 1)
    col = lax.broadcasted_iota(jnp.int32, tall.shape, 2) // width
    return jnp.where(row == col, tall, jnp.zeros((), BF16)).reshape(targets * count, count * width)


def segments(margin):
    sizes = [BINS - STRIDE * b + margin + 1 for b in range(BLOCKS)]
    offsets = [sum(sizes[:b]) for b in range(BLOCKS)]
    lanes = -(-sum(sizes) // LANES) * LANES
    return sizes, offsets, lanes


def shifted(values, offset):
    if offset == 0:
        return values
    channels, extent = values.shape
    edge = jnp.zeros((channels, abs(offset)), values.dtype)
    if offset >= 0:
        return jnp.concatenate([values[:, offset:], edge], axis=1)
    return jnp.concatenate([edge, values[:, : extent + offset]], axis=1)


def main_kernel(
    height,
    groups,
    place_ref,
    *refs,
):
    feature_refs = refs[: 2 * BLOCKS - 1]
    (
        trunk_in,
        trunk_out,
        pair_weight,
        rate_ref,
        conv_a,
        conv_b,
        mix_a,
        mix_b,
        head,
        row_weight,
        stitched_ref,
        keep_ref,
        *rest,
    ) = refs[2 * BLOCKS - 1 :]
    send_refs = rest[: STRIDE // height]
    taps_a, taps_b, grid_ref, final_ref = rest[STRIDE // height :]
    margin = 2
    sizes, offsets, lanes = segments(margin)
    tower_row = place_ref[0] * height
    channels = rate_ref.shape[0]
    depth = 3 * channels

    blocks = jnp.concatenate([r[...] for r in feature_refs], axis=1)
    extent = BINS
    windows = []
    for b in range(BLOCKS):
        first = (BLOCKS - 1 - b) * STRIDE
        windows.append(blocks[:, first : first + BINS].astype(F32))
    stream = jnp.concatenate(windows, axis=1)
    layers = trunk_in.shape[0]
    for layer in range(layers):
        dilation = max(1, extent // 2 ** (layers - layer))
        active = jax.nn.relu(stream)
        parts = [active[:, b * BINS : (b + 1) * BINS] for b in range(BLOCKS)]
        stacked = jnp.concatenate(
            [
                jnp.concatenate([shifted(p, o) for p in parts], axis=1).astype(BF16)
                for o in (-dilation, 0, dilation)
            ],
            axis=0,
        )
        inner = dot(trunk_in[layer], stacked)
        squeezed = jax.nn.relu(inner).astype(BF16)
        stream = stream + dot(trunk_out[layer], squeezed)
    projected = dot(pair_weight[...], jax.nn.relu(stream).astype(BF16))

    lane = lax.broadcasted_iota(jnp.int32, (1, lanes), 1)
    block_of = jnp.zeros((1, lanes), jnp.int32)
    start_of = jnp.zeros((1, lanes), jnp.int32)
    for b in range(1, BLOCKS):
        block_of = jnp.where(lane >= offsets[b], b, block_of)
        start_of = jnp.where(lane >= offsets[b], offsets[b], start_of)
    step = lane - start_of
    first_row = STRIDE * block_of + tower_row - margin
    column = first_row + step
    in_column = (column < BINS) & (column >= 0)

    right = []
    left = []
    for b in range(BLOCKS):
        begin = STRIDE * b + tower_row - margin
        turn = jnp.where(begin > 0, BINS - begin, -begin)
        terms = projected[:, b * BINS : (b + 1) * BINS]
        turned = pltpu.roll(terms, turn, 1)
        left.append(turned[:channels, :LANES])
        own = turned[channels:]
        if sizes[b] > BINS:
            own = jnp.concatenate([own, own[:, : sizes[b] - BINS]], axis=1)
        right.append(own[:, : sizes[b]])
    used = sum(sizes)
    if lanes > used:
        right.append(jnp.zeros((channels, lanes - used), F32))
    right = jnp.concatenate(right, axis=1)
    rate = jnp.broadcast_to(rate_ref[...], (channels, LANES))
    rate = jnp.concatenate([rate] * (lanes // LANES), axis=1)

    def place_taps(ref, slot, act):
        before = pltpu.roll(act, 1, 1)
        after = pltpu.roll(act, lanes - 1, 1)
        ref[pl.ds(slot * depth, channels), :] = before.astype(BF16)
        ref[pl.ds(slot * depth + channels, channels), :] = act.astype(BF16)
        ref[pl.ds(slot * depth + 2 * channels, channels), :] = after.astype(BF16)

    def inside(row):
        at = first_row + row
        return in_column & (at >= 0) & (at < BINS)

    for row in range(height + 2 * margin):
        apart = jnp.abs(step - row).astype(F32)
        decay = jnp.log1p(apart)
        tiles = []
        for tile in range(lanes // LANES):
            piece = None
            here = lane[:, tile * LANES : (tile + 1) * LANES]
            for b in range(BLOCKS):
                low, high = offsets[b], offsets[b] + sizes[b]
                if high <= tile * LANES or low >= (tile + 1) * LANES:
                    continue
                spread = jnp.broadcast_to(left[b][:, row : row + 1], (channels, LANES))
                piece = spread if piece is None else jnp.where(here >= low, spread, piece)
            tiles.append(piece)
        mixed = jnp.concatenate(tiles, axis=1) + right - rate * decay
        place_taps(taps_a, row, jnp.where(inside(row), jnp.maximum(mixed, 0.0), 0.0))

    span = groups[0]
    for group in range((height + 2) // span):
        first = group * span
        conv = dot(conv_a[...], taps_a[pl.ds(first * depth, (span + 2) * depth), :])
        update = dot(mix_a[...], jnp.maximum(conv, 0.0).astype(BF16))
        for r in range(span):
            row = first + r
            kept = taps_a[pl.ds((row + 1) * depth + channels, channels), :].astype(F32)
            grid = kept + update[r * channels : (r + 1) * channels]
            if 1 <= row <= height:
                grid_ref[pl.ds((row - 1) * channels, channels), :] = grid
            place_taps(taps_b, row, jnp.where(inside(row + 1), jnp.maximum(grid, 0.0), 0.0))
    span = groups[1]
    for group in range(height // span):
        first = group * span
        conv = dot(conv_b[...], taps_b[pl.ds(first * depth, (span + 2) * depth), :])
        update = dot(mix_b[...], jnp.maximum(conv, 0.0).astype(BF16))
        rows = pl.ds(first * channels, span * channels)
        final_ref[rows, :] = jnp.maximum(grid_ref[rows, :] + update, 0.0).astype(BF16)
    targets = head.shape[0] // height
    contact = dot(head[...], final_ref[...]).reshape(targets, height, lanes)

    local = lax.broadcasted_iota(jnp.int32, (height, BINS), 0)
    ahead = lax.broadcasted_iota(jnp.int32, (height, BINS), 1)
    weight_sum = jnp.zeros((height, BINS), F32)
    weights = []
    for b in range(BLOCKS):
        weight = jnp.concatenate([row_weight[b]] * (BINS // LANES), axis=1)
        reach = STRIDE * b + tower_row + local + ahead < BINS
        weight = jnp.where(reach, weight, 0.0)
        weights.append(weight)
        weight_sum = weight_sum + weight
    scale = 1.0 / jnp.maximum(weight_sum, 1.0)
    weights = [w * scale for w in weights]
    stitched = []
    map_row = lax.broadcasted_iota(jnp.int32, (height, lanes), 0)
    for t in range(targets):
        band = None
        skewed = contact[t]
        for bit in range((height - 1).bit_length()):
            turned = pltpu.roll(skewed, lanes - (1 << bit), 1)
            skewed = jnp.where((map_row >> bit) & 1 == 1, turned, skewed)
        for b in range(BLOCKS):
            first, reach = offsets[b] + margin, BINS - STRIDE * b
            piece = skewed[:, first : first + reach]
            if reach < BINS:
                piece = jnp.concatenate([piece, jnp.zeros((height, BINS - reach), F32)], axis=1)
            piece = piece * weights[b]
            band = piece if band is None else band + piece
        stitched_ref[t] = band
        stitched.append(band[:, : 2 * STRIDE])

    near = jnp.concatenate(stitched, axis=0)
    wide = 2 * STRIDE
    col = lax.broadcasted_iota(jnp.int32, (wide, wide), 0)
    corner = lax.broadcasted_iota(jnp.int32, (wide, wide), 1)
    box = ((col > corner) & (col <= corner + STRIDE) & (corner < STRIDE)).astype(F32)
    square = jnp.dot(near, box, preferred_element_type=F32, precision=lax.Precision.HIGHEST)
    at = lax.broadcasted_iota(jnp.int32, near.shape, 1)
    contact = jnp.where((at >= 1) & (at <= STRIDE), jnp.exp(near), 0.0)
    down = jnp.sum(contact, axis=1, keepdims=True)
    here = lax.broadcasted_iota(jnp.int32, (height, wide), 0)
    there = lax.broadcasted_iota(jnp.int32, (height, wide), 1)

    def by_row(values):
        rows = []
        for t in range(targets):
            own = pltpu.roll(
                values[t * height : (t + 1) * height], 0, 1, stride=1, stride_axis=0
            )
            rows.append(jnp.sum(own, axis=0, keepdims=True))
        return rows

    down_rows = []
    for t in range(targets):
        own = jnp.where(here == there, down[t * height : (t + 1) * height], 0.0)
        down_rows.append(jnp.sum(own, axis=0, keepdims=True))
    parts = jnp.concatenate(by_row(square) + by_row(contact) + down_rows, axis=0)
    keep_ref[...] = parts[:, :height]
    for k, ref in enumerate(send_refs):
        ref[...] = parts[: 2 * targets, (k + 1) * height : (k + 2) * height]


def per_device(
    genome_bases,
    stitch_weight,
    stem_weight,
    trunk_in,
    trunk_out,
    pair_weight,
    distance_rate,
    tower_conv,
    tower_mix,
    head_weight,
):
    towers = lax.axis_size("tower")
    height = STRIDE // towers
    tower_index = lax.axis_index("tower")
    genome_index = lax.axis_index("genome")
    own = stem(genome_bases, stem_weight)
    features = [
        own if d == 0 else from_behind(own, "genome", -d) for d in range(1 - BLOCKS, BLOCKS)
    ]
    groups = (3, 4)
    channels = distance_rate.shape[0]
    targets = head_weight.shape[0]
    conv_a = banded(tower_conv[0], groups[0])
    conv_b = banded(tower_conv[1], groups[1])
    mix_a = block_diagonal(tower_mix[0], groups[0])
    mix_b = block_diagonal(tower_mix[1], groups[1])
    head = head_by_row(head_weight, height)
    row_weight = lax.dynamic_slice_in_dim(
        stitch_weight.reshape(BLOCKS, STRIDE), tower_index * height, height, axis=1
    )
    row_weight = jnp.where(jnp.arange(BLOCKS)[:, None] <= genome_index, row_weight, 0)
    row_weight = jnp.broadcast_to(row_weight.astype(F32)[:, :, None], (BLOCKS, height, LANES))
    place = tower_index.astype(jnp.int32).reshape(1)
    lanes = segments(2)[2]
    steps = STRIDE // height
    vmem = pl.BlockSpec(memory_space=pltpu.VMEM)
    small = jax.ShapeDtypeStruct((2 * targets, height), F32)
    stitched, keep, *sends = pl.pallas_call(
        functools.partial(main_kernel, height, groups),
        out_shape=[
            jax.ShapeDtypeStruct((targets, height, BINS), F32),
            jax.ShapeDtypeStruct((3 * targets, height), F32),
        ]
        + [small] * steps,
        in_specs=[pl.BlockSpec(memory_space=pltpu.SMEM)] + [vmem] * (2 * BLOCKS - 1 + 10),
        out_specs=[vmem] * (2 + steps),
        scratch_shapes=[
            pltpu.VMEM(((height + 4) * 3 * channels, lanes), BF16),
            pltpu.VMEM(((height + 2) * 3 * channels, lanes), BF16),
            pltpu.VMEM((height * channels, lanes), F32),
            pltpu.VMEM((height * channels, lanes), BF16),
        ],
        compiler_params=pltpu.CompilerParams(vmem_limit_bytes=VMEM_BYTES),
        name="windows",
    )(
        place,
        *features,
        trunk_in,
        trunk_out,
        pair_weight,
        distance_rate.reshape(channels, 1),
        conv_a,
        conv_b,
        mix_a,
        mix_b,
        head,
        row_weight,
    )
    sums = keep[: 2 * targets]
    for k in range(steps):
        sums = sums + from_behind(sends[k], ("genome", "tower"), k + 1)
    row = (genome_index * towers + tower_index) * height + jnp.arange(height)
    missing = jnp.maximum(STRIDE - row, 0).astype(F32)
    upstream = sums[targets:] + missing[None]
    downstream = keep[2 * targets :]
    insulation = sums[:targets] / (STRIDE * STRIDE)
    direction = (downstream - upstream) / (downstream + upstream)
    return (stitched, jnp.stack([insulation, direction]))


def solution(mesh):
    placed = (P("genome"), P(), P(), P(), P(), P(), P(), P(), P(), P())
    return jax.shard_map(
        per_device,
        mesh=mesh,
        in_specs=placed,
        out_specs=(P(None, ("genome", "tower"), None), P(None, None, ("genome", "tower"))),
        check_vma=False,
    )
```

```python
import functools

import jax
import jax.numpy as jnp
from jax import lax
from jax.experimental import pallas as pl
from jax.experimental.pallas import tpu as pltpu
from jax.sharding import PartitionSpec as P

BP = 2048
STRIDE = 64
BINS = 256
BLOCKS = BINS // STRIDE
LANES = 128
F32 = jnp.float32
BF16 = jnp.bfloat16
VMEM_BYTES = 48 * 1024 * 1024


def dot(a, b):
    return jnp.dot(a, b, preferred_element_type=F32)


def stem_kernel(bins, bases_hbm, weight_hbm, out_ref, bases, weight, base_sem, weight_sem):
    groups = BP // LANES
    chunks = weight.shape[0]
    span = weight.shape[2]
    base_copy = pltpu.make_async_copy(bases_hbm, bases, base_sem)
    base_copy.start()
    copies = []
    for k in range(chunks):
        copy = pltpu.make_async_copy(
            weight_hbm.at[:, pl.ds(k * span, span)], weight.at[k], weight_sem.at[k]
        )
        copy.start()
        copies.append(copy)
    row = lax.broadcasted_iota(jnp.int32, (LANES, 4 * LANES), 0)
    col = lax.broadcasted_iota(jnp.int32, (LANES, 4 * LANES), 1)
    repeat = (row == col // 4).astype(F32).astype(BF16)
    letter = (lax.broadcasted_iota(jnp.int32, (bins, 4 * LANES), 1) % 4).astype(F32)
    base_copy.wait()
    total = None
    per_chunk = groups // chunks
    for k in range(chunks):
        hot = []
        for q in range(per_chunk):
            rows = bases[pl.ds(k * per_chunk + q, bins, stride=groups), :]
            spread = dot(rows.astype(F32).astype(BF16), repeat)
            hot.append(jnp.where(spread == letter, 1.0, 0.0).astype(BF16))
        hot = jnp.concatenate(hot, axis=1)
        copies[k].wait()
        part = lax.dot_general(
            weight[k], hot, (((1,), (1,)), ((), ())), preferred_element_type=F32
        )
        total = part if total is None else total + part
    total = total.astype(BF16)
    half = out_ref.shape[0]
    out_ref[...] = jnp.concatenate([total[:half], total[half:]], axis=1)


def stem(genome_bases, stem_weight):
    bins = genome_bases.shape[0] // BP
    channels, depth = stem_weight.shape
    chunks = 4
    return pl.pallas_call(
        functools.partial(stem_kernel, bins),
        out_shape=jax.ShapeDtypeStruct((channels // 2, 2 * bins), BF16),
        in_specs=[pl.BlockSpec(memory_space=pltpu.HBM)] * 2,
        out_specs=pl.BlockSpec(memory_space=pltpu.VMEM),
        scratch_shapes=[
            pltpu.VMEM((genome_bases.shape[0] // LANES, LANES), jnp.int32),
            pltpu.VMEM((chunks, channels, depth // chunks), BF16),
            pltpu.SemaphoreType.DMA,
            pltpu.SemaphoreType.DMA((chunks,)),
        ],
        compiler_params=pltpu.CompilerParams(vmem_limit_bytes=63 * 1024 * 1024),
        name="stem",
    )(genome_bases.reshape(-1, LANES), stem_weight)


def banded(kernel, rows):
    taps, out_channels, depth = kernel.shape
    flat = jnp.concatenate([kernel[u] for u in range(taps)], axis=1)
    bands = []
    for r in range(rows):
        parts = [flat]
        if r:
            parts.insert(0, jnp.zeros((out_channels, r * depth), BF16))
        if rows - 1 - r:
            parts.append(jnp.zeros((out_channels, (rows - 1 - r) * depth), BF16))
        bands.append(jnp.concatenate(parts, axis=1) if len(parts) > 1 else flat)
    return jnp.concatenate(bands, axis=0)


def block_diagonal(matrix, count):
    height, width = matrix.shape
    tiled = jnp.concatenate([jnp.concatenate([matrix] * count, axis=1)] * count, axis=0)
    row = lax.broadcasted_iota(jnp.int32, tiled.shape, 0) // height
    col = lax.broadcasted_iota(jnp.int32, tiled.shape, 1) // width
    return jnp.where(row == col, tiled, jnp.zeros((), BF16))


def head_by_row(head, count):
    targets, width = head.shape
    wide = jnp.concatenate([head] * count, axis=1)
    tall = jnp.broadcast_to(wide[:, None, :], (targets, count, count * width))
    row = lax.broadcasted_iota(jnp.int32, tall.shape, 1)
    col = lax.broadcasted_iota(jnp.int32, tall.shape, 2) // width
    return jnp.where(row == col, tall, jnp.zeros((), BF16)).reshape(targets * count, count * width)


def segments(margin):
    sizes = [BINS - STRIDE * b + margin + 1 for b in range(BLOCKS)]
    offsets = [sum(sizes[:b]) for b in range(BLOCKS)]
    lanes = -(-sum(sizes) // LANES) * LANES
    return sizes, offsets, lanes


def shifted(values, offset):
    if offset == 0:
        return values
    channels, extent = values.shape
    edge = jnp.zeros((channels, abs(offset)), values.dtype)
    if offset >= 0:
        return jnp.concatenate([values[:, offset:], edge], axis=1)
    return jnp.concatenate([edge, values[:, : extent + offset]], axis=1)


def main_kernel(
    height,
    groups,
    place_ref,
    *refs,
):
    (
        features,
        trunk_in,
        trunk_out,
        pair_weight,
        rate_ref,
        conv_a,
        conv_b,
        mix_a,
        mix_b,
        head,
        row_weight,
        stitched_ref,
        keep_ref,
        send_ref,
        taps_a,
        taps_b,
        grid_ref,
        final_ref,
    ) = refs
    margin = 2
    sizes, offsets, lanes = segments(margin)
    tower_row = place_ref[0] * height
    channels = rate_ref.shape[0]
    depth = 3 * channels

    starts = features.shape[0]
    blocks = []
    for d in range(1 - BLOCKS, BLOCKS):
        at = place_ref[1] + d
        block = features[jnp.clip(at, 0, starts - 1)]
        blocks.append(jnp.where((at >= 0) & (at < starts), block, jnp.zeros_like(block)))
    blocks = jnp.concatenate(
        [
            jnp.concatenate([half[:, :STRIDE] for half in blocks], axis=1),
            jnp.concatenate([half[:, STRIDE:] for half in blocks], axis=1),
        ],
        axis=0,
    )
    extent = BINS
    windows = []
    for b in range(BLOCKS):
        first = (BLOCKS - 1 - b) * STRIDE
        windows.append(blocks[:, first : first + BINS].astype(F32))
    stream = jnp.concatenate(windows, axis=1)
    layers = trunk_in.shape[0]
    for layer in range(layers):
        dilation = max(1, extent // 2 ** (layers - layer))
        active = jax.nn.relu(stream)
        parts = [active[:, b * BINS : (b + 1) * BINS] for b in range(BLOCKS)]
        stacked = jnp.concatenate(
            [
                jnp.concatenate([shifted(p, o) for p in parts], axis=1).astype(BF16)
                for o in (-dilation, 0, dilation)
            ],
            axis=0,
        )
        inner = dot(trunk_in[layer], stacked)
        squeezed = jax.nn.relu(inner).astype(BF16)
        stream = stream + dot(trunk_out[layer], squeezed)
    projected = dot(pair_weight[...], jax.nn.relu(stream).astype(BF16))

    lane = lax.broadcasted_iota(jnp.int32, (1, lanes), 1)
    block_of = jnp.zeros((1, lanes), jnp.int32)
    start_of = jnp.zeros((1, lanes), jnp.int32)
    for b in range(1, BLOCKS):
        block_of = jnp.where(lane >= offsets[b], b, block_of)
        start_of = jnp.where(lane >= offsets[b], offsets[b], start_of)
    step = lane - start_of
    first_row = STRIDE * block_of + tower_row - margin
    column = first_row + step
    in_column = (column < BINS) & (column >= 0)

    right = []
    left = []
    for b in range(BLOCKS):
        begin = STRIDE * b + tower_row - margin
        turn = jnp.where(begin > 0, BINS - begin, -begin)
        terms = projected[:, b * BINS : (b + 1) * BINS]
        turned = pltpu.roll(terms, turn, 1)
        left.append(turned[:channels, :LANES])
        own = turned[channels:]
        if sizes[b] > BINS:
            own = jnp.concatenate([own, own[:, : sizes[b] - BINS]], axis=1)
        right.append(own[:, : sizes[b]])
    used = sum(sizes)
    if lanes > used:
        right.append(jnp.zeros((channels, lanes - used), F32))
    right = jnp.concatenate(right, axis=1)
    rate = jnp.broadcast_to(rate_ref[...], (channels, LANES))
    rate = jnp.concatenate([rate] * (lanes // LANES), axis=1)

    def place_taps(ref, slot, act):
        before = pltpu.roll(act, 1, 1)
        after = pltpu.roll(act, lanes - 1, 1)
        ref[pl.ds(slot * depth, channels), :] = before.astype(BF16)
        ref[pl.ds(slot * depth + channels, channels), :] = act.astype(BF16)
        ref[pl.ds(slot * depth + 2 * channels, channels), :] = after.astype(BF16)

    def inside(row):
        at = first_row + row
        return in_column & (at >= 0) & (at < BINS)

    for row in range(height + 2 * margin):
        apart = jnp.abs(step - row).astype(F32)
        decay = jnp.log1p(apart)
        tiles = []
        for tile in range(lanes // LANES):
            piece = None
            here = lane[:, tile * LANES : (tile + 1) * LANES]
            for b in range(BLOCKS):
                low, high = offsets[b], offsets[b] + sizes[b]
                if high <= tile * LANES or low >= (tile + 1) * LANES:
                    continue
                spread = jnp.broadcast_to(left[b][:, row : row + 1], (channels, LANES))
                piece = spread if piece is None else jnp.where(here >= low, spread, piece)
            tiles.append(piece)
        mixed = jnp.concatenate(tiles, axis=1) + right - rate * decay
        place_taps(taps_a, row, jnp.where(inside(row), jnp.maximum(mixed, 0.0), 0.0))

    span = groups[0]
    for group in range((height + 2) // span):
        first = group * span
        conv = dot(conv_a[...], taps_a[pl.ds(first * depth, (span + 2) * depth), :])
        update = dot(mix_a[...], jnp.maximum(conv, 0.0).astype(BF16))
        for r in range(span):
            row = first + r
            kept = taps_a[pl.ds((row + 1) * depth + channels, channels), :].astype(F32)
            grid = kept + update[r * channels : (r + 1) * channels]
            if 1 <= row <= height:
                grid_ref[pl.ds((row - 1) * channels, channels), :] = grid
            place_taps(taps_b, row, jnp.where(inside(row + 1), jnp.maximum(grid, 0.0), 0.0))
    span = groups[1]
    for group in range(height // span):
        first = group * span
        conv = dot(conv_b[...], taps_b[pl.ds(first * depth, (span + 2) * depth), :])
        update = dot(mix_b[...], jnp.maximum(conv, 0.0).astype(BF16))
        rows = pl.ds(first * channels, span * channels)
        final_ref[rows, :] = jnp.maximum(grid_ref[rows, :] + update, 0.0).astype(BF16)
    targets = head.shape[0] // height
    contact = dot(head[...], final_ref[...]).reshape(targets, height, lanes)

    local = lax.broadcasted_iota(jnp.int32, (height, BINS), 0)
    ahead = lax.broadcasted_iota(jnp.int32, (height, BINS), 1)
    weight_sum = jnp.zeros((height, BINS), F32)
    weights = []
    for b in range(BLOCKS):
        weight = jnp.concatenate([row_weight[b]] * (BINS // LANES), axis=1)
        reach = STRIDE * b + tower_row + local + ahead < BINS
        weight = jnp.where(reach, weight, 0.0)
        weights.append(weight)
        weight_sum = weight_sum + weight
    scale = 1.0 / jnp.maximum(weight_sum, 1.0)
    weights = [w * scale for w in weights]
    stitched = []
    map_row = lax.broadcasted_iota(jnp.int32, (height, lanes), 0)
    for t in range(targets):
        band = None
        skewed = contact[t]
        for bit in range((height - 1).bit_length()):
            turned = pltpu.roll(skewed, lanes - (1 << bit), 1)
            skewed = jnp.where((map_row >> bit) & 1 == 1, turned, skewed)
        for b in range(BLOCKS):
            first, reach = offsets[b] + margin, BINS - STRIDE * b
            piece = skewed[:, first : first + reach]
            if reach < BINS:
                piece = jnp.concatenate([piece, jnp.zeros((height, BINS - reach), F32)], axis=1)
            piece = piece * weights[b]
            band = piece if band is None else band + piece
        stitched_ref[t] = band
        stitched.append(band[:, : 2 * STRIDE])

    near = jnp.concatenate(stitched, axis=0)
    wide = 2 * STRIDE
    col = lax.broadcasted_iota(jnp.int32, (wide, wide), 0)
    corner = lax.broadcasted_iota(jnp.int32, (wide, wide), 1)
    box = ((col > corner) & (col <= corner + STRIDE) & (corner < STRIDE)).astype(F32)
    square = jnp.dot(near, box, preferred_element_type=F32, precision=lax.Precision.HIGHEST)
    at = lax.broadcasted_iota(jnp.int32, near.shape, 1)
    contact = jnp.where((at >= 1) & (at <= STRIDE), jnp.exp(near), 0.0)
    down = jnp.sum(contact, axis=1, keepdims=True)
    here = lax.broadcasted_iota(jnp.int32, (height, wide), 0)
    there = lax.broadcasted_iota(jnp.int32, (height, wide), 1)

    def by_row(values):
        rows = []
        for t in range(targets):
            own = pltpu.roll(
                values[t * height : (t + 1) * height], 0, 1, stride=1, stride_axis=0
            )
            rows.append(jnp.sum(own, axis=0, keepdims=True))
        return rows

    down_rows = []
    for t in range(targets):
        own = jnp.where(here == there, down[t * height : (t + 1) * height], 0.0)
        down_rows.append(jnp.sum(own, axis=0, keepdims=True))
    rows = by_row(square) + by_row(contact)
    keep_ref[...] = jnp.concatenate(rows + down_rows, axis=0)
    send_ref[...] = jnp.zeros_like(send_ref)
    per_row = LANES // height
    slots = send_ref.shape[0]
    own = place_ref[1] * (STRIDE // height) + place_ref[0]
    first = lax.broadcasted_iota(jnp.int32, (per_row, LANES), 1) < height
    packs = [
        jnp.concatenate(
            rows[p : p + per_row]
            + [jnp.zeros((1, LANES), F32)] * (per_row - len(rows[p : p + per_row])),
            axis=0,
        )
        for p in range(0, len(rows), per_row)
    ]
    for k in range(1, STRIDE // height + 1):
        packed = []
        for pack in packs:
            turned = jnp.where(first, pltpu.roll(pack, LANES - k * height, 1), 0.0)
            turned = pltpu.roll(turned, 0, 1, stride=height, stride_axis=0)
            packed.append(jnp.sum(turned, axis=0, keepdims=True))

        @pl.when(own + k < slots)
        def _():
            send_ref[own + k] = jnp.concatenate(packed, axis=0)


def finish_kernel(height, place_ref, keep_ref, got_ref, out_ref):
    targets = out_ref.shape[0]
    per_row = LANES // height
    keep = keep_ref[...][:, :height]
    got = jnp.sum(got_ref[...], axis=0)
    rows = []
    for q in range(2 * targets):
        at = (q % per_row) * height
        rows.append(got[q // per_row : q // per_row + 1, at : at + height])
    sums = keep[: 2 * targets] + jnp.concatenate(rows, axis=0)
    own = place_ref[1] * (STRIDE // height) + place_ref[0]
    row = own * height + lax.broadcasted_iota(jnp.int32, (targets, height), 1)
    upstream = sums[targets:] + jnp.maximum(STRIDE - row, 0).astype(F32)
    downstream = keep[2 * targets :]
    insulation = sums[:targets] / (STRIDE * STRIDE)
    direction = (downstream - upstream) / (downstream + upstream)
    for t in range(targets):
        out_ref[t] = jnp.concatenate([insulation[t : t + 1], direction[t : t + 1]], axis=0)


def per_device(
    genome_bases,
    stitch_weight,
    stem_weight,
    trunk_in,
    trunk_out,
    pair_weight,
    distance_rate,
    tower_conv,
    tower_mix,
    head_weight,
):
    towers = lax.axis_size("tower")
    height = STRIDE // towers
    tower_index = lax.axis_index("tower")
    genome_index = lax.axis_index("genome")
    own = stem(genome_bases, stem_weight)
    features = lax.all_gather(own, "genome")
    groups = (3, 4)
    channels = distance_rate.shape[0]
    targets = head_weight.shape[0]
    conv_a = banded(tower_conv[0], groups[0])
    conv_b = banded(tower_conv[1], groups[1])
    mix_a = block_diagonal(tower_mix[0], groups[0])
    mix_b = block_diagonal(tower_mix[1], groups[1])
    head = head_by_row(head_weight, height)
    row_weight = lax.dynamic_slice_in_dim(
        stitch_weight.reshape(BLOCKS, STRIDE), tower_index * height, height, axis=1
    )
    row_weight = jnp.where(jnp.arange(BLOCKS)[:, None] <= genome_index, row_weight, 0)
    row_weight = jnp.broadcast_to(row_weight.astype(F32)[:, :, None], (BLOCKS, height, LANES))
    place = jnp.stack([tower_index, genome_index]).astype(jnp.int32)
    lanes = segments(2)[2]
    slots = lax.axis_size("genome") * towers
    packs = -(-2 * targets * height // LANES)
    vmem = pl.BlockSpec(memory_space=pltpu.VMEM)
    smem = pl.BlockSpec(memory_space=pltpu.SMEM)
    stitched, keep, send = pl.pallas_call(
        functools.partial(main_kernel, height, groups),
        out_shape=[
            jax.ShapeDtypeStruct((targets, height, BINS), F32),
            jax.ShapeDtypeStruct((3 * targets, LANES), F32),
            jax.ShapeDtypeStruct((slots, packs, LANES), F32),
        ],
        in_specs=[smem] + [vmem] * 11,
        out_specs=[vmem] * 3,
        scratch_shapes=[
            pltpu.VMEM(((height + 4) * 3 * channels, lanes), BF16),
            pltpu.VMEM(((height + 2) * 3 * channels, lanes), BF16),
            pltpu.VMEM((height * channels, lanes), F32),
            pltpu.VMEM((height * channels, lanes), BF16),
        ],
        compiler_params=pltpu.CompilerParams(vmem_limit_bytes=VMEM_BYTES),
        name="windows",
    )(
        place,
        features,
        trunk_in,
        trunk_out,
        pair_weight,
        distance_rate.reshape(channels, 1),
        conv_a,
        conv_b,
        mix_a,
        mix_b,
        head,
        row_weight,
    )
    got = lax.all_to_all(send, ("genome", "tower"), 0, 0, tiled=True)
    scores = pl.pallas_call(
        functools.partial(finish_kernel, height),
        out_shape=jax.ShapeDtypeStruct((targets, 2, height), F32),
        in_specs=[smem, vmem, vmem],
        out_specs=vmem,
        name="finish",
    )(place, keep, got)
    return (stitched, jnp.transpose(scores, (1, 0, 2)))


def solution(mesh):
    placed = (P("genome"), P(), P(), P(), P(), P(), P(), P(), P(), P())
    return jax.shard_map(
        per_device,
        mesh=mesh,
        in_specs=placed,
        out_specs=(P(None, ("genome", "tower"), None), P(None, None, ("genome", "tower"))),
        check_vma=False,
    )
```

```python
import functools

import jax
import jax.numpy as jnp
from jax import lax
from jax.experimental import pallas as pl
from jax.experimental.pallas import tpu as pltpu
from jax.sharding import PartitionSpec as P

BP = 2048
STRIDE = 64
BINS = 256
BLOCKS = BINS // STRIDE
LANES = 128
F32 = jnp.float32
BF16 = jnp.bfloat16
VMEM_BYTES = 48 * 1024 * 1024


def dot(a, b):
    return jnp.dot(a, b, preferred_element_type=F32)


def stem_kernel(bins, bases_hbm, weight_hbm, out_ref, bases, weight, base_sem, weight_sem):
    groups = BP // LANES
    chunks = weight.shape[0]
    span = weight.shape[2]
    base_copy = pltpu.make_async_copy(bases_hbm, bases, base_sem)
    base_copy.start()
    copies = []
    for k in range(chunks):
        copy = pltpu.make_async_copy(
            weight_hbm.at[:, pl.ds(k * span, span)], weight.at[k], weight_sem.at[k]
        )
        copy.start()
        copies.append(copy)
    row = lax.broadcasted_iota(jnp.int32, (LANES, 4 * LANES), 0)
    col = lax.broadcasted_iota(jnp.int32, (LANES, 4 * LANES), 1)
    repeat = (row == col // 4).astype(F32).astype(BF16)
    letter = (lax.broadcasted_iota(jnp.int32, (bins, 4 * LANES), 1) % 4).astype(F32)
    base_copy.wait()
    total = None
    per_chunk = groups // chunks
    for k in range(chunks):
        hot = []
        for q in range(per_chunk):
            rows = bases[pl.ds(k * per_chunk + q, bins, stride=groups), :]
            spread = dot(rows.astype(F32).astype(BF16), repeat)
            hot.append(jnp.where(spread == letter, 1.0, 0.0).astype(BF16))
        hot = jnp.concatenate(hot, axis=1)
        copies[k].wait()
        part = lax.dot_general(
            weight[k], hot, (((1,), (1,)), ((), ())), preferred_element_type=F32
        )
        total = part if total is None else total + part
    total = total.astype(BF16)
    half = out_ref.shape[1]
    packed = jnp.concatenate([total[:half], total[half:]], axis=1)
    for slot in range(out_ref.shape[0]):
        out_ref[slot] = packed


def stem(genome_bases, stem_weight, slots):
    bins = genome_bases.shape[0] // BP
    channels, depth = stem_weight.shape
    chunks = 4
    return pl.pallas_call(
        functools.partial(stem_kernel, bins),
        out_shape=jax.ShapeDtypeStruct((slots, channels // 2, 2 * bins), BF16),
        in_specs=[pl.BlockSpec(memory_space=pltpu.HBM)] * 2,
        out_specs=pl.BlockSpec(memory_space=pltpu.VMEM),
        scratch_shapes=[
            pltpu.VMEM((genome_bases.shape[0] // LANES, LANES), jnp.int32),
            pltpu.VMEM((chunks, channels, depth // chunks), BF16),
            pltpu.SemaphoreType.DMA,
            pltpu.SemaphoreType.DMA((chunks,)),
        ],
        compiler_params=pltpu.CompilerParams(vmem_limit_bytes=63 * 1024 * 1024),
        name="stem",
    )(genome_bases.reshape(-1, LANES), stem_weight)


def banded(kernel, rows):
    taps, out_channels, depth = kernel.shape
    flat = jnp.concatenate([kernel[u] for u in range(taps)], axis=1)
    bands = []
    for r in range(rows):
        parts = [flat]
        if r:
            parts.insert(0, jnp.zeros((out_channels, r * depth), BF16))
        if rows - 1 - r:
            parts.append(jnp.zeros((out_channels, (rows - 1 - r) * depth), BF16))
        bands.append(jnp.concatenate(parts, axis=1) if len(parts) > 1 else flat)
    return jnp.concatenate(bands, axis=0)


def block_diagonal(matrix, count):
    height, width = matrix.shape
    tiled = jnp.concatenate([jnp.concatenate([matrix] * count, axis=1)] * count, axis=0)
    row = lax.broadcasted_iota(jnp.int32, tiled.shape, 0) // height
    col = lax.broadcasted_iota(jnp.int32, tiled.shape, 1) // width
    return jnp.where(row == col, tiled, jnp.zeros((), BF16))


def head_by_row(head, count):
    targets, width = head.shape
    wide = jnp.concatenate([head] * count, axis=1)
    tall = jnp.broadcast_to(wide[:, None, :], (targets, count, count * width))
    row = lax.broadcasted_iota(jnp.int32, tall.shape, 1)
    col = lax.broadcasted_iota(jnp.int32, tall.shape, 2) // width
    return jnp.where(row == col, tall, jnp.zeros((), BF16)).reshape(targets * count, count * width)


def segments(margin):
    sizes = [BINS - STRIDE * b + margin + 1 for b in range(BLOCKS)]
    offsets = [sum(sizes[:b]) for b in range(BLOCKS)]
    lanes = -(-sum(sizes) // LANES) * LANES
    return sizes, offsets, lanes


def shifted(values, offset):
    if offset == 0:
        return values
    channels, extent = values.shape
    edge = jnp.zeros((channels, abs(offset)), values.dtype)
    if offset >= 0:
        return jnp.concatenate([values[:, offset:], edge], axis=1)
    return jnp.concatenate([edge, values[:, : extent + offset]], axis=1)


def main_kernel(
    height,
    groups,
    place_ref,
    *refs,
):
    (
        features,
        trunk_in,
        trunk_out,
        pair_weight,
        rate_ref,
        conv_ref,
        mix_ref,
        head_ref,
        stitch_ref,
        stitched_ref,
        keep_ref,
        send_ref,
        taps_a,
        taps_b,
        grid_ref,
        final_ref,
    ) = refs
    margin = 2
    sizes, offsets, lanes = segments(margin)
    tower_row = place_ref[0] * height
    channels = rate_ref.shape[1]
    depth = 3 * channels
    conv_a = banded(conv_ref[0], groups[0])
    conv_b = banded(conv_ref[1], groups[1])
    mix_a = block_diagonal(mix_ref[0], groups[0])
    mix_b = block_diagonal(mix_ref[1], groups[1])
    head = head_by_row(head_ref[...], height)

    starts = features.shape[0]
    blocks = []
    for d in range(1 - BLOCKS, BLOCKS):
        at = place_ref[1] + d
        block = features[jnp.clip(at, 0, starts - 1)]
        blocks.append(jnp.where((at >= 0) & (at < starts), block, jnp.zeros_like(block)))
    blocks = jnp.concatenate(
        [
            jnp.concatenate([half[:, :STRIDE] for half in blocks], axis=1),
            jnp.concatenate([half[:, STRIDE:] for half in blocks], axis=1),
        ],
        axis=0,
    )
    extent = BINS
    windows = []
    for b in range(BLOCKS):
        first = (BLOCKS - 1 - b) * STRIDE
        windows.append(blocks[:, first : first + BINS].astype(F32))
    stream = jnp.concatenate(windows, axis=1)
    layers = trunk_in.shape[0]
    for layer in range(layers):
        dilation = max(1, extent // 2 ** (layers - layer))
        active = jax.nn.relu(stream)
        parts = [active[:, b * BINS : (b + 1) * BINS] for b in range(BLOCKS)]
        stacked = jnp.concatenate(
            [
                jnp.concatenate([shifted(p, o) for p in parts], axis=1).astype(BF16)
                for o in (-dilation, 0, dilation)
            ],
            axis=0,
        )
        inner = dot(trunk_in[layer], stacked)
        squeezed = jax.nn.relu(inner).astype(BF16)
        stream = stream + lax.dot_general(
            trunk_out[layer], squeezed, (((0,), (0,)), ((), ())), preferred_element_type=F32
        )
    projected = dot(pair_weight[...], jax.nn.relu(stream).astype(BF16))

    lane = lax.broadcasted_iota(jnp.int32, (1, lanes), 1)
    block_of = jnp.zeros((1, lanes), jnp.int32)
    start_of = jnp.zeros((1, lanes), jnp.int32)
    for b in range(1, BLOCKS):
        block_of = jnp.where(lane >= offsets[b], b, block_of)
        start_of = jnp.where(lane >= offsets[b], offsets[b], start_of)
    step = lane - start_of
    first_row = STRIDE * block_of + tower_row - margin
    column = first_row + step
    in_column = (column < BINS) & (column >= 0)

    right = []
    left = []
    for b in range(BLOCKS):
        begin = STRIDE * b + tower_row - margin
        turn = jnp.where(begin > 0, BINS - begin, -begin)
        terms = projected[:, b * BINS : (b + 1) * BINS]
        turned = pltpu.roll(terms, turn, 1)
        left.append(turned[:channels, :LANES])
        own = turned[channels:]
        if sizes[b] > BINS:
            own = jnp.concatenate([own, own[:, : sizes[b] - BINS]], axis=1)
        right.append(own[:, : sizes[b]])
    used = sum(sizes)
    if lanes > used:
        right.append(jnp.zeros((channels, lanes - used), F32))
    right = jnp.concatenate(right, axis=1)
    row = lax.broadcasted_iota(jnp.int32, (channels, channels), 0)
    col = lax.broadcasted_iota(jnp.int32, (channels, channels), 1)
    rate = jnp.sum(jnp.where(row == col, rate_ref[...], 0.0), axis=1, keepdims=True)
    rate = jnp.broadcast_to(rate, (channels, LANES))
    rate = jnp.concatenate([rate] * (lanes // LANES), axis=1)

    def place_taps(ref, slot, act):
        before = pltpu.roll(act, 1, 1)
        after = pltpu.roll(act, lanes - 1, 1)
        ref[pl.ds(slot * depth, channels), :] = before.astype(BF16)
        ref[pl.ds(slot * depth + channels, channels), :] = act.astype(BF16)
        ref[pl.ds(slot * depth + 2 * channels, channels), :] = after.astype(BF16)

    def inside(row):
        at = first_row + row
        return in_column & (at >= 0) & (at < BINS)

    for row in range(height + 2 * margin):
        apart = jnp.abs(step - row).astype(F32)
        decay = jnp.log1p(apart)
        tiles = []
        for tile in range(lanes // LANES):
            piece = None
            here = lane[:, tile * LANES : (tile + 1) * LANES]
            for b in range(BLOCKS):
                low, high = offsets[b], offsets[b] + sizes[b]
                if high <= tile * LANES or low >= (tile + 1) * LANES:
                    continue
                spread = jnp.broadcast_to(left[b][:, row : row + 1], (channels, LANES))
                piece = spread if piece is None else jnp.where(here >= low, spread, piece)
            tiles.append(piece)
        mixed = jnp.concatenate(tiles, axis=1) + right - rate * decay
        place_taps(taps_a, row, jnp.where(inside(row), jnp.maximum(mixed, 0.0), 0.0))

    span = groups[0]
    for group in range((height + 2) // span):
        first = group * span
        conv = dot(conv_a, taps_a[pl.ds(first * depth, (span + 2) * depth), :])
        update = dot(mix_a, jnp.maximum(conv, 0.0).astype(BF16))
        for r in range(span):
            row = first + r
            kept = taps_a[pl.ds((row + 1) * depth + channels, channels), :].astype(F32)
            grid = kept + update[r * channels : (r + 1) * channels]
            if 1 <= row <= height:
                grid_ref[pl.ds((row - 1) * channels, channels), :] = grid
            place_taps(taps_b, row, jnp.where(inside(row + 1), jnp.maximum(grid, 0.0), 0.0))
    span = groups[1]
    for group in range(height // span):
        first = group * span
        conv = dot(conv_b, taps_b[pl.ds(first * depth, (span + 2) * depth), :])
        update = dot(mix_b, jnp.maximum(conv, 0.0).astype(BF16))
        rows = pl.ds(first * channels, span * channels)
        final_ref[rows, :] = jnp.maximum(grid_ref[rows, :] + update, 0.0).astype(BF16)
    targets = head.shape[0] // height
    contact = dot(head, final_ref[...]).reshape(targets, height, lanes)

    local = lax.broadcasted_iota(jnp.int32, (height, BINS), 0)
    ahead = lax.broadcasted_iota(jnp.int32, (height, BINS), 1)
    weight_sum = jnp.zeros((height, BINS), F32)
    weights = []
    for b in range(BLOCKS):
        weight = jnp.where(ahead == STRIDE * b + tower_row + local, stitch_ref[...], 0)
        weight = jnp.sum(weight.astype(F32), axis=1, keepdims=True)
        weight = jnp.where(place_ref[1] >= b, weight, 0.0)
        reach = STRIDE * b + tower_row + local + ahead < BINS
        weight = jnp.where(reach, weight, 0.0)
        weights.append(weight)
        weight_sum = weight_sum + weight
    scale = 1.0 / jnp.maximum(weight_sum, 1.0)
    weights = [w * scale for w in weights]
    stitched = []
    map_row = lax.broadcasted_iota(jnp.int32, (height, lanes), 0)
    for t in range(targets):
        band = None
        skewed = contact[t]
        for bit in range((height - 1).bit_length()):
            turned = pltpu.roll(skewed, lanes - (1 << bit), 1)
            skewed = jnp.where((map_row >> bit) & 1 == 1, turned, skewed)
        for b in range(BLOCKS):
            first, reach = offsets[b] + margin, BINS - STRIDE * b
            piece = skewed[:, first : first + reach]
            if reach < BINS:
                piece = jnp.concatenate([piece, jnp.zeros((height, BINS - reach), F32)], axis=1)
            piece = piece * weights[b]
            band = piece if band is None else band + piece
        stitched_ref[t] = band
        stitched.append(band[:, : 2 * STRIDE])

    near = jnp.concatenate(stitched, axis=0)
    wide = 2 * STRIDE
    col = lax.broadcasted_iota(jnp.int32, (wide, wide), 0)
    corner = lax.broadcasted_iota(jnp.int32, (wide, wide), 1)
    box = ((col > corner) & (col <= corner + STRIDE) & (corner < STRIDE)).astype(F32)
    square = jnp.dot(near, box, preferred_element_type=F32, precision=lax.Precision.HIGHEST)
    at = lax.broadcasted_iota(jnp.int32, near.shape, 1)
    contact = jnp.where((at >= 1) & (at <= STRIDE), jnp.exp(near), 0.0)
    down = jnp.sum(contact, axis=1, keepdims=True)
    here = lax.broadcasted_iota(jnp.int32, (height, wide), 0)
    there = lax.broadcasted_iota(jnp.int32, (height, wide), 1)

    def by_row(values):
        rows = []
        for t in range(targets):
            own = pltpu.roll(
                values[t * height : (t + 1) * height], 0, 1, stride=1, stride_axis=0
            )
            rows.append(jnp.sum(own, axis=0, keepdims=True))
        return rows

    down_rows = []
    for t in range(targets):
        own = jnp.where(here == there, down[t * height : (t + 1) * height], 0.0)
        down_rows.append(jnp.sum(own, axis=0, keepdims=True))
    rows = by_row(square) + by_row(contact)
    keep_ref[...] = jnp.concatenate(rows + down_rows, axis=0)
    per_row = LANES // height
    first = lax.broadcasted_iota(jnp.int32, (per_row, LANES), 1) < height
    packs = [
        jnp.concatenate(
            rows[p : p + per_row]
            + [jnp.zeros((1, LANES), F32)] * (per_row - len(rows[p : p + per_row])),
            axis=0,
        )
        for p in range(0, len(rows), per_row)
    ]
    for k in range(1, STRIDE // height + 1):
        packed = []
        for pack in packs:
            turned = jnp.where(first, pltpu.roll(pack, LANES - k * height, 1), 0.0)
            turned = pltpu.roll(turned, 0, 1, stride=height, stride_axis=0)
            packed.append(jnp.sum(turned, axis=0, keepdims=True))

        send_ref[lax.rem(place_ref[0] + k, STRIDE // height)] = jnp.concatenate(packed, axis=0)


def finish_kernel(height, place_ref, keep_ref, near_ref, far_ref, out_ref):
    targets = out_ref.shape[0]
    per_row = LANES // height
    keep = keep_ref[...][:, :height]
    got = near_ref[...] + far_ref[...]
    rows = []
    for q in range(2 * targets):
        at = (q % per_row) * height
        rows.append(got[q // per_row : q // per_row + 1, at : at + height])
    sums = keep[: 2 * targets] + jnp.concatenate(rows, axis=0)
    own = place_ref[1] * (STRIDE // height) + place_ref[0]
    row = own * height + lax.broadcasted_iota(jnp.int32, (targets, height), 1)
    upstream = sums[targets:] + jnp.maximum(STRIDE - row, 0).astype(F32)
    downstream = keep[2 * targets :]
    insulation = sums[:targets] / (STRIDE * STRIDE)
    direction = (downstream - upstream) / (downstream + upstream)
    for t in range(targets):
        out_ref[t] = jnp.concatenate([insulation[t : t + 1], direction[t : t + 1]], axis=0)


def per_device(
    genome_bases,
    stitch_weight,
    stem_weight,
    trunk_in,
    trunk_out,
    pair_weight,
    distance_rate,
    tower_conv,
    tower_mix,
    head_weight,
):
    towers = lax.axis_size("tower")
    height = STRIDE // towers
    tower_index = lax.axis_index("tower")
    genome_index = lax.axis_index("genome")
    own = stem(genome_bases, stem_weight, lax.axis_size("genome"))
    features = lax.all_to_all(own, "genome", 0, 0, tiled=True)
    groups = (3, 4)
    channels = distance_rate.shape[0]
    targets = head_weight.shape[0]
    place = jnp.stack([tower_index, genome_index]).astype(jnp.int32)
    lanes = segments(2)[2]
    packs = -(-2 * targets * height // LANES)
    vmem = pl.BlockSpec(memory_space=pltpu.VMEM)
    smem = pl.BlockSpec(memory_space=pltpu.SMEM)
    stitched, keep, send = pl.pallas_call(
        functools.partial(main_kernel, height, groups),
        out_shape=[
            jax.ShapeDtypeStruct((targets, height, BINS), F32),
            jax.ShapeDtypeStruct((3 * targets, LANES), F32),
            jax.ShapeDtypeStruct((towers, packs, LANES), F32),
        ],
        in_specs=[smem] + [vmem] * 9,
        out_specs=[vmem] * 3,
        scratch_shapes=[
            pltpu.VMEM(((height + 4) * 3 * channels, lanes), BF16),
            pltpu.VMEM(((height + 2) * 3 * channels, lanes), BF16),
            pltpu.VMEM((height * channels, lanes), F32),
            pltpu.VMEM((height * channels, lanes), BF16),
        ],
        compiler_params=pltpu.CompilerParams(vmem_limit_bytes=VMEM_BYTES),
        name="windows",
    )(
        place,
        features,
        trunk_in,
        jnp.transpose(trunk_out, (0, 2, 1)),
        pair_weight,
        distance_rate.reshape(1, channels),
        tower_conv,
        tower_mix,
        head_weight,
        stitch_weight.reshape(1, BINS),
    )
    got = lax.all_to_all(send, "tower", 0, 0, tiled=True)
    before = (jnp.arange(towers) < tower_index)[:, None, None]
    near = jnp.sum(jnp.where(before, got, 0.0), axis=0)
    far = jnp.sum(jnp.where(before, 0.0, got), axis=0)
    starts = lax.axis_size("genome")
    far = lax.ppermute(far, "genome", [(i, i + 1) for i in range(starts - 1)])
    scores = pl.pallas_call(
        functools.partial(finish_kernel, height),
        out_shape=jax.ShapeDtypeStruct((targets, 2, height), F32),
        in_specs=[smem, vmem, vmem, vmem],
        out_specs=vmem,
        name="finish",
    )(place, keep, near, far)
    return (stitched, jnp.transpose(scores, (1, 0, 2)))


def solution(mesh):
    placed = (P("genome"), P(), P(), P(), P(), P(), P(), P(), P(), P())
    return jax.shard_map(
        per_device,
        mesh=mesh,
        in_specs=placed,
        out_specs=(P(None, ("genome", "tower"), None), P(None, None, ("genome", "tower"))),
        check_vma=False,
    )
```

```python
import functools

import jax
import jax.numpy as jnp
from jax import lax
from jax.experimental import pallas as pl
from jax.experimental.pallas import tpu as pltpu
from jax.sharding import PartitionSpec as P

BP = 2048
STRIDE = 64
BINS = 256
BLOCKS = BINS // STRIDE
LANES = 128
F32 = jnp.float32
BF16 = jnp.bfloat16
VMEM_BYTES = 48 * 1024 * 1024


def dot(a, b):
    return jnp.dot(a, b, preferred_element_type=F32)


def stem_kernel(bins, bases_hbm, weight_hbm, out_ref, bases, weight, base_sem, weight_sem):
    groups = BP // LANES
    chunks = weight.shape[0]
    span = weight.shape[2]
    base_copy = pltpu.make_async_copy(bases_hbm, bases, base_sem)
    base_copy.start()
    copies = []
    for k in range(chunks):
        copy = pltpu.make_async_copy(
            weight_hbm.at[:, pl.ds(k * span, span)], weight.at[k], weight_sem.at[k]
        )
        copy.start()
        copies.append(copy)
    row = lax.broadcasted_iota(jnp.int32, (LANES, 4 * LANES), 0)
    col = lax.broadcasted_iota(jnp.int32, (LANES, 4 * LANES), 1)
    repeat = (row == col // 4).astype(F32).astype(BF16)
    letter = (lax.broadcasted_iota(jnp.int32, (bins, 4 * LANES), 1) % 4).astype(F32)
    base_copy.wait()
    total = None
    per_chunk = groups // chunks
    for k in range(chunks):
        hot = []
        for q in range(per_chunk):
            rows = bases[pl.ds(k * per_chunk + q, bins, stride=groups), :]
            spread = dot(rows.astype(F32).astype(BF16), repeat)
            hot.append(jnp.where(spread == letter, 1.0, 0.0).astype(BF16))
        hot = jnp.concatenate(hot, axis=1)
        copies[k].wait()
        part = lax.dot_general(
            weight[k], hot, (((1,), (1,)), ((), ())), preferred_element_type=F32
        )
        total = part if total is None else total + part
    total = total.astype(BF16)
    half = out_ref.shape[1]
    packed = jnp.concatenate([total[:half], total[half:]], axis=1)
    for slot in range(out_ref.shape[0]):
        out_ref[slot] = packed


def stem(genome_bases, stem_weight, slots):
    bins = genome_bases.shape[0] // BP
    channels, depth = stem_weight.shape
    chunks = 4
    return pl.pallas_call(
        functools.partial(stem_kernel, bins),
        out_shape=jax.ShapeDtypeStruct((slots, channels // 2, 2 * bins), BF16),
        in_specs=[pl.BlockSpec(memory_space=pltpu.HBM)] * 2,
        out_specs=pl.BlockSpec(memory_space=pltpu.VMEM),
        scratch_shapes=[
            pltpu.VMEM((genome_bases.shape[0] // LANES, LANES), jnp.int32),
            pltpu.VMEM((chunks, channels, depth // chunks), BF16),
            pltpu.SemaphoreType.DMA,
            pltpu.SemaphoreType.DMA((chunks,)),
        ],
        compiler_params=pltpu.CompilerParams(vmem_limit_bytes=63 * 1024 * 1024),
        name="stem",
    )(genome_bases.reshape(-1, LANES), stem_weight)


def banded(kernel, rows):
    taps, out_channels, depth = kernel.shape
    flat = jnp.concatenate([kernel[u] for u in range(taps)], axis=1)
    bands = []
    for r in range(rows):
        parts = [flat]
        if r:
            parts.insert(0, jnp.zeros((out_channels, r * depth), BF16))
        if rows - 1 - r:
            parts.append(jnp.zeros((out_channels, (rows - 1 - r) * depth), BF16))
        bands.append(jnp.concatenate(parts, axis=1) if len(parts) > 1 else flat)
    return jnp.concatenate(bands, axis=0)


def block_diagonal(matrix, count):
    height, width = matrix.shape
    tiled = jnp.concatenate([jnp.concatenate([matrix] * count, axis=1)] * count, axis=0)
    row = lax.broadcasted_iota(jnp.int32, tiled.shape, 0) // height
    col = lax.broadcasted_iota(jnp.int32, tiled.shape, 1) // width
    return jnp.where(row == col, tiled, jnp.zeros((), BF16))


def head_by_row(head, count):
    targets, width = head.shape
    wide = jnp.concatenate([head] * count, axis=1)
    tall = jnp.broadcast_to(wide[:, None, :], (targets, count, count * width))
    row = lax.broadcasted_iota(jnp.int32, tall.shape, 1)
    col = lax.broadcasted_iota(jnp.int32, tall.shape, 2) // width
    return jnp.where(row == col, tall, jnp.zeros((), BF16)).reshape(targets * count, count * width)


def segments(margin):
    sizes = [BINS - STRIDE * b + margin + 1 for b in range(BLOCKS)]
    offsets = [sum(sizes[:b]) for b in range(BLOCKS)]
    lanes = -(-sum(sizes) // LANES) * LANES
    return sizes, offsets, lanes


def shifted(values, offset):
    if offset == 0:
        return values
    channels, extent = values.shape
    edge = jnp.zeros((channels, abs(offset)), values.dtype)
    if offset >= 0:
        return jnp.concatenate([values[:, offset:], edge], axis=1)
    return jnp.concatenate([edge, values[:, : extent + offset]], axis=1)


def main_kernel(
    height,
    groups,
    place_ref,
    *refs,
):
    (
        features,
        trunk_in,
        trunk_out,
        pair_weight,
        rate_ref,
        conv_ref,
        mix_ref,
        head_ref,
        stitch_ref,
        stitched_ref,
        keep_ref,
        send_ref,
        taps_a,
        taps_b,
        grid_ref,
        final_ref,
    ) = refs
    margin = 2
    sizes, offsets, lanes = segments(margin)
    tower_row = place_ref[0] * height
    channels = rate_ref.shape[1]
    depth = 3 * channels
    spans_a = {groups, (height + 2) % groups} - {0}
    spans_b = {groups, height % groups} - {0}
    conv_a = {span: banded(conv_ref[0], span) for span in sorted(spans_a)}
    conv_b = {span: banded(conv_ref[1], span) for span in sorted(spans_b)}
    mix_a = {span: block_diagonal(mix_ref[0], span) for span in sorted(spans_a)}
    mix_b = {span: block_diagonal(mix_ref[1], span) for span in sorted(spans_b)}
    head = head_by_row(head_ref[...], height)

    starts = features.shape[0]
    blocks = []
    for d in range(1 - BLOCKS, BLOCKS):
        at = place_ref[1] + d
        block = features[jnp.clip(at, 0, starts - 1)]
        blocks.append(jnp.where((at >= 0) & (at < starts), block, jnp.zeros_like(block)))
    blocks = jnp.concatenate(
        [
            jnp.concatenate([half[:, :STRIDE] for half in blocks], axis=1),
            jnp.concatenate([half[:, STRIDE:] for half in blocks], axis=1),
        ],
        axis=0,
    )
    extent = BINS
    windows = []
    for b in range(BLOCKS):
        first = (BLOCKS - 1 - b) * STRIDE
        windows.append(blocks[:, first : first + BINS].astype(F32))
    stream = jnp.concatenate(windows, axis=1)
    layers = trunk_in.shape[0]
    for layer in range(layers):
        dilation = max(1, extent // 2 ** (layers - layer))
        active = jax.nn.relu(stream)
        parts = [active[:, b * BINS : (b + 1) * BINS] for b in range(BLOCKS)]
        stacked = jnp.concatenate(
            [
                jnp.concatenate([shifted(p, o) for p in parts], axis=1).astype(BF16)
                for o in (-dilation, 0, dilation)
            ],
            axis=0,
        )
        inner = dot(trunk_in[layer], stacked)
        squeezed = jax.nn.relu(inner).astype(BF16)
        stream = stream + lax.dot_general(
            trunk_out[layer], squeezed, (((0,), (0,)), ((), ())), preferred_element_type=F32
        )
    projected = dot(pair_weight[...], jax.nn.relu(stream).astype(BF16))

    lane = lax.broadcasted_iota(jnp.int32, (1, lanes), 1)
    block_of = jnp.zeros((1, lanes), jnp.int32)
    start_of = jnp.zeros((1, lanes), jnp.int32)
    for b in range(1, BLOCKS):
        block_of = jnp.where(lane >= offsets[b], b, block_of)
        start_of = jnp.where(lane >= offsets[b], offsets[b], start_of)
    step = lane - start_of
    first_row = STRIDE * block_of + tower_row - margin
    column = first_row + step
    in_column = (column < BINS) & (column >= 0)

    right = []
    left = []
    for b in range(BLOCKS):
        begin = STRIDE * b + tower_row - margin
        turn = jnp.where(begin > 0, BINS - begin, -begin)
        terms = projected[:, b * BINS : (b + 1) * BINS]
        turned = pltpu.roll(terms, turn, 1)
        left.append(turned[:channels, :LANES])
        own = turned[channels:]
        if sizes[b] > BINS:
            own = jnp.concatenate([own, own[:, : sizes[b] - BINS]], axis=1)
        right.append(own[:, : sizes[b]])
    used = sum(sizes)
    if lanes > used:
        right.append(jnp.zeros((channels, lanes - used), F32))
    right = jnp.concatenate(right, axis=1)
    row = lax.broadcasted_iota(jnp.int32, (channels, channels), 0)
    col = lax.broadcasted_iota(jnp.int32, (channels, channels), 1)
    rate = jnp.sum(jnp.where(row == col, rate_ref[...], 0.0), axis=1, keepdims=True)
    rate = jnp.broadcast_to(rate, (channels, LANES))
    rate = jnp.concatenate([rate] * (lanes // LANES), axis=1)

    def place_taps(ref, slot, act):
        before = pltpu.roll(act, 1, 1)
        after = pltpu.roll(act, lanes - 1, 1)
        ref[pl.ds(slot * depth, channels), :] = before.astype(BF16)
        ref[pl.ds(slot * depth + channels, channels), :] = act.astype(BF16)
        ref[pl.ds(slot * depth + 2 * channels, channels), :] = after.astype(BF16)

    def inside(row):
        at = first_row + row
        return in_column & (at >= 0) & (at < BINS)

    for row in range(height + 2 * margin):
        apart = jnp.abs(step - row).astype(F32)
        decay = jnp.log1p(apart)
        tiles = []
        for tile in range(lanes // LANES):
            piece = None
            here = lane[:, tile * LANES : (tile + 1) * LANES]
            for b in range(BLOCKS):
                low, high = offsets[b], offsets[b] + sizes[b]
                if high <= tile * LANES or low >= (tile + 1) * LANES:
                    continue
                spread = jnp.broadcast_to(left[b][:, row : row + 1], (channels, LANES))
                piece = spread if piece is None else jnp.where(here >= low, spread, piece)
            tiles.append(piece)
        mixed = jnp.concatenate(tiles, axis=1) + right - rate * decay
        place_taps(taps_a, row, jnp.where(inside(row), jnp.maximum(mixed, 0.0), 0.0))

    for first in range(0, height + 2, groups):
        span = min(groups, height + 2 - first)
        conv = dot(conv_a[span], taps_a[pl.ds(first * depth, (span + 2) * depth), :])
        update = dot(mix_a[span], jnp.maximum(conv, 0.0).astype(BF16))
        for r in range(span):
            row = first + r
            kept = taps_a[pl.ds((row + 1) * depth + channels, channels), :].astype(F32)
            grid = kept + update[r * channels : (r + 1) * channels]
            if 1 <= row <= height:
                grid_ref[pl.ds((row - 1) * channels, channels), :] = grid
            place_taps(taps_b, row, jnp.where(inside(row + 1), jnp.maximum(grid, 0.0), 0.0))
    for first in range(0, height, groups):
        span = min(groups, height - first)
        conv = dot(conv_b[span], taps_b[pl.ds(first * depth, (span + 2) * depth), :])
        update = dot(mix_b[span], jnp.maximum(conv, 0.0).astype(BF16))
        rows = pl.ds(first * channels, span * channels)
        final_ref[rows, :] = jnp.maximum(grid_ref[rows, :] + update, 0.0).astype(BF16)
    targets = head.shape[0] // height
    contact = dot(head, final_ref[...]).reshape(targets, height, lanes)

    local = lax.broadcasted_iota(jnp.int32, (height, BINS), 0)
    ahead = lax.broadcasted_iota(jnp.int32, (height, BINS), 1)
    weight_sum = jnp.zeros((height, BINS), F32)
    weights = []
    for b in range(BLOCKS):
        weight = jnp.where(ahead == STRIDE * b + tower_row + local, stitch_ref[...], 0)
        weight = jnp.sum(weight.astype(F32), axis=1, keepdims=True)
        weight = jnp.where(place_ref[1] >= b, weight, 0.0)
        reach = STRIDE * b + tower_row + local + ahead < BINS
        weight = jnp.where(reach, weight, 0.0)
        weights.append(weight)
        weight_sum = weight_sum + weight
    scale = 1.0 / jnp.maximum(weight_sum, 1.0)
    weights = [w * scale for w in weights]
    stitched = []
    map_row = lax.broadcasted_iota(jnp.int32, (height, lanes), 0)
    for t in range(targets):
        band = None
        skewed = contact[t]
        for bit in range((height - 1).bit_length()):
            turned = pltpu.roll(skewed, lanes - (1 << bit), 1)
            skewed = jnp.where((map_row >> bit) & 1 == 1, turned, skewed)
        for b in range(BLOCKS):
            first, reach = offsets[b] + margin, BINS - STRIDE * b
            piece = skewed[:, first : first + reach]
            if reach < BINS:
                piece = jnp.concatenate([piece, jnp.zeros((height, BINS - reach), F32)], axis=1)
            piece = piece * weights[b]
            band = piece if band is None else band + piece
        stitched_ref[t] = band
        stitched.append(band[:, : 2 * STRIDE])

    near = jnp.concatenate(stitched, axis=0)
    wide = 2 * STRIDE
    col = lax.broadcasted_iota(jnp.int32, (wide, wide), 0)
    corner = lax.broadcasted_iota(jnp.int32, (wide, wide), 1)
    box = ((col > corner) & (col <= corner + STRIDE) & (corner < STRIDE)).astype(F32)
    square = jnp.dot(near, box, preferred_element_type=F32, precision=lax.Precision.HIGHEST)
    at = lax.broadcasted_iota(jnp.int32, near.shape, 1)
    contact = jnp.where((at >= 1) & (at <= STRIDE), jnp.exp(near), 0.0)
    down = jnp.sum(contact, axis=1, keepdims=True)
    here = lax.broadcasted_iota(jnp.int32, (height, wide), 0)
    there = lax.broadcasted_iota(jnp.int32, (height, wide), 1)

    def by_row(values):
        rows = []
        for t in range(targets):
            own = pltpu.roll(
                values[t * height : (t + 1) * height], 0, 1, stride=1, stride_axis=0
            )
            rows.append(jnp.sum(own, axis=0, keepdims=True))
        return rows

    down_rows = []
    for t in range(targets):
        own = jnp.where(here == there, down[t * height : (t + 1) * height], 0.0)
        down_rows.append(jnp.sum(own, axis=0, keepdims=True))
    rows = by_row(square) + by_row(contact)
    keep_ref[...] = jnp.concatenate(rows + down_rows, axis=0)
    per_row = LANES // height
    first = lax.broadcasted_iota(jnp.int32, (per_row, LANES), 1) < height
    packs = [
        jnp.concatenate(
            rows[p : p + per_row]
            + [jnp.zeros((1, LANES), F32)] * (per_row - len(rows[p : p + per_row])),
            axis=0,
        )
        for p in range(0, len(rows), per_row)
    ]
    for k in range(1, STRIDE // height + 1):
        packed = []
        for pack in packs:
            turned = jnp.where(first, pltpu.roll(pack, LANES - k * height, 1), 0.0)
            turned = pltpu.roll(turned, 0, 1, stride=height, stride_axis=0)
            packed.append(jnp.sum(turned, axis=0, keepdims=True))

        send_ref[lax.rem(place_ref[0] + k, STRIDE // height)] = jnp.concatenate(packed, axis=0)


def finish_kernel(height, place_ref, keep_ref, got_ref, out_ref):
    targets = out_ref.shape[0]
    per_row = LANES // height
    keep = keep_ref[...][:, :height]
    got = jnp.sum(got_ref[...], axis=0)
    rows = []
    for q in range(2 * targets):
        at = (q % per_row) * height
        rows.append(got[q // per_row : q // per_row + 1, at : at + height])
    sums = keep[: 2 * targets] + jnp.concatenate(rows, axis=0)
    own = place_ref[1] * (STRIDE // height) + place_ref[0]
    row = own * height + lax.broadcasted_iota(jnp.int32, (targets, height), 1)
    upstream = sums[targets:] + jnp.maximum(STRIDE - row, 0).astype(F32)
    downstream = keep[2 * targets :]
    insulation = sums[:targets] / (STRIDE * STRIDE)
    direction = (downstream - upstream) / (downstream + upstream)
    for t in range(targets):
        out_ref[t] = jnp.concatenate([insulation[t : t + 1], direction[t : t + 1]], axis=0)


def per_device(
    genome_bases,
    stitch_weight,
    stem_weight,
    trunk_in,
    trunk_out,
    pair_weight,
    distance_rate,
    tower_conv,
    tower_mix,
    head_weight,
):
    towers = lax.axis_size("tower")
    height = STRIDE // towers
    tower_index = lax.axis_index("tower")
    genome_index = lax.axis_index("genome")
    own = stem(genome_bases, stem_weight, lax.axis_size("genome"))
    features = lax.all_to_all(own, "genome", 0, 0, tiled=True)
    groups = 3
    channels = distance_rate.shape[0]
    targets = head_weight.shape[0]
    place = jnp.stack([tower_index, genome_index]).astype(jnp.int32)
    lanes = segments(2)[2]
    packs = -(-2 * targets * height // LANES)
    vmem = pl.BlockSpec(memory_space=pltpu.VMEM)
    smem = pl.BlockSpec(memory_space=pltpu.SMEM)
    stitched, keep, send = pl.pallas_call(
        functools.partial(main_kernel, height, groups),
        out_shape=[
            jax.ShapeDtypeStruct((targets, height, BINS), F32),
            jax.ShapeDtypeStruct((3 * targets, LANES), F32),
            jax.ShapeDtypeStruct((towers, packs, LANES), F32),
        ],
        in_specs=[smem] + [vmem] * 9,
        out_specs=[vmem] * 3,
        scratch_shapes=[
            pltpu.VMEM(((height + 4) * 3 * channels, lanes), BF16),
            pltpu.VMEM(((height + 2) * 3 * channels, lanes), BF16),
            pltpu.VMEM((height * channels, lanes), F32),
            pltpu.VMEM((height * channels, lanes), BF16),
        ],
        compiler_params=pltpu.CompilerParams(vmem_limit_bytes=VMEM_BYTES),
        name="windows",
    )(
        place,
        features,
        trunk_in,
        jnp.transpose(trunk_out, (0, 2, 1)),
        pair_weight,
        distance_rate.reshape(1, channels),
        tower_conv,
        tower_mix,
        head_weight,
        stitch_weight.reshape(1, BINS),
    )
    starts = lax.axis_size("genome")
    passed = lax.ppermute(send, "genome", [(i, i + 1) for i in range(starts - 1)])
    ahead = (jnp.arange(towers) > tower_index)[:, None, None]
    got = lax.all_to_all(jnp.where(ahead, send, passed), "tower", 0, 0, tiled=True)
    scores = pl.pallas_call(
        functools.partial(finish_kernel, height),
        out_shape=jax.ShapeDtypeStruct((targets, 2, height), F32),
        in_specs=[smem, vmem, vmem],
        out_specs=vmem,
        compiler_params=pltpu.CompilerParams(vmem_limit_bytes=2 * 1024 * 1024),
        name="finish",
    )(place, keep, got)
    return (stitched, jnp.transpose(scores, (1, 0, 2)))


def solution(mesh):
    placed = (P("genome"), P(), P(), P(), P(), P(), P(), P(), P(), P())
    return jax.shard_map(
        per_device,
        mesh=mesh,
        in_specs=placed,
        out_specs=(P(None, ("genome", "tower"), None), P(None, None, ("genome", "tower"))),
        check_vma=False,
    )
```

```python
import functools

import jax
import jax.numpy as jnp
from jax import lax
from jax.experimental import pallas as pl
from jax.experimental.pallas import tpu as pltpu
from jax.sharding import PartitionSpec as P

BP = 2048
STRIDE = 64
BINS = 256
BLOCKS = BINS // STRIDE
LANES = 128
F32 = jnp.float32
BF16 = jnp.bfloat16
VMEM_BYTES = 48 * 1024 * 1024


def dot(a, b):
    return jnp.dot(a, b, preferred_element_type=F32)


def stem_kernel(bins, bases_hbm, weight_hbm, out_ref, bases, weight, base_sem, weight_sem):
    groups = BP // LANES
    chunks = weight.shape[0]
    span = weight.shape[2]
    base_copy = pltpu.make_async_copy(bases_hbm, bases, base_sem)
    base_copy.start()
    copies = []
    for k in range(chunks):
        copy = pltpu.make_async_copy(
            weight_hbm.at[:, pl.ds(k * span, span)], weight.at[k], weight_sem.at[k]
        )
        copy.start()
        copies.append(copy)
    row = lax.broadcasted_iota(jnp.int32, (LANES, 4 * LANES), 0)
    col = lax.broadcasted_iota(jnp.int32, (LANES, 4 * LANES), 1)
    repeat = (row == col // 4).astype(F32).astype(BF16)
    letter = (lax.broadcasted_iota(jnp.int32, (bins, 4 * LANES), 1) % 4).astype(F32)
    base_copy.wait()
    total = None
    per_chunk = groups // chunks
    for k in range(chunks):
        hot = []
        for q in range(per_chunk):
            rows = bases[pl.ds(k * per_chunk + q, bins, stride=groups), :]
            spread = dot(rows.astype(F32).astype(BF16), repeat)
            hot.append(jnp.where(spread == letter, 1.0, 0.0).astype(BF16))
        hot = jnp.concatenate(hot, axis=1)
        copies[k].wait()
        part = lax.dot_general(
            weight[k], hot, (((1,), (1,)), ((), ())), preferred_element_type=F32
        )
        total = part if total is None else total + part
    total = total.astype(BF16)
    half = out_ref.shape[1]
    packed = jnp.concatenate([total[:half], total[half:]], axis=1)
    for slot in range(out_ref.shape[0]):
        out_ref[slot] = packed


def stem(genome_bases, stem_weight, slots):
    bins = genome_bases.shape[0] // BP
    channels, depth = stem_weight.shape
    chunks = 4
    return pl.pallas_call(
        functools.partial(stem_kernel, bins),
        out_shape=jax.ShapeDtypeStruct((slots, channels // 2, 2 * bins), BF16),
        in_specs=[pl.BlockSpec(memory_space=pltpu.HBM)] * 2,
        out_specs=pl.BlockSpec(memory_space=pltpu.VMEM),
        scratch_shapes=[
            pltpu.VMEM((genome_bases.shape[0] // LANES, LANES), jnp.int32),
            pltpu.VMEM((chunks, channels, depth // chunks), BF16),
            pltpu.SemaphoreType.DMA,
            pltpu.SemaphoreType.DMA((chunks,)),
        ],
        compiler_params=pltpu.CompilerParams(vmem_limit_bytes=63 * 1024 * 1024),
        name="stem",
    )(genome_bases.reshape(-1, LANES), stem_weight)


def banded(kernel, rows):
    taps, out_channels, depth = kernel.shape
    flat = jnp.concatenate([kernel[u] for u in range(taps)], axis=1)
    bands = []
    for r in range(rows):
        parts = [flat]
        if r:
            parts.insert(0, jnp.zeros((out_channels, r * depth), BF16))
        if rows - 1 - r:
            parts.append(jnp.zeros((out_channels, (rows - 1 - r) * depth), BF16))
        bands.append(jnp.concatenate(parts, axis=1) if len(parts) > 1 else flat)
    return jnp.concatenate(bands, axis=0)


def block_diagonal(matrix, count):
    height, width = matrix.shape
    tiled = jnp.concatenate([jnp.concatenate([matrix] * count, axis=1)] * count, axis=0)
    row = lax.broadcasted_iota(jnp.int32, tiled.shape, 0) // height
    col = lax.broadcasted_iota(jnp.int32, tiled.shape, 1) // width
    return jnp.where(row == col, tiled, jnp.zeros((), BF16))


def head_by_row(head, count):
    targets, width = head.shape
    wide = jnp.concatenate([head] * count, axis=1)
    tall = jnp.broadcast_to(wide[:, None, :], (targets, count, count * width))
    row = lax.broadcasted_iota(jnp.int32, tall.shape, 1)
    col = lax.broadcasted_iota(jnp.int32, tall.shape, 2) // width
    return jnp.where(row == col, tall, jnp.zeros((), BF16)).reshape(targets * count, count * width)


def segments(margin):
    sizes = [BINS - STRIDE * b + margin + 1 for b in range(BLOCKS)]
    offsets = [sum(sizes[:b]) for b in range(BLOCKS)]
    lanes = -(-sum(sizes) // LANES) * LANES
    return sizes, offsets, lanes


def shifted(values, offset):
    if offset == 0:
        return values
    channels, extent = values.shape
    edge = jnp.zeros((channels, abs(offset)), values.dtype)
    if offset >= 0:
        return jnp.concatenate([values[:, offset:], edge], axis=1)
    return jnp.concatenate([edge, values[:, : extent + offset]], axis=1)


def main_kernel(
    height,
    groups,
    place_ref,
    *refs,
):
    (
        features,
        trunk_in,
        trunk_out,
        pair_weight,
        rate_ref,
        conv_ref,
        mix_ref,
        head_ref,
        stitch_ref,
        stitched_ref,
        keep_ref,
        send_ref,
        taps_a,
        taps_b,
        grid_ref,
        final_ref,
    ) = refs
    margin = 2
    sizes, offsets, lanes = segments(margin)
    tower_row = place_ref[0] * height
    channels = rate_ref.shape[1]
    depth = 3 * channels
    spans_a = {groups, (height + 2) % groups} - {0}
    spans_b = {groups, height % groups} - {0}
    conv_a = {span: banded(conv_ref[0], span) for span in sorted(spans_a)}
    conv_b = {span: banded(conv_ref[1], span) for span in sorted(spans_b)}
    mix_a = {span: block_diagonal(mix_ref[0], span) for span in sorted(spans_a)}
    mix_b = {span: block_diagonal(mix_ref[1], span) for span in sorted(spans_b)}
    head = head_by_row(head_ref[...], height)

    starts = features.shape[0]
    blocks = []
    for d in range(1 - BLOCKS, BLOCKS):
        at = place_ref[1] + d
        block = features[jnp.clip(at, 0, starts - 1)]
        blocks.append(jnp.where((at >= 0) & (at < starts), block, jnp.zeros_like(block)))
    blocks = jnp.concatenate(
        [
            jnp.concatenate([half[:, :STRIDE] for half in blocks], axis=1),
            jnp.concatenate([half[:, STRIDE:] for half in blocks], axis=1),
        ],
        axis=0,
    )
    extent = BINS
    windows = []
    for b in range(BLOCKS):
        first = (BLOCKS - 1 - b) * STRIDE
        windows.append(blocks[:, first : first + BINS].astype(F32))
    stream = jnp.concatenate(windows, axis=1)
    layers = trunk_in.shape[0]
    for layer in range(layers):
        dilation = max(1, extent // 2 ** (layers - layer))
        active = jnp.maximum(stream, 0.0).astype(BF16)
        width = active.shape[0]
        flat = trunk_in[layer]
        mid = flat.shape[0]
        tall = jnp.concatenate([flat[:, q * width : (q + 1) * width] for q in range(3)], axis=0)
        taps = dot(tall, active)
        inner = taps[mid : 2 * mid] + jnp.concatenate(
            [
                shifted(taps[:mid, b * BINS : (b + 1) * BINS], -dilation)
                + shifted(taps[2 * mid :, b * BINS : (b + 1) * BINS], dilation)
                for b in range(BLOCKS)
            ],
            axis=1,
        )
        squeezed = jax.nn.relu(inner).astype(BF16)
        stream = stream + lax.dot_general(
            trunk_out[layer], squeezed, (((0,), (0,)), ((), ())), preferred_element_type=F32
        )
    projected = dot(pair_weight[...], jax.nn.relu(stream).astype(BF16))

    lane = lax.broadcasted_iota(jnp.int32, (1, lanes), 1)
    block_of = jnp.zeros((1, lanes), jnp.int32)
    start_of = jnp.zeros((1, lanes), jnp.int32)
    for b in range(1, BLOCKS):
        block_of = jnp.where(lane >= offsets[b], b, block_of)
        start_of = jnp.where(lane >= offsets[b], offsets[b], start_of)
    step = lane - start_of
    first_row = STRIDE * block_of + tower_row - margin
    column = first_row + step
    in_column = (column < BINS) & (column >= 0)

    right = []
    left = []
    for b in range(BLOCKS):
        begin = STRIDE * b + tower_row - margin
        turn = jnp.where(begin > 0, BINS - begin, -begin)
        terms = projected[:, b * BINS : (b + 1) * BINS]
        turned = pltpu.roll(terms, turn, 1)
        left.append(turned[:channels, :LANES])
        own = turned[channels:]
        if sizes[b] > BINS:
            own = jnp.concatenate([own, own[:, : sizes[b] - BINS]], axis=1)
        right.append(own[:, : sizes[b]])
    used = sum(sizes)
    if lanes > used:
        right.append(jnp.zeros((channels, lanes - used), F32))
    right = jnp.concatenate(right, axis=1)
    row = lax.broadcasted_iota(jnp.int32, (channels, channels), 0)
    col = lax.broadcasted_iota(jnp.int32, (channels, channels), 1)
    rate = jnp.sum(jnp.where(row == col, rate_ref[...], 0.0), axis=1, keepdims=True)
    rate = jnp.broadcast_to(rate, (channels, LANES))
    rate = jnp.concatenate([rate] * (lanes // LANES), axis=1)

    def place_taps(ref, slot, act):
        act = act.astype(BF16)
        ref[pl.ds(slot * depth, channels), :] = pltpu.roll(act, 1, 1)
        ref[pl.ds(slot * depth + channels, channels), :] = act
        ref[pl.ds(slot * depth + 2 * channels, channels), :] = pltpu.roll(act, lanes - 1, 1)

    def inside(row):
        at = first_row + row
        return in_column & (at >= 0) & (at < BINS)

    for row in range(height + 2 * margin):
        apart = jnp.abs(step - row).astype(F32)
        decay = jnp.log1p(apart)
        tiles = []
        for tile in range(lanes // LANES):
            piece = None
            here = lane[:, tile * LANES : (tile + 1) * LANES]
            for b in range(BLOCKS):
                low, high = offsets[b], offsets[b] + sizes[b]
                if high <= tile * LANES or low >= (tile + 1) * LANES:
                    continue
                spread = jnp.broadcast_to(left[b][:, row : row + 1], (channels, LANES))
                piece = spread if piece is None else jnp.where(here >= low, spread, piece)
            tiles.append(piece)
        mixed = jnp.concatenate(tiles, axis=1) + right - rate * decay
        place_taps(taps_a, row, jnp.where(inside(row), jnp.maximum(mixed, 0.0), 0.0))

    for first in range(0, height + 2, groups):
        span = min(groups, height + 2 - first)
        conv = dot(conv_a[span], taps_a[pl.ds(first * depth, (span + 2) * depth), :])
        update = dot(mix_a[span], jnp.maximum(conv, 0.0).astype(BF16))
        for r in range(span):
            row = first + r
            kept = taps_a[pl.ds((row + 1) * depth + channels, channels), :].astype(F32)
            grid = kept + update[r * channels : (r + 1) * channels]
            if 1 <= row <= height:
                grid_ref[pl.ds((row - 1) * channels, channels), :] = grid
            place_taps(taps_b, row, jnp.where(inside(row + 1), jnp.maximum(grid, 0.0), 0.0))
    for first in range(0, height, groups):
        span = min(groups, height - first)
        conv = dot(conv_b[span], taps_b[pl.ds(first * depth, (span + 2) * depth), :])
        update = dot(mix_b[span], jnp.maximum(conv, 0.0).astype(BF16))
        rows = pl.ds(first * channels, span * channels)
        final_ref[rows, :] = jnp.maximum(grid_ref[rows, :] + update, 0.0).astype(BF16)
    targets = head.shape[0] // height
    contact = dot(head, final_ref[...]).reshape(targets, height, lanes)

    local = lax.broadcasted_iota(jnp.int32, (height, BINS), 0)
    ahead = lax.broadcasted_iota(jnp.int32, (height, BINS), 1)
    weight_sum = jnp.zeros((height, BINS), F32)
    weights = []
    for b in range(BLOCKS):
        weight = jnp.where(ahead == STRIDE * b + tower_row + local, stitch_ref[...], 0)
        weight = jnp.sum(weight.astype(F32), axis=1, keepdims=True)
        weight = jnp.where(place_ref[1] >= b, weight, 0.0)
        reach = STRIDE * b + tower_row + local + ahead < BINS
        weight = jnp.where(reach, weight, 0.0)
        weights.append(weight)
        weight_sum = weight_sum + weight
    scale = 1.0 / jnp.maximum(weight_sum, 1.0)
    weights = [w * scale for w in weights]
    stitched = []
    map_row = lax.broadcasted_iota(jnp.int32, (height, lanes), 0)
    for t in range(targets):
        band = None
        skewed = contact[t]
        for bit in range((height - 1).bit_length()):
            turned = pltpu.roll(skewed, lanes - (1 << bit), 1)
            skewed = jnp.where((map_row >> bit) & 1 == 1, turned, skewed)
        for b in range(BLOCKS):
            first, reach = offsets[b] + margin, BINS - STRIDE * b
            piece = skewed[:, first : first + reach]
            if reach < BINS:
                piece = jnp.concatenate([piece, jnp.zeros((height, BINS - reach), F32)], axis=1)
            piece = piece * weights[b]
            band = piece if band is None else band + piece
        stitched_ref[t] = band
        stitched.append(band[:, : 2 * STRIDE])

    near = jnp.concatenate(stitched, axis=0)
    wide = 2 * STRIDE
    col = lax.broadcasted_iota(jnp.int32, (wide, wide), 0)
    corner = lax.broadcasted_iota(jnp.int32, (wide, wide), 1)
    box = ((col > corner) & (col <= corner + STRIDE) & (corner < STRIDE)).astype(F32)
    square = jnp.dot(near, box, preferred_element_type=F32, precision=lax.Precision.HIGHEST)
    at = lax.broadcasted_iota(jnp.int32, near.shape, 1)
    contact = jnp.where((at >= 1) & (at <= STRIDE), jnp.exp(near), 0.0)
    down = jnp.sum(contact, axis=1, keepdims=True)
    here = lax.broadcasted_iota(jnp.int32, (height, wide), 0)
    there = lax.broadcasted_iota(jnp.int32, (height, wide), 1)

    def by_row(values):
        rows = []
        for t in range(targets):
            own = pltpu.roll(
                values[t * height : (t + 1) * height], 0, 1, stride=1, stride_axis=0
            )
            rows.append(jnp.sum(own, axis=0, keepdims=True))
        return rows

    down_rows = []
    for t in range(targets):
        own = jnp.where(here == there, down[t * height : (t + 1) * height], 0.0)
        down_rows.append(jnp.sum(own, axis=0, keepdims=True))
    rows = by_row(square) + by_row(contact)
    keep_ref[...] = jnp.concatenate(rows + down_rows, axis=0)
    per_row = LANES // height
    first = lax.broadcasted_iota(jnp.int32, (per_row, LANES), 1) < height
    packs = [
        jnp.concatenate(
            rows[p : p + per_row]
            + [jnp.zeros((1, LANES), F32)] * (per_row - len(rows[p : p + per_row])),
            axis=0,
        )
        for p in range(0, len(rows), per_row)
    ]
    for k in range(1, STRIDE // height + 1):
        packed = []
        for pack in packs:
            turned = jnp.where(first, pltpu.roll(pack, LANES - k * height, 1), 0.0)
            turned = pltpu.roll(turned, 0, 1, stride=height, stride_axis=0)
            packed.append(jnp.sum(turned, axis=0, keepdims=True))

        send_ref[lax.rem(place_ref[0] + k, STRIDE // height)] = jnp.concatenate(packed, axis=0)


def finish_kernel(height, place_ref, keep_ref, got_ref, out_ref):
    targets = out_ref.shape[0]
    per_row = LANES // height
    keep = keep_ref[...][:, :height]
    got = jnp.sum(got_ref[...], axis=0)
    rows = []
    for q in range(2 * targets):
        at = (q % per_row) * height
        rows.append(got[q // per_row : q // per_row + 1, at : at + height])
    sums = keep[: 2 * targets] + jnp.concatenate(rows, axis=0)
    own = place_ref[1] * (STRIDE // height) + place_ref[0]
    row = own * height + lax.broadcasted_iota(jnp.int32, (targets, height), 1)
    upstream = sums[targets:] + jnp.maximum(STRIDE - row, 0).astype(F32)
    downstream = keep[2 * targets :]
    insulation = sums[:targets] / (STRIDE * STRIDE)
    direction = (downstream - upstream) / (downstream + upstream)
    for t in range(targets):
        out_ref[t] = jnp.concatenate([insulation[t : t + 1], direction[t : t + 1]], axis=0)


def per_device(
    genome_bases,
    stitch_weight,
    stem_weight,
    trunk_in,
    trunk_out,
    pair_weight,
    distance_rate,
    tower_conv,
    tower_mix,
    head_weight,
):
    towers = lax.axis_size("tower")
    height = STRIDE // towers
    tower_index = lax.axis_index("tower")
    genome_index = lax.axis_index("genome")
    own = stem(genome_bases, stem_weight, lax.axis_size("genome"))
    features = lax.all_to_all(own, "genome", 0, 0, tiled=True)
    groups = 3
    channels = distance_rate.shape[0]
    targets = head_weight.shape[0]
    place = jnp.stack([tower_index, genome_index]).astype(jnp.int32)
    lanes = segments(2)[2]
    packs = -(-2 * targets * height // LANES)
    vmem = pl.BlockSpec(memory_space=pltpu.VMEM)
    smem = pl.BlockSpec(memory_space=pltpu.SMEM)
    stitched, keep, send = pl.pallas_call(
        functools.partial(main_kernel, height, groups),
        out_shape=[
            jax.ShapeDtypeStruct((targets, height, BINS), F32),
            jax.ShapeDtypeStruct((3 * targets, LANES), F32),
            jax.ShapeDtypeStruct((towers, packs, LANES), F32),
        ],
        in_specs=[smem] + [vmem] * 9,
        out_specs=[vmem] * 3,
        scratch_shapes=[
            pltpu.VMEM(((height + 4) * 3 * channels, lanes), BF16),
            pltpu.VMEM(((height + 2) * 3 * channels, lanes), BF16),
            pltpu.VMEM((height * channels, lanes), F32),
            pltpu.VMEM((height * channels, lanes), BF16),
        ],
        compiler_params=pltpu.CompilerParams(vmem_limit_bytes=VMEM_BYTES),
        name="windows",
    )(
        place,
        features,
        trunk_in,
        jnp.transpose(trunk_out, (0, 2, 1)),
        pair_weight,
        distance_rate.reshape(1, channels),
        tower_conv,
        tower_mix,
        head_weight,
        stitch_weight.reshape(1, BINS),
    )
    starts = lax.axis_size("genome")
    passed = lax.ppermute(send, "genome", [(i, i + 1) for i in range(starts - 1)])
    ahead = (jnp.arange(towers) > tower_index)[:, None, None]
    got = lax.all_to_all(jnp.where(ahead, send, passed), "tower", 0, 0, tiled=True)
    scores = pl.pallas_call(
        functools.partial(finish_kernel, height),
        out_shape=jax.ShapeDtypeStruct((targets, 2, height), F32),
        in_specs=[smem, vmem, vmem],
        out_specs=vmem,
        compiler_params=pltpu.CompilerParams(vmem_limit_bytes=2 * 1024 * 1024),
        name="finish",
    )(place, keep, got)
    return (stitched, jnp.transpose(scores, (1, 0, 2)))


def solution(mesh):
    placed = (P("genome"), P(), P(), P(), P(), P(), P(), P(), P(), P())
    return jax.shard_map(
        per_device,
        mesh=mesh,
        in_specs=placed,
        out_specs=(P(None, ("genome", "tower"), None), P(None, None, ("genome", "tower"))),
        check_vma=False,
    )
```

```python
import functools

import jax
import jax.numpy as jnp
from jax import lax
from jax.experimental import pallas as pl
from jax.experimental.pallas import tpu as pltpu
from jax.sharding import PartitionSpec as P

BP = 2048
STRIDE = 64
BINS = 256
BLOCKS = BINS // STRIDE
LANES = 128
F32 = jnp.float32
BF16 = jnp.bfloat16
VMEM_BYTES = 40 * 1024 * 1024


def dot(a, b):
    return jnp.dot(a, b, preferred_element_type=F32)


def stem_kernel(bins, bases_hbm, weight_hbm, out_ref, bases, weight, base_sem, weight_sem):
    groups = BP // LANES
    chunks = weight.shape[0]
    span = weight.shape[2]
    base_copy = pltpu.make_async_copy(bases_hbm, bases, base_sem)
    base_copy.start()
    copies = []
    for k in range(chunks):
        copy = pltpu.make_async_copy(
            weight_hbm.at[:, pl.ds(k * span, span)], weight.at[k], weight_sem.at[k]
        )
        copy.start()
        copies.append(copy)
    row = lax.broadcasted_iota(jnp.int32, (LANES, 4 * LANES), 0)
    col = lax.broadcasted_iota(jnp.int32, (LANES, 4 * LANES), 1)
    repeat = (row == col // 4).astype(F32).astype(BF16)
    letter = (lax.broadcasted_iota(jnp.int32, (bins, 4 * LANES), 1) % 4).astype(F32)
    base_copy.wait()
    total = None
    per_chunk = groups // chunks
    for k in range(chunks):
        hot = []
        for q in range(per_chunk):
            rows = bases[pl.ds(k * per_chunk + q, bins, stride=groups), :]
            spread = dot(rows.astype(F32).astype(BF16), repeat)
            hot.append(jnp.where(spread == letter, 1.0, 0.0).astype(BF16))
        hot = jnp.concatenate(hot, axis=1)
        copies[k].wait()
        part = lax.dot_general(
            weight[k], hot, (((1,), (1,)), ((), ())), preferred_element_type=F32
        )
        total = part if total is None else total + part
    total = total.astype(BF16)
    half = out_ref.shape[1]
    packed = jnp.concatenate([total[:half], total[half:]], axis=1)
    for slot in range(out_ref.shape[0]):
        out_ref[slot] = packed


def stem(genome_bases, stem_weight, slots):
    bins = genome_bases.shape[0] // BP
    channels, depth = stem_weight.shape
    chunks = 4
    return pl.pallas_call(
        functools.partial(stem_kernel, bins),
        out_shape=jax.ShapeDtypeStruct((slots, channels // 2, 2 * bins), BF16),
        in_specs=[pl.BlockSpec(memory_space=pltpu.HBM)] * 2,
        out_specs=pl.BlockSpec(memory_space=pltpu.VMEM),
        scratch_shapes=[
            pltpu.VMEM((genome_bases.shape[0] // LANES, LANES), jnp.int32),
            pltpu.VMEM((chunks, channels, depth // chunks), BF16),
            pltpu.SemaphoreType.DMA,
            pltpu.SemaphoreType.DMA((chunks,)),
        ],
        compiler_params=pltpu.CompilerParams(vmem_limit_bytes=63 * 1024 * 1024),
        name="stem",
    )(genome_bases.reshape(-1, LANES), stem_weight)


def banded(kernel, rows):
    taps, out_channels, depth = kernel.shape
    flat = jnp.concatenate([kernel[u] for u in range(taps)], axis=1)
    bands = []
    for r in range(rows):
        parts = [flat]
        if r:
            parts.insert(0, jnp.zeros((out_channels, r * depth), BF16))
        if rows - 1 - r:
            parts.append(jnp.zeros((out_channels, (rows - 1 - r) * depth), BF16))
        bands.append(jnp.concatenate(parts, axis=1) if len(parts) > 1 else flat)
    return jnp.concatenate(bands, axis=0)


def block_diagonal(matrix, count):
    height, width = matrix.shape
    tiled = jnp.concatenate([jnp.concatenate([matrix] * count, axis=1)] * count, axis=0)
    row = lax.broadcasted_iota(jnp.int32, tiled.shape, 0) // height
    col = lax.broadcasted_iota(jnp.int32, tiled.shape, 1) // width
    return jnp.where(row == col, tiled, jnp.zeros((), BF16))


def head_by_row(head, count):
    targets, width = head.shape
    wide = jnp.concatenate([head] * count, axis=1)
    tall = jnp.broadcast_to(wide[:, None, :], (targets, count, count * width))
    row = lax.broadcasted_iota(jnp.int32, tall.shape, 1)
    col = lax.broadcasted_iota(jnp.int32, tall.shape, 2) // width
    return jnp.where(row == col, tall, jnp.zeros((), BF16)).reshape(targets * count, count * width)


MARGIN = 2
NEAR = 2 * STRIDE


def segments(begin, height):
    sizes = []
    for b in range(BLOCKS):
        size = BINS - STRIDE * b + MARGIN + 1 - begin
        if size > MARGIN + 1:
            sizes.append(min(size, NEAR + height - 1 + 2 * MARGIN))
    offsets = [sum(sizes[:b]) for b in range(len(sizes))]
    lanes = -(-sum(sizes) // LANES) * LANES
    return sizes, offsets, lanes


def shifted(values, offset):
    if offset == 0:
        return values
    channels, extent = values.shape
    edge = jnp.zeros((channels, abs(offset)), values.dtype)
    if offset >= 0:
        return jnp.concatenate([values[:, offset:], edge], axis=1)
    return jnp.concatenate([edge, values[:, : extent + offset]], axis=1)


def tower_band(height, groups, begin, place_ref, left, right, weight_refs, scratch):
    rate_ref, conv_ref, mix_ref, head_ref, stitch_ref = weight_refs
    taps_a, taps_b, grid_ref, final_ref = scratch
    sizes, offsets, lanes = segments(begin, height)
    tower_row = place_ref[0] * height
    channels = rate_ref.shape[1]
    depth = 3 * channels
    spans_a = {groups, (height + 2) % groups} - {0}
    spans_b = {groups, height % groups} - {0}
    conv_a = {span: banded(conv_ref[0], span) for span in sorted(spans_a)}
    conv_b = {span: banded(conv_ref[1], span) for span in sorted(spans_b)}
    mix_a = {span: block_diagonal(mix_ref[0], span) for span in sorted(spans_a)}
    mix_b = {span: block_diagonal(mix_ref[1], span) for span in sorted(spans_b)}
    head = head_by_row(head_ref[...], height)

    lane = lax.broadcasted_iota(jnp.int32, (1, lanes), 1)
    block_of = jnp.zeros((1, lanes), jnp.int32)
    start_of = jnp.zeros((1, lanes), jnp.int32)
    for b in range(1, len(sizes)):
        block_of = jnp.where(lane >= offsets[b], b, block_of)
        start_of = jnp.where(lane >= offsets[b], offsets[b], start_of)
    step = lane - start_of
    first_row = STRIDE * block_of + tower_row - MARGIN
    column = first_row + begin + step
    in_column = (column < BINS) & (column >= 0)

    row = lax.broadcasted_iota(jnp.int32, (channels, channels), 0)
    col = lax.broadcasted_iota(jnp.int32, (channels, channels), 1)
    rate = jnp.sum(jnp.where(row == col, rate_ref[...], 0.0), axis=1, keepdims=True)
    rate = jnp.broadcast_to(rate, (channels, LANES))
    rate = jnp.concatenate([rate] * (lanes // LANES), axis=1)

    def place_taps(ref, slot, act):
        act = act.astype(BF16)
        ref[pl.ds(slot * depth, channels), :] = pltpu.roll(act, 1, 1)
        ref[pl.ds(slot * depth + channels, channels), :] = act
        ref[pl.ds(slot * depth + 2 * channels, channels), :] = pltpu.roll(act, lanes - 1, 1)

    def inside(row):
        at = first_row + row
        return in_column & (at >= 0) & (at < BINS)

    for row in range(height + 2 * MARGIN):
        apart = jnp.abs(begin + step - row).astype(F32)
        decay = jnp.log1p(apart)
        tiles = []
        for tile in range(lanes // LANES):
            piece = None
            here = lane[:, tile * LANES : (tile + 1) * LANES]
            for b in range(len(sizes)):
                low, high = offsets[b], offsets[b] + sizes[b]
                if high <= tile * LANES or low >= (tile + 1) * LANES:
                    continue
                spread = jnp.broadcast_to(left[b][:, row : row + 1], (channels, LANES))
                piece = spread if piece is None else jnp.where(here >= low, spread, piece)
            tiles.append(piece)
        mixed = jnp.concatenate(tiles, axis=1) + right - rate * decay
        place_taps(taps_a, row, jnp.where(inside(row), jnp.maximum(mixed, 0.0), 0.0))

    for first in range(0, height + 2, groups):
        span = min(groups, height + 2 - first)
        conv = dot(conv_a[span], taps_a[pl.ds(first * depth, (span + 2) * depth), :])
        update = dot(mix_a[span], jnp.maximum(conv, 0.0).astype(BF16))
        for r in range(span):
            row = first + r
            kept = taps_a[pl.ds((row + 1) * depth + channels, channels), :].astype(F32)
            grid = kept + update[r * channels : (r + 1) * channels]
            if 1 <= row <= height:
                grid_ref[pl.ds((row - 1) * channels, channels), :] = grid
            place_taps(taps_b, row, jnp.where(inside(row + 1), jnp.maximum(grid, 0.0), 0.0))
    for first in range(0, height, groups):
        span = min(groups, height - first)
        conv = dot(conv_b[span], taps_b[pl.ds(first * depth, (span + 2) * depth), :])
        update = dot(mix_b[span], jnp.maximum(conv, 0.0).astype(BF16))
        rows = pl.ds(first * channels, span * channels)
        final_ref[rows, :] = jnp.maximum(grid_ref[rows, :] + update, 0.0).astype(BF16)
    targets = head.shape[0] // height
    contact = dot(head, final_ref[...]).reshape(targets, height, lanes)

    at = lax.broadcasted_iota(jnp.int32, (height, BINS), 0)
    bin_of = lax.broadcasted_iota(jnp.int32, (height, BINS), 1)
    local = lax.broadcasted_iota(jnp.int32, (height, NEAR), 0)
    ahead = lax.broadcasted_iota(jnp.int32, (height, NEAR), 1) + begin
    weight_sum = jnp.zeros((height, NEAR), F32)
    weights = []
    for b in range(len(sizes)):
        weight = jnp.where(bin_of == STRIDE * b + tower_row + at, stitch_ref[...], 0)
        weight = jnp.sum(weight.astype(F32), axis=1, keepdims=True)
        weight = jnp.where(place_ref[1] >= b, weight, 0.0)
        reach = STRIDE * b + tower_row + local + ahead < BINS
        weight = jnp.where(reach, weight, 0.0)
        weights.append(weight)
        weight_sum = weight_sum + weight
    scale = 1.0 / jnp.maximum(weight_sum, 1.0)
    weights = [w * scale for w in weights]
    bands = []
    map_row = lax.broadcasted_iota(jnp.int32, (height, lanes), 0)
    for t in range(targets):
        band = None
        skewed = contact[t]
        for bit in range((height - 1).bit_length()):
            turned = pltpu.roll(skewed, lanes - (1 << bit), 1)
            skewed = jnp.where((map_row >> bit) & 1 == 1, turned, skewed)
        for b in range(len(sizes)):
            first, reach = offsets[b] + MARGIN, min(NEAR, BINS - STRIDE * b - begin)
            piece = skewed[:, first : first + reach]
            if reach < NEAR:
                piece = jnp.concatenate([piece, jnp.zeros((height, NEAR - reach), F32)], axis=1)
            piece = piece * weights[b]
            band = piece if band is None else band + piece
        bands.append(band)
    return bands


def near_kernel(
    height,
    groups,
    place_ref,
    features,
    trunk_in,
    trunk_out,
    pair_weight,
    rate_ref,
    conv_ref,
    mix_ref,
    head_ref,
    stitch_ref,
    near_ref,
    keep_ref,
    send_ref,
    left_ref,
    right_ref,
    *scratch,
):
    tower_row = place_ref[0] * height
    channels = rate_ref.shape[1]
    targets = head_ref.shape[0]

    starts = features.shape[0]
    blocks = []
    for d in range(1 - BLOCKS, BLOCKS):
        at = place_ref[1] + d
        block = features[jnp.clip(at, 0, starts - 1)]
        blocks.append(jnp.where((at >= 0) & (at < starts), block, jnp.zeros_like(block)))
    blocks = jnp.concatenate(
        [
            jnp.concatenate([half[:, :STRIDE] for half in blocks], axis=1),
            jnp.concatenate([half[:, STRIDE:] for half in blocks], axis=1),
        ],
        axis=0,
    )
    extent = BINS
    windows = []
    for b in range(BLOCKS):
        first = (BLOCKS - 1 - b) * STRIDE
        windows.append(blocks[:, first : first + BINS].astype(F32))
    stream = jnp.concatenate(windows, axis=1)
    layers = trunk_in.shape[0]
    for layer in range(layers):
        dilation = max(1, extent // 2 ** (layers - layer))
        active = jnp.maximum(stream, 0.0).astype(BF16)
        width = active.shape[0]
        flat = trunk_in[layer]
        mid = flat.shape[0]
        tall = jnp.concatenate([flat[:, q * width : (q + 1) * width] for q in range(3)], axis=0)
        taps = dot(tall, active)
        inner = taps[mid : 2 * mid] + jnp.concatenate(
            [
                shifted(taps[:mid, b * BINS : (b + 1) * BINS], -dilation)
                + shifted(taps[2 * mid :, b * BINS : (b + 1) * BINS], dilation)
                for b in range(BLOCKS)
            ],
            axis=1,
        )
        squeezed = jax.nn.relu(inner).astype(BF16)
        stream = stream + lax.dot_general(
            trunk_out[layer], squeezed, (((0,), (0,)), ((), ())), preferred_element_type=F32
        )
    projected = dot(pair_weight[...], jax.nn.relu(stream).astype(BF16))

    left = []
    parts = {0: [], NEAR: []}
    for b in range(BLOCKS):
        start = STRIDE * b + tower_row - MARGIN
        turn = jnp.where(start > 0, BINS - start, -start)
        turned = pltpu.roll(projected[:, b * BINS : (b + 1) * BINS], turn, 1)
        left.append(turned[:channels, :LANES])
        own = jnp.concatenate([turned[channels:], turned[channels:, :LANES]], axis=1)
        for begin, terms in parts.items():
            sizes = segments(begin, height)[0]
            if b < len(sizes):
                terms.append(own[:, begin : begin + sizes[b]])
    for begin, terms in parts.items():
        sizes, _, lanes = segments(begin, height)
        if lanes > sum(sizes):
            terms.append(jnp.zeros((channels, lanes - sum(sizes)), F32))
        parts[begin] = jnp.concatenate(terms, axis=1)
    right_ref[...] = parts[NEAR]
    for b in range(left_ref.shape[0]):
        left_ref[b] = left[b]
    weight_refs = (rate_ref, conv_ref, mix_ref, head_ref, stitch_ref)
    stitched = tower_band(
        height, groups, 0, place_ref, left, parts[0], weight_refs, scratch
    )
    for t in range(targets):
        near_ref[t] = stitched[t]

    near = jnp.concatenate(stitched, axis=0)
    wide = 2 * STRIDE
    col = lax.broadcasted_iota(jnp.int32, (wide, wide), 0)
    corner = lax.broadcasted_iota(jnp.int32, (wide, wide), 1)
    box = ((col > corner) & (col <= corner + STRIDE) & (corner < STRIDE)).astype(F32)
    square = jnp.dot(near, box, preferred_element_type=F32, precision=lax.Precision.HIGHEST)
    at = lax.broadcasted_iota(jnp.int32, near.shape, 1)
    contact = jnp.where((at >= 1) & (at <= STRIDE), jnp.exp(near), 0.0)
    down = jnp.sum(contact, axis=1, keepdims=True)
    here = lax.broadcasted_iota(jnp.int32, (height, wide), 0)
    there = lax.broadcasted_iota(jnp.int32, (height, wide), 1)

    def by_row(values):
        rows = []
        for t in range(targets):
            own = pltpu.roll(
                values[t * height : (t + 1) * height], 0, 1, stride=1, stride_axis=0
            )
            rows.append(jnp.sum(own, axis=0, keepdims=True))
        return rows

    down_rows = []
    for t in range(targets):
        own = jnp.where(here == there, down[t * height : (t + 1) * height], 0.0)
        down_rows.append(jnp.sum(own, axis=0, keepdims=True))
    rows = by_row(square) + by_row(contact)
    keep_ref[...] = jnp.concatenate(rows + down_rows, axis=0)
    per_row = LANES // height
    first = lax.broadcasted_iota(jnp.int32, (per_row, LANES), 1) < height
    packs = [
        jnp.concatenate(
            rows[p : p + per_row]
            + [jnp.zeros((1, LANES), F32)] * (per_row - len(rows[p : p + per_row])),
            axis=0,
        )
        for p in range(0, len(rows), per_row)
    ]
    for k in range(1, STRIDE // height + 1):
        packed = []
        for pack in packs:
            turned = jnp.where(first, pltpu.roll(pack, LANES - k * height, 1), 0.0)
            turned = pltpu.roll(turned, 0, 1, stride=height, stride_axis=0)
            packed.append(jnp.sum(turned, axis=0, keepdims=True))

        send_ref[lax.rem(place_ref[0] + k, STRIDE // height)] = jnp.concatenate(packed, axis=0)


def far_kernel(
    height,
    groups,
    place_ref,
    near_ref,
    left_ref,
    right_ref,
    rate_ref,
    conv_ref,
    mix_ref,
    head_ref,
    stitch_ref,
    stitched_ref,
    *scratch,
):
    left = [left_ref[b] for b in range(left_ref.shape[0])]
    weight_refs = (rate_ref, conv_ref, mix_ref, head_ref, stitch_ref)
    bands = tower_band(
        height, groups, NEAR, place_ref, left, right_ref[...], weight_refs, scratch
    )
    for t in range(stitched_ref.shape[0]):
        stitched_ref[t] = jnp.concatenate([near_ref[t], bands[t]], axis=1)


def finish_kernel(height, place_ref, keep_ref, got_ref, out_ref):
    targets = out_ref.shape[0]
    per_row = LANES // height
    keep = keep_ref[...][:, :height]
    got = jnp.sum(got_ref[...], axis=0)
    rows = []
    for q in range(2 * targets):
        at = (q % per_row) * height
        rows.append(got[q // per_row : q // per_row + 1, at : at + height])
    sums = keep[: 2 * targets] + jnp.concatenate(rows, axis=0)
    own = place_ref[1] * (STRIDE // height) + place_ref[0]
    row = own * height + lax.broadcasted_iota(jnp.int32, (targets, height), 1)
    upstream = sums[targets:] + jnp.maximum(STRIDE - row, 0).astype(F32)
    downstream = keep[2 * targets :]
    insulation = sums[:targets] / (STRIDE * STRIDE)
    direction = (downstream - upstream) / (downstream + upstream)
    for t in range(targets):
        out_ref[t] = jnp.concatenate([insulation[t : t + 1], direction[t : t + 1]], axis=0)


def per_device(
    genome_bases,
    stitch_weight,
    stem_weight,
    trunk_in,
    trunk_out,
    pair_weight,
    distance_rate,
    tower_conv,
    tower_mix,
    head_weight,
):
    towers = lax.axis_size("tower")
    height = STRIDE // towers
    tower_index = lax.axis_index("tower")
    genome_index = lax.axis_index("genome")
    own = stem(genome_bases, stem_weight, lax.axis_size("genome"))
    features = lax.all_to_all(own, "genome", 0, 0, tiled=True)
    groups = 3
    channels = distance_rate.shape[0]
    targets = head_weight.shape[0]
    place = jnp.stack([tower_index, genome_index]).astype(jnp.int32)
    packs = -(-2 * targets * height // LANES)
    vmem = pl.BlockSpec(memory_space=pltpu.VMEM)
    smem = pl.BlockSpec(memory_space=pltpu.SMEM)

    def scratch(begin):
        lanes = segments(begin, height)[2]
        return [
            pltpu.VMEM(((height + 4) * 3 * channels, lanes), BF16),
            pltpu.VMEM(((height + 2) * 3 * channels, lanes), BF16),
            pltpu.VMEM((height * channels, lanes), F32),
            pltpu.VMEM((height * channels, lanes), BF16),
        ]

    weights = (
        distance_rate.reshape(1, channels),
        tower_conv,
        tower_mix,
        head_weight,
        stitch_weight.reshape(1, BINS),
    )
    far_sizes, _, far_lanes = segments(NEAR, height)
    near, keep, send, left, right = pl.pallas_call(
        functools.partial(near_kernel, height, groups),
        out_shape=[
            jax.ShapeDtypeStruct((targets, height, NEAR), F32),
            jax.ShapeDtypeStruct((3 * targets, LANES), F32),
            jax.ShapeDtypeStruct((towers, packs, LANES), F32),
            jax.ShapeDtypeStruct((len(far_sizes), channels, LANES), F32),
            jax.ShapeDtypeStruct((channels, far_lanes), F32),
        ],
        in_specs=[smem] + [vmem] * 9,
        out_specs=[vmem] * 5,
        scratch_shapes=scratch(0),
        compiler_params=pltpu.CompilerParams(vmem_limit_bytes=VMEM_BYTES),
        name="near",
    )(
        place,
        features,
        trunk_in,
        jnp.transpose(trunk_out, (0, 2, 1)),
        pair_weight,
        *weights,
    )
    stitched = pl.pallas_call(
        functools.partial(far_kernel, height, groups),
        out_shape=jax.ShapeDtypeStruct((targets, height, BINS), F32),
        in_specs=[smem] + [vmem] * 8,
        out_specs=vmem,
        scratch_shapes=scratch(NEAR),
        compiler_params=pltpu.CompilerParams(vmem_limit_bytes=VMEM_BYTES),
        cost_estimate=pl.CostEstimate(
            flops=2 * (2 * height + 2) * far_lanes * channels * channels * 40,
            bytes_accessed=1 << 20,
            transcendentals=0,
        ),
        name="far",
    )(place, near, left, right, *weights)
    starts = lax.axis_size("genome")
    passed = lax.ppermute(send, "genome", [(i, i + 1) for i in range(starts - 1)])
    ahead = (jnp.arange(towers) > tower_index)[:, None, None]
    got = lax.all_to_all(jnp.where(ahead, send, passed), "tower", 0, 0, tiled=True)
    scores = pl.pallas_call(
        functools.partial(finish_kernel, height),
        out_shape=jax.ShapeDtypeStruct((targets, 2, height), F32),
        in_specs=[smem, vmem, vmem],
        out_specs=vmem,
        compiler_params=pltpu.CompilerParams(vmem_limit_bytes=2 * 1024 * 1024),
        name="finish",
    )(place, keep, got)
    return (stitched, jnp.transpose(scores, (1, 0, 2)))


def solution(mesh):
    placed = (P("genome"), P(), P(), P(), P(), P(), P(), P(), P(), P())
    return jax.shard_map(
        per_device,
        mesh=mesh,
        in_specs=placed,
        out_specs=(P(None, ("genome", "tower"), None), P(None, None, ("genome", "tower"))),
        check_vma=False,
    )
```

```python
import functools

import jax
import jax.numpy as jnp
from jax import lax
from jax.experimental import pallas as pl
from jax.experimental.pallas import tpu as pltpu
from jax.sharding import PartitionSpec as P

BP = 2048
STRIDE = 64
BINS = 256
BLOCKS = BINS // STRIDE
LANES = 128
F32 = jnp.float32
BF16 = jnp.bfloat16
VMEM_BYTES = 40 * 1024 * 1024


def dot(a, b):
    return jnp.dot(a, b, preferred_element_type=F32)


def stem_kernel(bins, bases_hbm, weight_hbm, out_ref, bases, weight, base_sem, weight_sem):
    groups = BP // LANES
    chunks = weight.shape[0]
    span = weight.shape[2]
    base_copy = pltpu.make_async_copy(bases_hbm, bases, base_sem)
    base_copy.start()
    copies = []
    for k in range(chunks):
        copy = pltpu.make_async_copy(
            weight_hbm.at[:, pl.ds(k * span, span)], weight.at[k], weight_sem.at[k]
        )
        copy.start()
        copies.append(copy)
    row = lax.broadcasted_iota(jnp.int32, (LANES, 4 * LANES), 0)
    col = lax.broadcasted_iota(jnp.int32, (LANES, 4 * LANES), 1)
    repeat = (row == col // 4).astype(F32).astype(BF16)
    letter = (lax.broadcasted_iota(jnp.int32, (bins, 4 * LANES), 1) % 4).astype(F32)
    base_copy.wait()
    total = None
    per_chunk = groups // chunks
    for k in range(chunks):
        hot = []
        for q in range(per_chunk):
            rows = bases[pl.ds(k * per_chunk + q, bins, stride=groups), :]
            spread = dot(rows.astype(F32).astype(BF16), repeat)
            hot.append(jnp.where(spread == letter, 1.0, 0.0).astype(BF16))
        hot = jnp.concatenate(hot, axis=1)
        copies[k].wait()
        part = lax.dot_general(
            weight[k], hot, (((1,), (1,)), ((), ())), preferred_element_type=F32
        )
        total = part if total is None else total + part
    total = total.astype(BF16)
    half = out_ref.shape[1]
    packed = jnp.concatenate([total[:half], total[half:]], axis=1)
    for slot in range(out_ref.shape[0]):
        out_ref[slot] = packed


def stem(genome_bases, stem_weight, slots):
    bins = genome_bases.shape[0] // BP
    channels, depth = stem_weight.shape
    chunks = 4
    return pl.pallas_call(
        functools.partial(stem_kernel, bins),
        out_shape=jax.ShapeDtypeStruct((slots, channels // 2, 2 * bins), BF16),
        in_specs=[pl.BlockSpec(memory_space=pltpu.HBM)] * 2,
        out_specs=pl.BlockSpec(memory_space=pltpu.VMEM),
        scratch_shapes=[
            pltpu.VMEM((genome_bases.shape[0] // LANES, LANES), jnp.int32),
            pltpu.VMEM((chunks, channels, depth // chunks), BF16),
            pltpu.SemaphoreType.DMA,
            pltpu.SemaphoreType.DMA((chunks,)),
        ],
        compiler_params=pltpu.CompilerParams(vmem_limit_bytes=63 * 1024 * 1024),
        name="stem",
    )(genome_bases.reshape(-1, LANES), stem_weight)


def banded(kernel, rows):
    taps, out_channels, depth = kernel.shape
    flat = jnp.concatenate([kernel[u] for u in range(taps)], axis=1)
    bands = []
    for r in range(rows):
        parts = [flat]
        if r:
            parts.insert(0, jnp.zeros((out_channels, r * depth), BF16))
        if rows - 1 - r:
            parts.append(jnp.zeros((out_channels, (rows - 1 - r) * depth), BF16))
        bands.append(jnp.concatenate(parts, axis=1) if len(parts) > 1 else flat)
    return jnp.concatenate(bands, axis=0)


def block_diagonal(matrix, count):
    height, width = matrix.shape
    tiled = jnp.concatenate([jnp.concatenate([matrix] * count, axis=1)] * count, axis=0)
    row = lax.broadcasted_iota(jnp.int32, tiled.shape, 0) // height
    col = lax.broadcasted_iota(jnp.int32, tiled.shape, 1) // width
    return jnp.where(row == col, tiled, jnp.zeros((), BF16))


def head_by_row(head, count):
    targets, width = head.shape
    wide = jnp.concatenate([head] * count, axis=1)
    tall = jnp.broadcast_to(wide[:, None, :], (targets, count, count * width))
    row = lax.broadcasted_iota(jnp.int32, tall.shape, 1)
    col = lax.broadcasted_iota(jnp.int32, tall.shape, 2) // width
    return jnp.where(row == col, tall, jnp.zeros((), BF16)).reshape(targets * count, count * width)


def segments(margin):
    sizes = [BINS - STRIDE * b + margin + 1 for b in range(BLOCKS)]
    offsets = [sum(sizes[:b]) for b in range(BLOCKS)]
    lanes = -(-sum(sizes) // LANES) * LANES
    return sizes, offsets, lanes


def shifted(values, offset):
    if offset == 0:
        return values
    channels, extent = values.shape
    edge = jnp.zeros((channels, abs(offset)), values.dtype)
    if offset >= 0:
        return jnp.concatenate([values[:, offset:], edge], axis=1)
    return jnp.concatenate([edge, values[:, : extent + offset]], axis=1)


def spans_of(rows, groups):
    return sorted({groups, rows % groups} - {0})


def prepare_kernel(
    height,
    groups,
    place_ref,
    _,
    trunk_in,
    rate_in,
    conv_in,
    mix_in,
    head_in,
    stitch_in,
    trunk_ref,
    rate_ref,
    decay_ref,
    inside_ref,
    head_ref,
    stitch_ref,
    *conv_refs,
):
    margin = 2
    sizes, offsets, lanes = segments(margin)
    tower_row = place_ref[0] * height
    for layer in range(trunk_in.shape[0]):
        flat = trunk_in[layer]
        width = flat.shape[1] // 3
        trunk_ref[layer] = jnp.concatenate(
            [flat[:, q * width : (q + 1) * width] for q in range(3)], axis=0
        )
    at = 0
    for block, rows in enumerate((height + 2, height)):
        for span in spans_of(rows, groups):
            conv_refs[at][...] = banded(conv_in[block], span)
            conv_refs[at + 1][...] = block_diagonal(mix_in[block], span)
            at += 2
    head_ref[...] = head_by_row(head_in[...], height)
    channels = rate_in.shape[1]
    row = lax.broadcasted_iota(jnp.int32, (channels, channels), 0)
    col = lax.broadcasted_iota(jnp.int32, (channels, channels), 1)
    rate = jnp.sum(jnp.where(row == col, rate_in[...], 0.0), axis=1, keepdims=True)
    rate_ref[...] = jnp.broadcast_to(rate, rate_ref.shape)

    lane = lax.broadcasted_iota(jnp.int32, (height + 2 * margin, lanes), 1)
    block_of = jnp.zeros((height + 2 * margin, lanes), jnp.int32)
    start_of = jnp.zeros((height + 2 * margin, lanes), jnp.int32)
    for b in range(1, BLOCKS):
        block_of = jnp.where(lane >= offsets[b], b, block_of)
        start_of = jnp.where(lane >= offsets[b], offsets[b], start_of)
    step = lane - start_of
    first_row = STRIDE * block_of + tower_row - margin
    column = first_row + step
    in_column = (column < BINS) & (column >= 0)

    row = lax.broadcasted_iota(jnp.int32, (height + 2 * margin, lanes), 0)
    decay_ref[...] = jnp.log1p(jnp.abs(step - row).astype(F32))
    at = first_row + row
    inside_ref[...] = jnp.where(in_column & (at >= 0) & (at < BINS), 1.0, 0.0)

    local = lax.broadcasted_iota(jnp.int32, (height, BINS), 0)
    ahead = lax.broadcasted_iota(jnp.int32, (height, BINS), 1)
    weight_sum = jnp.zeros((height, BINS), F32)
    weights = []
    for b in range(BLOCKS):
        weight = jnp.where(ahead == STRIDE * b + tower_row + local, stitch_in[...], 0)
        weight = jnp.sum(weight.astype(F32), axis=1, keepdims=True)
        weight = jnp.where(place_ref[1] >= b, weight, 0.0)
        reach = STRIDE * b + tower_row + local + ahead < BINS
        weight = jnp.where(reach, weight, 0.0)
        weights.append(weight)
        weight_sum = weight_sum + weight
    scale = 1.0 / jnp.maximum(weight_sum, 1.0)
    for b in range(BLOCKS):
        stitch_ref[b] = weights[b] * scale


def main_kernel(
    height,
    groups,
    place_ref,
    features,
    trunk_out,
    pair_weight,
    trunk_in,
    rate_ref,
    decay_ref,
    inside_ref,
    head_ref,
    stitch_ref,
    *rest,
):
    margin = 2
    sizes, offsets, lanes = segments(margin)
    tower_row = place_ref[0] * height
    channels = rate_ref.shape[0]
    depth = 3 * channels
    rest = list(rest)
    conv_a, conv_b, mix_a, mix_b = {}, {}, {}, {}
    for span in spans_of(height + 2, groups):
        conv_a[span], mix_a[span] = rest.pop(0), rest.pop(0)
    for span in spans_of(height, groups):
        conv_b[span], mix_b[span] = rest.pop(0), rest.pop(0)
    stitched_ref, keep_ref, send_ref, taps_a, taps_b, grid_ref, final_ref = rest

    starts = features.shape[0]
    blocks = []
    for d in range(1 - BLOCKS, BLOCKS):
        at = place_ref[1] + d
        block = features[jnp.clip(at, 0, starts - 1)]
        blocks.append(jnp.where((at >= 0) & (at < starts), block, jnp.zeros_like(block)))
    blocks = jnp.concatenate(
        [
            jnp.concatenate([half[:, :STRIDE] for half in blocks], axis=1),
            jnp.concatenate([half[:, STRIDE:] for half in blocks], axis=1),
        ],
        axis=0,
    )
    extent = BINS
    windows = []
    for b in range(BLOCKS):
        first = (BLOCKS - 1 - b) * STRIDE
        windows.append(blocks[:, first : first + BINS].astype(F32))
    stream = jnp.concatenate(windows, axis=1)
    layers = trunk_in.shape[0]
    for layer in range(layers):
        dilation = max(1, extent // 2 ** (layers - layer))
        active = jnp.maximum(stream, 0.0).astype(BF16)
        mid = trunk_in.shape[1] // 3
        taps = dot(trunk_in[layer], active)
        inner = taps[mid : 2 * mid] + jnp.concatenate(
            [
                shifted(taps[:mid, b * BINS : (b + 1) * BINS], -dilation)
                + shifted(taps[2 * mid :, b * BINS : (b + 1) * BINS], dilation)
                for b in range(BLOCKS)
            ],
            axis=1,
        )
        squeezed = jax.nn.relu(inner).astype(BF16)
        stream = stream + lax.dot_general(
            trunk_out[layer], squeezed, (((0,), (0,)), ((), ())), preferred_element_type=F32
        )
    projected = dot(pair_weight[...], jax.nn.relu(stream).astype(BF16))

    right = []
    left = []
    for b in range(BLOCKS):
        begin = STRIDE * b + tower_row - margin
        turn = jnp.where(begin > 0, BINS - begin, -begin)
        terms = projected[:, b * BINS : (b + 1) * BINS]
        turned = pltpu.roll(terms, turn, 1)
        left.append(turned[:channels, :LANES])
        own = turned[channels:]
        if sizes[b] > BINS:
            own = jnp.concatenate([own, own[:, : sizes[b] - BINS]], axis=1)
        right.append(own[:, : sizes[b]])
    used = sum(sizes)
    if lanes > used:
        right.append(jnp.zeros((channels, lanes - used), F32))
    right = jnp.concatenate(right, axis=1)
    rate = jnp.concatenate([rate_ref[...]] * (lanes // LANES), axis=1)
    lane = lax.broadcasted_iota(jnp.int32, (1, lanes), 1)

    def place_taps(ref, slot, act):
        act = act.astype(BF16)
        ref[pl.ds(slot * depth, channels), :] = pltpu.roll(act, 1, 1)
        ref[pl.ds(slot * depth + channels, channels), :] = act
        ref[pl.ds(slot * depth + 2 * channels, channels), :] = pltpu.roll(act, lanes - 1, 1)

    for row in range(height + 2 * margin):
        tiles = []
        for tile in range(lanes // LANES):
            piece = None
            here = lane[:, tile * LANES : (tile + 1) * LANES]
            for b in range(BLOCKS):
                low, high = offsets[b], offsets[b] + sizes[b]
                if high <= tile * LANES or low >= (tile + 1) * LANES:
                    continue
                spread = jnp.broadcast_to(left[b][:, row : row + 1], (channels, LANES))
                piece = spread if piece is None else jnp.where(here >= low, spread, piece)
            tiles.append(piece)
        mixed = jnp.concatenate(tiles, axis=1) + right - rate * decay_ref[pl.ds(row, 1), :]
        place_taps(taps_a, row, jnp.maximum(mixed, 0.0) * inside_ref[pl.ds(row, 1), :])

    for first in range(0, height + 2, groups):
        span = min(groups, height + 2 - first)
        conv = dot(conv_a[span][...], taps_a[pl.ds(first * depth, (span + 2) * depth), :])
        update = dot(mix_a[span][...], jnp.maximum(conv, 0.0).astype(BF16))
        for r in range(span):
            row = first + r
            kept = taps_a[pl.ds((row + 1) * depth + channels, channels), :].astype(F32)
            grid = kept + update[r * channels : (r + 1) * channels]
            if 1 <= row <= height:
                grid_ref[pl.ds((row - 1) * channels, channels), :] = grid
            place_taps(taps_b, row, jnp.maximum(grid, 0.0) * inside_ref[pl.ds(row + 1, 1), :])
    for first in range(0, height, groups):
        span = min(groups, height - first)
        conv = dot(conv_b[span][...], taps_b[pl.ds(first * depth, (span + 2) * depth), :])
        update = dot(mix_b[span][...], jnp.maximum(conv, 0.0).astype(BF16))
        rows = pl.ds(first * channels, span * channels)
        final_ref[rows, :] = jnp.maximum(grid_ref[rows, :] + update, 0.0).astype(BF16)
    targets = head_ref.shape[0] // height
    contact = dot(head_ref[...], final_ref[...]).reshape(targets, height, lanes)

    stitched = []
    map_row = lax.broadcasted_iota(jnp.int32, (height, lanes), 0)
    for t in range(targets):
        band = None
        skewed = contact[t]
        for bit in range((height - 1).bit_length()):
            turned = pltpu.roll(skewed, lanes - (1 << bit), 1)
            skewed = jnp.where((map_row >> bit) & 1 == 1, turned, skewed)
        for b in range(BLOCKS):
            first, reach = offsets[b] + margin, BINS - STRIDE * b
            piece = skewed[:, first : first + reach]
            if reach < BINS:
                piece = jnp.concatenate([piece, jnp.zeros((height, BINS - reach), F32)], axis=1)
            piece = piece * stitch_ref[b]
            band = piece if band is None else band + piece
        stitched_ref[t] = band
        stitched.append(band[:, : 2 * STRIDE])

    near = jnp.concatenate(stitched, axis=0)
    wide = 2 * STRIDE
    col = lax.broadcasted_iota(jnp.int32, (wide, wide), 0)
    corner = lax.broadcasted_iota(jnp.int32, (wide, wide), 1)
    box = ((col > corner) & (col <= corner + STRIDE) & (corner < STRIDE)).astype(F32)
    square = jnp.dot(near, box, preferred_element_type=F32, precision=lax.Precision.HIGHEST)
    at = lax.broadcasted_iota(jnp.int32, near.shape, 1)
    contact = jnp.where((at >= 1) & (at <= STRIDE), jnp.exp(near), 0.0)
    down = jnp.sum(contact, axis=1, keepdims=True)
    here = lax.broadcasted_iota(jnp.int32, (height, wide), 0)
    there = lax.broadcasted_iota(jnp.int32, (height, wide), 1)

    def by_row(values):
        rows = []
        for t in range(targets):
            own = pltpu.roll(
                values[t * height : (t + 1) * height], 0, 1, stride=1, stride_axis=0
            )
            rows.append(jnp.sum(own, axis=0, keepdims=True))
        return rows

    down_rows = []
    for t in range(targets):
        own = jnp.where(here == there, down[t * height : (t + 1) * height], 0.0)
        down_rows.append(jnp.sum(own, axis=0, keepdims=True))
    rows = by_row(square) + by_row(contact)
    own = (place_ref[1] * (STRIDE // height) + place_ref[0]) * height
    missing = STRIDE - own - lax.broadcasted_iota(jnp.int32, (1, LANES), 1)
    missing = jnp.maximum(missing, 0).astype(F32)
    up_rows = [row + missing for row in rows[targets:]]
    keep_ref[...] = jnp.concatenate(rows[:targets] + up_rows + down_rows, axis=0)
    per_row = LANES // height
    first = lax.broadcasted_iota(jnp.int32, (per_row, LANES), 1) < height
    packs = [
        jnp.concatenate(
            rows[p : p + per_row]
            + [jnp.zeros((1, LANES), F32)] * (per_row - len(rows[p : p + per_row])),
            axis=0,
        )
        for p in range(0, len(rows), per_row)
    ]
    for k in range(1, STRIDE // height + 1):
        packed = []
        for pack in packs:
            turned = jnp.where(first, pltpu.roll(pack, LANES - k * height, 1), 0.0)
            turned = pltpu.roll(turned, 0, 1, stride=height, stride_axis=0)
            packed.append(jnp.sum(turned, axis=0, keepdims=True))

        send_ref[lax.rem(place_ref[0] + k, STRIDE // height)] = jnp.concatenate(packed, axis=0)


def finish_kernel(height, keep_ref, got_ref, out_ref):
    targets = out_ref.shape[0]
    per_row = LANES // height
    keep = keep_ref[...][:, :height]
    got = jnp.sum(got_ref[...], axis=0)
    rows = []
    for q in range(2 * targets):
        at = (q % per_row) * height
        rows.append(got[q // per_row : q // per_row + 1, at : at + height])
    sums = keep[: 2 * targets] + jnp.concatenate(rows, axis=0)
    upstream = sums[targets:]
    downstream = keep[2 * targets :]
    insulation = sums[:targets] / (STRIDE * STRIDE)
    direction = (downstream - upstream) / (downstream + upstream)
    for t in range(targets):
        out_ref[t] = jnp.concatenate([insulation[t : t + 1], direction[t : t + 1]], axis=0)


def per_device(
    genome_bases,
    stitch_weight,
    stem_weight,
    trunk_in,
    trunk_out,
    pair_weight,
    distance_rate,
    tower_conv,
    tower_mix,
    head_weight,
):
    towers = lax.axis_size("tower")
    height = STRIDE // towers
    tower_index = lax.axis_index("tower")
    genome_index = lax.axis_index("genome")
    own = stem(genome_bases, stem_weight, lax.axis_size("genome"))
    features = lax.all_to_all(own, "genome", 0, 0, tiled=True)
    groups = 3
    channels = distance_rate.shape[0]
    targets = head_weight.shape[0]
    place = jnp.stack([tower_index, genome_index]).astype(jnp.int32)
    lanes = segments(2)[2]
    packs = -(-2 * targets * height // LANES)
    vmem = pl.BlockSpec(memory_space=pltpu.VMEM)
    smem = pl.BlockSpec(memory_space=pltpu.SMEM)
    layers, mid, width = trunk_in.shape
    rows = height + 4
    shapes = [
        jax.ShapeDtypeStruct((layers, 3 * mid, width // 3), BF16),
        jax.ShapeDtypeStruct((channels, LANES), F32),
        jax.ShapeDtypeStruct((rows, lanes), F32),
        jax.ShapeDtypeStruct((rows, lanes), F32),
        jax.ShapeDtypeStruct((targets * height, height * channels), BF16),
        jax.ShapeDtypeStruct((BLOCKS, height, BINS), F32),
    ]
    for count in (height + 2, height):
        for span in spans_of(count, groups):
            tall = span * channels
            shapes.append(jax.ShapeDtypeStruct((tall, (span + 2) * 3 * channels), BF16))
            shapes.append(jax.ShapeDtypeStruct((tall, tall), BF16))
    prepared = pl.pallas_call(
        functools.partial(prepare_kernel, height, groups),
        out_shape=shapes,
        in_specs=[smem, pl.BlockSpec(memory_space=pltpu.HBM)] + [vmem] * 6,
        out_specs=[vmem] * len(shapes),
        compiler_params=pltpu.CompilerParams(vmem_limit_bytes=8 * 1024 * 1024),
        cost_estimate=pl.CostEstimate(flops=10**9, bytes_accessed=1 << 22, transcendentals=0),
        name="prepare",
    )(
        place,
        own,
        trunk_in,
        distance_rate.reshape(1, channels),
        tower_conv,
        tower_mix,
        head_weight,
        stitch_weight.reshape(1, BINS),
    )
    stitched, keep, send = pl.pallas_call(
        functools.partial(main_kernel, height, groups),
        out_shape=[
            jax.ShapeDtypeStruct((targets, height, BINS), F32),
            jax.ShapeDtypeStruct((3 * targets, LANES), F32),
            jax.ShapeDtypeStruct((towers, packs, LANES), F32),
        ],
        in_specs=[smem] + [vmem] * (3 + len(shapes)),
        out_specs=[vmem] * 3,
        scratch_shapes=[
            pltpu.VMEM((rows * 3 * channels, lanes), BF16),
            pltpu.VMEM(((height + 2) * 3 * channels, lanes), BF16),
            pltpu.VMEM((height * channels, lanes), F32),
            pltpu.VMEM((height * channels, lanes), BF16),
        ],
        compiler_params=pltpu.CompilerParams(vmem_limit_bytes=VMEM_BYTES),
        name="windows",
    )(place, features, jnp.transpose(trunk_out, (0, 2, 1)), pair_weight, *prepared)
    starts = lax.axis_size("genome")
    passed = lax.ppermute(send, "genome", [(i, i + 1) for i in range(starts - 1)])
    ahead = (jnp.arange(towers) > tower_index)[:, None, None]
    got = lax.all_to_all(jnp.where(ahead, send, passed), "tower", 0, 0, tiled=True)
    scores = pl.pallas_call(
        functools.partial(finish_kernel, height),
        out_shape=jax.ShapeDtypeStruct((targets, 2, height), F32),
        in_specs=[vmem, vmem],
        out_specs=vmem,
        compiler_params=pltpu.CompilerParams(vmem_limit_bytes=2 * 1024 * 1024),
        name="finish",
    )(keep, got)
    return (stitched, jnp.transpose(scores, (1, 0, 2)))


def solution(mesh):
    placed = (P("genome"), P(), P(), P(), P(), P(), P(), P(), P(), P())
    return jax.shard_map(
        per_device,
        mesh=mesh,
        in_specs=placed,
        out_specs=(P(None, ("genome", "tower"), None), P(None, None, ("genome", "tower"))),
        check_vma=False,
    )
```

```python
import functools

import jax
import jax.numpy as jnp
from jax import lax
from jax.experimental import pallas as pl
from jax.experimental.pallas import tpu as pltpu
from jax.sharding import PartitionSpec as P

BP = 2048
STRIDE = 64
BINS = 256
BLOCKS = BINS // STRIDE
LANES = 128
F32 = jnp.float32
BF16 = jnp.bfloat16
VMEM_BYTES = 40 * 1024 * 1024


def dot(a, b):
    return jnp.dot(a, b, preferred_element_type=F32)


def stem_kernel(bins, bases_hbm, weight_hbm, out_ref, bases, weight, base_sem, weight_sem):
    groups = BP // LANES
    chunks = weight.shape[0]
    span = weight.shape[2]
    base_copy = pltpu.make_async_copy(bases_hbm, bases, base_sem)
    base_copy.start()
    copies = []
    for k in range(chunks):
        copy = pltpu.make_async_copy(
            weight_hbm.at[:, pl.ds(k * span, span)], weight.at[k], weight_sem.at[k]
        )
        copy.start()
        copies.append(copy)
    row = lax.broadcasted_iota(jnp.int32, (LANES, 4 * LANES), 0)
    col = lax.broadcasted_iota(jnp.int32, (LANES, 4 * LANES), 1)
    repeat = (row == col // 4).astype(F32).astype(BF16)
    letter = (lax.broadcasted_iota(jnp.int32, (bins, 4 * LANES), 1) % 4).astype(F32)
    base_copy.wait()
    total = None
    per_chunk = groups // chunks
    for k in range(chunks):
        hot = []
        for q in range(per_chunk):
            rows = bases[pl.ds(k * per_chunk + q, bins, stride=groups), :]
            spread = dot(rows.astype(F32).astype(BF16), repeat)
            hot.append(jnp.where(spread == letter, 1.0, 0.0).astype(BF16))
        hot = jnp.concatenate(hot, axis=1)
        copies[k].wait()
        part = lax.dot_general(
            weight[k], hot, (((1,), (1,)), ((), ())), preferred_element_type=F32
        )
        total = part if total is None else total + part
    total = total.astype(BF16)
    half = out_ref.shape[1]
    packed = jnp.concatenate([total[:half], total[half:]], axis=1)
    for slot in range(out_ref.shape[0]):
        out_ref[slot] = packed


def stem(genome_bases, stem_weight, slots):
    bins = genome_bases.shape[0] // BP
    channels, depth = stem_weight.shape
    chunks = 4
    return pl.pallas_call(
        functools.partial(stem_kernel, bins),
        out_shape=jax.ShapeDtypeStruct((slots, channels // 2, 2 * bins), BF16),
        in_specs=[pl.BlockSpec(memory_space=pltpu.HBM)] * 2,
        out_specs=pl.BlockSpec(memory_space=pltpu.VMEM),
        scratch_shapes=[
            pltpu.VMEM((genome_bases.shape[0] // LANES, LANES), jnp.int32),
            pltpu.VMEM((chunks, channels, depth // chunks), BF16),
            pltpu.SemaphoreType.DMA,
            pltpu.SemaphoreType.DMA((chunks,)),
        ],
        compiler_params=pltpu.CompilerParams(vmem_limit_bytes=63 * 1024 * 1024),
        name="stem",
    )(genome_bases.reshape(-1, LANES), stem_weight)


def banded(kernel, rows):
    taps, out_channels, depth = kernel.shape
    flat = jnp.concatenate([kernel[u] for u in range(taps)], axis=1)
    bands = []
    for r in range(rows):
        parts = [flat]
        if r:
            parts.insert(0, jnp.zeros((out_channels, r * depth), BF16))
        if rows - 1 - r:
            parts.append(jnp.zeros((out_channels, (rows - 1 - r) * depth), BF16))
        bands.append(jnp.concatenate(parts, axis=1) if len(parts) > 1 else flat)
    return jnp.concatenate(bands, axis=0)


def block_diagonal(matrix, count):
    height, width = matrix.shape
    tiled = jnp.concatenate([jnp.concatenate([matrix] * count, axis=1)] * count, axis=0)
    row = lax.broadcasted_iota(jnp.int32, tiled.shape, 0) // height
    col = lax.broadcasted_iota(jnp.int32, tiled.shape, 1) // width
    return jnp.where(row == col, tiled, jnp.zeros((), BF16))


def head_by_row(head, count):
    targets, width = head.shape
    wide = jnp.concatenate([head] * count, axis=1)
    tall = jnp.broadcast_to(wide[:, None, :], (targets, count, count * width))
    row = lax.broadcasted_iota(jnp.int32, tall.shape, 1)
    col = lax.broadcasted_iota(jnp.int32, tall.shape, 2) // width
    return jnp.where(row == col, tall, jnp.zeros((), BF16)).reshape(targets * count, count * width)


def segments(margin):
    sizes = [BINS - STRIDE * b + margin + 1 for b in range(BLOCKS)]
    offsets = [sum(sizes[:b]) for b in range(BLOCKS)]
    lanes = -(-sum(sizes) // LANES) * LANES
    return sizes, offsets, lanes


def shifted(values, offset):
    if offset == 0:
        return values
    channels, extent = values.shape
    edge = jnp.zeros((channels, abs(offset)), values.dtype)
    if offset >= 0:
        return jnp.concatenate([values[:, offset:], edge], axis=1)
    return jnp.concatenate([edge, values[:, : extent + offset]], axis=1)


def spans_of(rows, groups):
    return sorted({groups, rows % groups} - {0})


def prepare_kernel(
    height,
    groups,
    place_ref,
    _,
    trunk_in,
    rate_in,
    conv_in,
    mix_in,
    head_in,
    stitch_in,
    trunk_ref,
    rate_ref,
    decay_ref,
    inside_ref,
    head_ref,
    stitch_ref,
    *conv_refs,
):
    margin = 2
    sizes, offsets, lanes = segments(margin)
    tower_row = place_ref[0] * height
    for layer in range(trunk_in.shape[0]):
        flat = trunk_in[layer]
        width = flat.shape[1] // 3
        trunk_ref[layer] = jnp.concatenate(
            [flat[:, q * width : (q + 1) * width] for q in range(3)], axis=0
        )
    at = 0
    for block, rows in enumerate((height + 2, height)):
        for span in spans_of(rows, groups):
            conv_refs[at][...] = banded(conv_in[block], span)
            conv_refs[at + 1][...] = block_diagonal(mix_in[block], span)
            at += 2
    head_ref[...] = head_by_row(head_in[...], height)
    channels = rate_in.shape[1]
    row = lax.broadcasted_iota(jnp.int32, (channels, channels), 0)
    col = lax.broadcasted_iota(jnp.int32, (channels, channels), 1)
    rate = jnp.sum(jnp.where(row == col, rate_in[...], 0.0), axis=1, keepdims=True)
    rate_ref[...] = jnp.broadcast_to(rate, rate_ref.shape)

    lane = lax.broadcasted_iota(jnp.int32, (height + 2 * margin, lanes), 1)
    block_of = jnp.zeros((height + 2 * margin, lanes), jnp.int32)
    start_of = jnp.zeros((height + 2 * margin, lanes), jnp.int32)
    for b in range(1, BLOCKS):
        block_of = jnp.where(lane >= offsets[b], b, block_of)
        start_of = jnp.where(lane >= offsets[b], offsets[b], start_of)
    step = lane - start_of
    first_row = STRIDE * block_of + tower_row - margin
    column = first_row + step
    in_column = (column < BINS) & (column >= 0)

    row = lax.broadcasted_iota(jnp.int32, (height + 2 * margin, lanes), 0)
    decay_ref[...] = jnp.log1p(jnp.abs(step - row).astype(F32))
    at = first_row + row
    inside_ref[...] = jnp.where(in_column & (at >= 0) & (at < BINS), 1.0, 0.0)

    local = lax.broadcasted_iota(jnp.int32, (height, BINS), 0)
    ahead = lax.broadcasted_iota(jnp.int32, (height, BINS), 1)
    weight_sum = jnp.zeros((height, BINS), F32)
    weights = []
    for b in range(BLOCKS):
        weight = jnp.where(ahead == STRIDE * b + tower_row + local, stitch_in[...], 0)
        weight = jnp.sum(weight.astype(F32), axis=1, keepdims=True)
        weight = jnp.where(place_ref[1] >= b, weight, 0.0)
        reach = STRIDE * b + tower_row + local + ahead < BINS
        weight = jnp.where(reach, weight, 0.0)
        weights.append(weight)
        weight_sum = weight_sum + weight
    scale = 1.0 / jnp.maximum(weight_sum, 1.0)
    for b in range(BLOCKS):
        stitch_ref[b] = weights[b] * scale


def main_kernel(
    height,
    groups,
    place_ref,
    features,
    trunk_out,
    pair_weight,
    trunk_in,
    rate_ref,
    decay_ref,
    inside_ref,
    head_ref,
    stitch_ref,
    *rest,
):
    margin = 2
    sizes, offsets, lanes = segments(margin)
    tower_row = place_ref[0] * height
    channels = rate_ref.shape[0]
    depth = 3 * channels
    rest = list(rest)
    conv_a, conv_b, mix_a, mix_b = {}, {}, {}, {}
    for span in spans_of(height + 2, groups):
        conv_a[span], mix_a[span] = rest.pop(0), rest.pop(0)
    for span in spans_of(height, groups):
        conv_b[span], mix_b[span] = rest.pop(0), rest.pop(0)
    stitched_ref, keep_ref, send_ref, taps_a, taps_b, grid_ref, final_ref, squeezed_ref = rest

    starts = features.shape[0]
    blocks = []
    for d in range(1 - BLOCKS, BLOCKS):
        at = place_ref[1] + d
        block = features[jnp.clip(at, 0, starts - 1)]
        blocks.append(jnp.where((at >= 0) & (at < starts), block, jnp.zeros_like(block)))
    blocks = jnp.concatenate(
        [
            jnp.concatenate([half[:, :STRIDE] for half in blocks], axis=1),
            jnp.concatenate([half[:, STRIDE:] for half in blocks], axis=1),
        ],
        axis=0,
    )
    extent = BINS
    windows = []
    for b in range(BLOCKS):
        first = (BLOCKS - 1 - b) * STRIDE
        windows.append(blocks[:, first : first + BINS].astype(F32))
    stream = jnp.concatenate(windows, axis=1)
    layers = trunk_in.shape[0]
    for layer in range(layers):
        dilation = max(1, extent // 2 ** (layers - layer))
        active = jnp.maximum(stream, 0.0).astype(BF16)
        mid = trunk_in.shape[1] // 3
        taps = dot(trunk_in[layer], active)
        inner = taps[mid : 2 * mid] + jnp.concatenate(
            [
                shifted(taps[:mid, b * BINS : (b + 1) * BINS], -dilation)
                + shifted(taps[2 * mid :, b * BINS : (b + 1) * BINS], dilation)
                for b in range(BLOCKS)
            ],
            axis=1,
        )
        squeezed = jax.nn.relu(inner).astype(BF16)
        stream = stream + lax.dot_general(
            trunk_out[layer], squeezed, (((0,), (0,)), ((), ())), preferred_element_type=F32
        )
    projected = dot(pair_weight[...], jax.nn.relu(stream).astype(BF16))

    right = []
    left = []
    for b in range(BLOCKS):
        begin = STRIDE * b + tower_row - margin
        turn = jnp.where(begin > 0, BINS - begin, -begin)
        terms = projected[:, b * BINS : (b + 1) * BINS]
        turned = pltpu.roll(terms, turn, 1)
        left.append(turned[:channels, :LANES])
        own = turned[channels:]
        if sizes[b] > BINS:
            own = jnp.concatenate([own, own[:, : sizes[b] - BINS]], axis=1)
        right.append(own[:, : sizes[b]])
    used = sum(sizes)
    if lanes > used:
        right.append(jnp.zeros((channels, lanes - used), F32))
    right = jnp.concatenate(right, axis=1)
    rate = jnp.concatenate([rate_ref[...]] * (lanes // LANES), axis=1)
    lane = lax.broadcasted_iota(jnp.int32, (1, lanes), 1)

    def place_taps(ref, slot, act):
        act = act.astype(BF16)
        ref[pl.ds(slot * depth, channels), :] = pltpu.roll(act, 1, 1)
        ref[pl.ds(slot * depth + channels, channels), :] = act
        ref[pl.ds(slot * depth + 2 * channels, channels), :] = pltpu.roll(act, lanes - 1, 1)

    for row in range(height + 2 * margin):
        tiles = []
        for tile in range(lanes // LANES):
            piece = None
            here = lane[:, tile * LANES : (tile + 1) * LANES]
            for b in range(BLOCKS):
                low, high = offsets[b], offsets[b] + sizes[b]
                if high <= tile * LANES or low >= (tile + 1) * LANES:
                    continue
                spread = jnp.broadcast_to(left[b][:, row : row + 1], (channels, LANES))
                piece = spread if piece is None else jnp.where(here >= low, spread, piece)
            tiles.append(piece)
        mixed = jnp.concatenate(tiles, axis=1) + right - rate * decay_ref[pl.ds(row, 1), :]
        place_taps(taps_a, row, jnp.maximum(mixed, 0.0) * inside_ref[pl.ds(row, 1), :])

    def convolve(kernels, taps, rows):
        for first in range(0, rows, groups):
            span = min(groups, rows - first)
            conv = dot(kernels[span][...], taps[pl.ds(first * depth, (span + 2) * depth), :])
            squeezed_ref[pl.ds(first * channels, span * channels), :] = jnp.maximum(
                conv, 0.0
            ).astype(BF16)

    convolve(conv_a, taps_a, height + 2)
    for first in range(0, height + 2, groups):
        span = min(groups, height + 2 - first)
        update = dot(
            mix_a[span][...], squeezed_ref[pl.ds(first * channels, span * channels), :]
        )
        for r in range(span):
            row = first + r
            kept = taps_a[pl.ds((row + 1) * depth + channels, channels), :].astype(F32)
            grid = kept + update[r * channels : (r + 1) * channels]
            if 1 <= row <= height:
                grid_ref[pl.ds((row - 1) * channels, channels), :] = grid
            place_taps(taps_b, row, jnp.maximum(grid, 0.0) * inside_ref[pl.ds(row + 1, 1), :])
    convolve(conv_b, taps_b, height)
    for first in range(0, height, groups):
        span = min(groups, height - first)
        rows = pl.ds(first * channels, span * channels)
        update = dot(mix_b[span][...], squeezed_ref[rows, :])
        final_ref[rows, :] = jnp.maximum(grid_ref[rows, :] + update, 0.0).astype(BF16)
    targets = head_ref.shape[0] // height
    contact = dot(head_ref[...], final_ref[...]).reshape(targets, height, lanes)

    stitched = []
    map_row = lax.broadcasted_iota(jnp.int32, (height, lanes), 0)
    for t in range(targets):
        band = None
        skewed = contact[t]
        for bit in range((height - 1).bit_length()):
            turned = pltpu.roll(skewed, lanes - (1 << bit), 1)
            skewed = jnp.where((map_row >> bit) & 1 == 1, turned, skewed)
        for b in range(BLOCKS):
            first, reach = offsets[b] + margin, BINS - STRIDE * b
            piece = skewed[:, first : first + reach]
            if reach < BINS:
                piece = jnp.concatenate([piece, jnp.zeros((height, BINS - reach), F32)], axis=1)
            piece = piece * stitch_ref[b]
            band = piece if band is None else band + piece
        stitched_ref[t] = band
        stitched.append(band[:, : 2 * STRIDE])

    near = jnp.concatenate(stitched, axis=0)
    wide = 2 * STRIDE
    col = lax.broadcasted_iota(jnp.int32, (wide, wide), 0)
    corner = lax.broadcasted_iota(jnp.int32, (wide, wide), 1)
    box = ((col > corner) & (col <= corner + STRIDE) & (corner < STRIDE)).astype(F32)
    square = jnp.dot(near, box, preferred_element_type=F32, precision=lax.Precision.HIGHEST)
    at = lax.broadcasted_iota(jnp.int32, near.shape, 1)
    contact = jnp.where((at >= 1) & (at <= STRIDE), jnp.exp(near), 0.0)
    down = jnp.sum(contact, axis=1, keepdims=True)
    here = lax.broadcasted_iota(jnp.int32, (height, wide), 0)
    there = lax.broadcasted_iota(jnp.int32, (height, wide), 1)

    def by_row(values):
        rows = []
        for t in range(targets):
            own = pltpu.roll(
                values[t * height : (t + 1) * height], 0, 1, stride=1, stride_axis=0
            )
            rows.append(jnp.sum(own, axis=0, keepdims=True))
        return rows

    down_rows = []
    for t in range(targets):
        own = jnp.where(here == there, down[t * height : (t + 1) * height], 0.0)
        down_rows.append(jnp.sum(own, axis=0, keepdims=True))
    rows = by_row(square) + by_row(contact)
    own = (place_ref[1] * (STRIDE // height) + place_ref[0]) * height
    missing = STRIDE - own - lax.broadcasted_iota(jnp.int32, (1, LANES), 1)
    missing = jnp.maximum(missing, 0).astype(F32)
    up_rows = [row + missing for row in rows[targets:]]
    keep_ref[...] = jnp.concatenate(rows[:targets] + up_rows + down_rows, axis=0)
    per_row = LANES // height
    first = lax.broadcasted_iota(jnp.int32, (per_row, LANES), 1) < height
    packs = [
        jnp.concatenate(
            rows[p : p + per_row]
            + [jnp.zeros((1, LANES), F32)] * (per_row - len(rows[p : p + per_row])),
            axis=0,
        )
        for p in range(0, len(rows), per_row)
    ]
    for k in range(1, STRIDE // height + 1):
        packed = []
        for pack in packs:
            turned = jnp.where(first, pltpu.roll(pack, LANES - k * height, 1), 0.0)
            turned = pltpu.roll(turned, 0, 1, stride=height, stride_axis=0)
            packed.append(jnp.sum(turned, axis=0, keepdims=True))

        send_ref[lax.rem(place_ref[0] + k, STRIDE // height)] = jnp.concatenate(packed, axis=0)


def finish_kernel(height, keep_ref, got_ref, out_ref):
    targets = out_ref.shape[0]
    per_row = LANES // height
    keep = keep_ref[...][:, :height]
    got = jnp.sum(got_ref[...], axis=0)
    rows = []
    for q in range(2 * targets):
        at = (q % per_row) * height
        rows.append(got[q // per_row : q // per_row + 1, at : at + height])
    sums = keep[: 2 * targets] + jnp.concatenate(rows, axis=0)
    upstream = sums[targets:]
    downstream = keep[2 * targets :]
    insulation = sums[:targets] / (STRIDE * STRIDE)
    direction = (downstream - upstream) / (downstream + upstream)
    for t in range(targets):
        out_ref[t] = jnp.concatenate([insulation[t : t + 1], direction[t : t + 1]], axis=0)


def per_device(
    genome_bases,
    stitch_weight,
    stem_weight,
    trunk_in,
    trunk_out,
    pair_weight,
    distance_rate,
    tower_conv,
    tower_mix,
    head_weight,
):
    towers = lax.axis_size("tower")
    height = STRIDE // towers
    tower_index = lax.axis_index("tower")
    genome_index = lax.axis_index("genome")
    own = stem(genome_bases, stem_weight, lax.axis_size("genome"))
    features = lax.all_to_all(own, "genome", 0, 0, tiled=True)
    groups = 3
    channels = distance_rate.shape[0]
    targets = head_weight.shape[0]
    place = jnp.stack([tower_index, genome_index]).astype(jnp.int32)
    lanes = segments(2)[2]
    packs = -(-2 * targets * height // LANES)
    vmem = pl.BlockSpec(memory_space=pltpu.VMEM)
    smem = pl.BlockSpec(memory_space=pltpu.SMEM)
    layers, mid, width = trunk_in.shape
    rows = height + 4
    shapes = [
        jax.ShapeDtypeStruct((layers, 3 * mid, width // 3), BF16),
        jax.ShapeDtypeStruct((channels, LANES), F32),
        jax.ShapeDtypeStruct((rows, lanes), F32),
        jax.ShapeDtypeStruct((rows, lanes), F32),
        jax.ShapeDtypeStruct((targets * height, height * channels), BF16),
        jax.ShapeDtypeStruct((BLOCKS, height, BINS), F32),
    ]
    for count in (height + 2, height):
        for span in spans_of(count, groups):
            tall = span * channels
            shapes.append(jax.ShapeDtypeStruct((tall, (span + 2) * 3 * channels), BF16))
            shapes.append(jax.ShapeDtypeStruct((tall, tall), BF16))
    prepared = pl.pallas_call(
        functools.partial(prepare_kernel, height, groups),
        out_shape=shapes,
        in_specs=[smem, pl.BlockSpec(memory_space=pltpu.HBM)] + [vmem] * 6,
        out_specs=[vmem] * len(shapes),
        compiler_params=pltpu.CompilerParams(vmem_limit_bytes=8 * 1024 * 1024),
        cost_estimate=pl.CostEstimate(flops=10**9, bytes_accessed=1 << 22, transcendentals=0),
        name="prepare",
    )(
        place,
        own,
        trunk_in,
        distance_rate.reshape(1, channels),
        tower_conv,
        tower_mix,
        head_weight,
        stitch_weight.reshape(1, BINS),
    )
    stitched, keep, send = pl.pallas_call(
        functools.partial(main_kernel, height, groups),
        out_shape=[
            jax.ShapeDtypeStruct((targets, height, BINS), F32),
            jax.ShapeDtypeStruct((3 * targets, LANES), F32),
            jax.ShapeDtypeStruct((towers, packs, LANES), F32),
        ],
        in_specs=[smem] + [vmem] * (3 + len(shapes)),
        out_specs=[vmem] * 3,
        scratch_shapes=[
            pltpu.VMEM((rows * 3 * channels, lanes), BF16),
            pltpu.VMEM(((height + 2) * 3 * channels, lanes), BF16),
            pltpu.VMEM((height * channels, lanes), F32),
            pltpu.VMEM((height * channels, lanes), BF16),
            pltpu.VMEM(((height + 2) * channels, lanes), BF16),
        ],
        compiler_params=pltpu.CompilerParams(vmem_limit_bytes=VMEM_BYTES),
        name="windows",
    )(place, features, jnp.transpose(trunk_out, (0, 2, 1)), pair_weight, *prepared)
    starts = lax.axis_size("genome")
    passed = lax.ppermute(send, "genome", [(i, i + 1) for i in range(starts - 1)])
    ahead = (jnp.arange(towers) > tower_index)[:, None, None]
    got = lax.all_to_all(jnp.where(ahead, send, passed), "tower", 0, 0, tiled=True)
    scores = pl.pallas_call(
        functools.partial(finish_kernel, height),
        out_shape=jax.ShapeDtypeStruct((targets, 2, height), F32),
        in_specs=[vmem, vmem],
        out_specs=vmem,
        compiler_params=pltpu.CompilerParams(vmem_limit_bytes=2 * 1024 * 1024),
        name="finish",
    )(keep, got)
    return (stitched, jnp.transpose(scores, (1, 0, 2)))


def solution(mesh):
    placed = (P("genome"), P(), P(), P(), P(), P(), P(), P(), P(), P())
    return jax.shard_map(
        per_device,
        mesh=mesh,
        in_specs=placed,
        out_specs=(P(None, ("genome", "tower"), None), P(None, None, ("genome", "tower"))),
        check_vma=False,
    )
```

```python
import functools

import jax
import jax.numpy as jnp
from jax import lax
from jax.experimental import pallas as pl
from jax.experimental.pallas import tpu as pltpu
from jax.sharding import PartitionSpec as P

BP = 2048
STRIDE = 64
BINS = 256
BLOCKS = BINS // STRIDE
LANES = 128
F32 = jnp.float32
BF16 = jnp.bfloat16
VMEM_BYTES = 40 * 1024 * 1024


def dot(a, b):
    return jnp.dot(a, b, preferred_element_type=F32)


def stem_kernel(bins, bases_hbm, weight_hbm, out_ref, bases, weight, base_sem, weight_sem):
    groups = BP // LANES
    chunks = weight.shape[0]
    span = weight.shape[2]
    base_copy = pltpu.make_async_copy(bases_hbm, bases, base_sem)
    base_copy.start()
    copies = []
    for k in range(chunks):
        copy = pltpu.make_async_copy(
            weight_hbm.at[:, pl.ds(k * span, span)], weight.at[k], weight_sem.at[k]
        )
        copy.start()
        copies.append(copy)
    row = lax.broadcasted_iota(jnp.int32, (LANES, 4 * LANES), 0)
    col = lax.broadcasted_iota(jnp.int32, (LANES, 4 * LANES), 1)
    repeat = (row == col // 4).astype(F32).astype(BF16)
    letter = (lax.broadcasted_iota(jnp.int32, (bins, 4 * LANES), 1) % 4).astype(F32)
    base_copy.wait()
    total = None
    per_chunk = groups // chunks
    for k in range(chunks):
        hot = []
        for q in range(per_chunk):
            rows = bases[pl.ds(k * per_chunk + q, bins, stride=groups), :]
            spread = dot(rows.astype(F32).astype(BF16), repeat)
            hot.append(jnp.where(spread == letter, 1.0, 0.0).astype(BF16))
        hot = jnp.concatenate(hot, axis=1)
        copies[k].wait()
        part = lax.dot_general(
            weight[k], hot, (((1,), (1,)), ((), ())), preferred_element_type=F32
        )
        total = part if total is None else total + part
    total = total.astype(BF16)
    half = out_ref.shape[1]
    packed = jnp.concatenate([total[:half], total[half:]], axis=1)
    for slot in range(out_ref.shape[0]):
        out_ref[slot] = packed


def stem(genome_bases, stem_weight, slots):
    bins = genome_bases.shape[0] // BP
    channels, depth = stem_weight.shape
    chunks = 4
    return pl.pallas_call(
        functools.partial(stem_kernel, bins),
        out_shape=jax.ShapeDtypeStruct((slots, channels // 2, 2 * bins), BF16),
        in_specs=[pl.BlockSpec(memory_space=pltpu.HBM)] * 2,
        out_specs=pl.BlockSpec(memory_space=pltpu.VMEM),
        scratch_shapes=[
            pltpu.VMEM((genome_bases.shape[0] // LANES, LANES), jnp.int32),
            pltpu.VMEM((chunks, channels, depth // chunks), BF16),
            pltpu.SemaphoreType.DMA,
            pltpu.SemaphoreType.DMA((chunks,)),
        ],
        compiler_params=pltpu.CompilerParams(vmem_limit_bytes=63 * 1024 * 1024),
        name="stem",
    )(genome_bases.reshape(-1, LANES), stem_weight)


def banded(kernel, rows):
    taps, out_channels, depth = kernel.shape
    flat = jnp.concatenate([kernel[u] for u in range(taps)], axis=1)
    bands = []
    for r in range(rows):
        parts = [flat]
        if r:
            parts.insert(0, jnp.zeros((out_channels, r * depth), BF16))
        if rows - 1 - r:
            parts.append(jnp.zeros((out_channels, (rows - 1 - r) * depth), BF16))
        bands.append(jnp.concatenate(parts, axis=1) if len(parts) > 1 else flat)
    return jnp.concatenate(bands, axis=0)


def block_diagonal(matrix, count):
    height, width = matrix.shape
    tiled = jnp.concatenate([jnp.concatenate([matrix] * count, axis=1)] * count, axis=0)
    row = lax.broadcasted_iota(jnp.int32, tiled.shape, 0) // height
    col = lax.broadcasted_iota(jnp.int32, tiled.shape, 1) // width
    return jnp.where(row == col, tiled, jnp.zeros((), BF16))


def head_by_row(head, count):
    targets, width = head.shape
    wide = jnp.concatenate([head] * count, axis=1)
    tall = jnp.broadcast_to(wide[:, None, :], (targets, count, count * width))
    row = lax.broadcasted_iota(jnp.int32, tall.shape, 1)
    col = lax.broadcasted_iota(jnp.int32, tall.shape, 2) // width
    return jnp.where(row == col, tall, jnp.zeros((), BF16)).reshape(targets * count, count * width)


def segments(margin, height):
    whole = [BINS - STRIDE * b + margin + 1 for b in range(BLOCKS)]
    near = 2 * STRIDE + height - 1 + 2 * margin
    parts = [(b, b, whole[b]) for b in range(BLOCKS)]
    parts += [(b + 1, b, min(whole[b], near)) for b in range(BLOCKS)]
    sizes = [part[2] for part in parts]
    offsets = [sum(sizes[:k]) for k in range(len(sizes))]
    lanes = -(-sum(sizes) // LANES) * LANES
    return parts, offsets, lanes


def shifted(values, offset):
    if offset == 0:
        return values
    channels, extent = values.shape
    edge = jnp.zeros((channels, abs(offset)), values.dtype)
    if offset >= 0:
        return jnp.concatenate([values[:, offset:], edge], axis=1)
    return jnp.concatenate([edge, values[:, : extent + offset]], axis=1)


def spans_of(rows, groups):
    return sorted({groups, rows % groups} - {0})


def prepare_kernel(
    height,
    groups,
    place_ref,
    _,
    trunk_in,
    rate_in,
    conv_in,
    mix_in,
    head_in,
    stitch_in,
    trunk_ref,
    rate_ref,
    decay_ref,
    inside_ref,
    head_ref,
    stitch_ref,
    *conv_refs,
):
    margin = 2
    parts, offsets, lanes = segments(margin, height)
    tower_row = place_ref[0] * height
    for layer in range(trunk_in.shape[0]):
        flat = trunk_in[layer]
        width = flat.shape[1] // 3
        trunk_ref[layer] = jnp.concatenate(
            [flat[:, q * width : (q + 1) * width] for q in range(3)], axis=0
        )
    at = 0
    for block, rows in enumerate((height + 2, height)):
        for span in spans_of(rows, groups):
            conv_refs[at][...] = banded(conv_in[block], span)
            conv_refs[at + 1][...] = block_diagonal(mix_in[block], span)
            at += 2
    head_ref[...] = head_by_row(head_in[...], height)
    channels = rate_in.shape[1]
    row = lax.broadcasted_iota(jnp.int32, (channels, channels), 0)
    col = lax.broadcasted_iota(jnp.int32, (channels, channels), 1)
    rate = jnp.sum(jnp.where(row == col, rate_in[...], 0.0), axis=1, keepdims=True)
    rate_ref[...] = jnp.broadcast_to(rate, rate_ref.shape)

    lane = lax.broadcasted_iota(jnp.int32, (height + 2 * margin, lanes), 1)
    block_of = jnp.zeros((height + 2 * margin, lanes), jnp.int32)
    start_of = jnp.zeros((height + 2 * margin, lanes), jnp.int32)
    for (_, b, _), offset in zip(parts, offsets):
        block_of = jnp.where(lane >= offset, b, block_of)
        start_of = jnp.where(lane >= offset, offset, start_of)
    step = lane - start_of
    first_row = STRIDE * block_of + tower_row - margin
    column = first_row + step
    in_column = (column < BINS) & (column >= 0)

    row = lax.broadcasted_iota(jnp.int32, (height + 2 * margin, lanes), 0)
    decay_ref[...] = jnp.log1p(jnp.abs(step - row).astype(F32))
    at = first_row + row
    inside_ref[...] = jnp.where(in_column & (at >= 0) & (at < BINS), 1.0, 0.0)

    local = lax.broadcasted_iota(jnp.int32, (height, BINS), 0)
    ahead = lax.broadcasted_iota(jnp.int32, (height, BINS), 1)
    for back in range(2):
        weight_sum = jnp.zeros((height, BINS), F32)
        weights = []
        for b in range(BLOCKS):
            weight = jnp.where(ahead == STRIDE * b + tower_row + local, stitch_in[...], 0)
            weight = jnp.sum(weight.astype(F32), axis=1, keepdims=True)
            weight = jnp.where(place_ref[1] - back >= b, weight, 0.0)
            reach = STRIDE * b + tower_row + local + ahead < BINS
            weight = jnp.where(reach, weight, 0.0)
            weights.append(weight)
            weight_sum = weight_sum + weight
        scale = 1.0 / jnp.maximum(weight_sum, 1.0)
        for b in range(BLOCKS):
            stitch_ref[back * BLOCKS + b] = weights[b] * scale


def main_kernel(
    height,
    groups,
    place_ref,
    features,
    trunk_out,
    pair_weight,
    trunk_in,
    rate_ref,
    decay_ref,
    inside_ref,
    head_ref,
    stitch_ref,
    *rest,
):
    margin = 2
    parts, offsets, lanes = segments(margin, height)
    tower_row = place_ref[0] * height
    channels = rate_ref.shape[0]
    depth = 3 * channels
    rest = list(rest)
    conv_a, conv_b, mix_a, mix_b = {}, {}, {}, {}
    for span in spans_of(height + 2, groups):
        conv_a[span], mix_a[span] = rest.pop(0), rest.pop(0)
    for span in spans_of(height, groups):
        conv_b[span], mix_b[span] = rest.pop(0), rest.pop(0)
    stitched_ref, keep_ref, send_ref, taps_a, taps_b, grid_ref, final_ref, squeezed_ref = rest

    starts = features.shape[0]
    blocks = []
    for d in range(-BLOCKS, BLOCKS):
        at = place_ref[1] + d
        block = features[jnp.clip(at, 0, starts - 1)]
        blocks.append(jnp.where((at >= 0) & (at < starts), block, jnp.zeros_like(block)))
    blocks = jnp.concatenate(
        [
            jnp.concatenate([half[:, :STRIDE] for half in blocks], axis=1),
            jnp.concatenate([half[:, STRIDE:] for half in blocks], axis=1),
        ],
        axis=0,
    )
    extent = BINS
    windows = []
    for b in range(BLOCKS + 1):
        first = (BLOCKS - b) * STRIDE
        windows.append(blocks[:, first : first + BINS].astype(F32))
    stream = jnp.concatenate(windows, axis=1)
    layers = trunk_in.shape[0]
    for layer in range(layers):
        dilation = max(1, extent // 2 ** (layers - layer))
        active = jnp.maximum(stream, 0.0).astype(BF16)
        mid = trunk_in.shape[1] // 3
        taps = dot(trunk_in[layer], active)
        inner = taps[mid : 2 * mid] + jnp.concatenate(
            [
                shifted(taps[:mid, b * BINS : (b + 1) * BINS], -dilation)
                + shifted(taps[2 * mid :, b * BINS : (b + 1) * BINS], dilation)
                for b in range(BLOCKS + 1)
            ],
            axis=1,
        )
        squeezed = jax.nn.relu(inner).astype(BF16)
        stream = stream + lax.dot_general(
            trunk_out[layer], squeezed, (((0,), (0,)), ((), ())), preferred_element_type=F32
        )
    projected = dot(pair_weight[...], jax.nn.relu(stream).astype(BF16))

    right = []
    left = []
    for window, b, size in parts:
        begin = STRIDE * b + tower_row - margin
        turn = jnp.where(begin > 0, BINS - begin, -begin)
        terms = projected[:, window * BINS : (window + 1) * BINS]
        turned = pltpu.roll(terms, turn, 1)
        left.append(turned[:channels, :LANES])
        own = turned[channels:]
        if size > BINS:
            own = jnp.concatenate([own, own[:, : size - BINS]], axis=1)
        right.append(own[:, :size])
    used = sum(part[2] for part in parts)
    if lanes > used:
        right.append(jnp.zeros((channels, lanes - used), F32))
    right = jnp.concatenate(right, axis=1)
    rate = jnp.concatenate([rate_ref[...]] * (lanes // LANES), axis=1)
    lane = lax.broadcasted_iota(jnp.int32, (1, lanes), 1)

    def place_taps(ref, slot, act):
        act = act.astype(BF16)
        ref[pl.ds(slot * depth, channels), :] = pltpu.roll(act, 1, 1)
        ref[pl.ds(slot * depth + channels, channels), :] = act
        ref[pl.ds(slot * depth + 2 * channels, channels), :] = pltpu.roll(act, lanes - 1, 1)

    for row in range(height + 2 * margin):
        tiles = []
        for tile in range(lanes // LANES):
            piece = None
            here = lane[:, tile * LANES : (tile + 1) * LANES]
            for b in range(len(parts)):
                low, high = offsets[b], offsets[b] + parts[b][2]
                if high <= tile * LANES or low >= (tile + 1) * LANES:
                    continue
                spread = jnp.broadcast_to(left[b][:, row : row + 1], (channels, LANES))
                piece = spread if piece is None else jnp.where(here >= low, spread, piece)
            tiles.append(piece)
        mixed = jnp.concatenate(tiles, axis=1) + right - rate * decay_ref[pl.ds(row, 1), :]
        place_taps(taps_a, row, jnp.maximum(mixed, 0.0) * inside_ref[pl.ds(row, 1), :])

    def convolve(kernels, taps, rows):
        for first in range(0, rows, groups):
            span = min(groups, rows - first)
            conv = dot(kernels[span][...], taps[pl.ds(first * depth, (span + 2) * depth), :])
            squeezed_ref[pl.ds(first * channels, span * channels), :] = jnp.maximum(
                conv, 0.0
            ).astype(BF16)

    convolve(conv_a, taps_a, height + 2)
    for first in range(0, height + 2, groups):
        span = min(groups, height + 2 - first)
        update = dot(
            mix_a[span][...], squeezed_ref[pl.ds(first * channels, span * channels), :]
        )
        for r in range(span):
            row = first + r
            kept = taps_a[pl.ds((row + 1) * depth + channels, channels), :].astype(F32)
            grid = kept + update[r * channels : (r + 1) * channels]
            if 1 <= row <= height:
                grid_ref[pl.ds((row - 1) * channels, channels), :] = grid
            place_taps(taps_b, row, jnp.maximum(grid, 0.0) * inside_ref[pl.ds(row + 1, 1), :])
    convolve(conv_b, taps_b, height)
    for first in range(0, height, groups):
        span = min(groups, height - first)
        rows = pl.ds(first * channels, span * channels)
        update = dot(mix_b[span][...], squeezed_ref[rows, :])
        final_ref[rows, :] = jnp.maximum(grid_ref[rows, :] + update, 0.0).astype(BF16)
    targets = head_ref.shape[0] // height
    contact = dot(head_ref[...], final_ref[...]).reshape(targets, height, lanes)

    wide = 2 * STRIDE
    stitched, before = [], []
    map_row = lax.broadcasted_iota(jnp.int32, (height, lanes), 0)
    for t in range(targets):
        skewed = contact[t]
        for bit in range((height - 1).bit_length()):
            turned = pltpu.roll(skewed, lanes - (1 << bit), 1)
            skewed = jnp.where((map_row >> bit) & 1 == 1, turned, skewed)
        for back, width, bands in ((0, BINS, stitched), (1, wide, before)):
            band = None
            for b in range(BLOCKS):
                k = back * BLOCKS + b
                first, reach = offsets[k] + margin, min(width, BINS - STRIDE * b)
                piece = skewed[:, first : first + reach]
                if reach < width:
                    piece = jnp.concatenate(
                        [piece, jnp.zeros((height, width - reach), F32)], axis=1
                    )
                piece = piece * stitch_ref[k][:, :width]
                band = piece if band is None else band + piece
            bands.append(band)
        stitched_ref[t] = stitched[t]

    near = jnp.concatenate([band[:, :wide] for band in stitched] + before, axis=0)
    col = lax.broadcasted_iota(jnp.int32, (wide, wide), 0)
    corner = lax.broadcasted_iota(jnp.int32, (wide, wide), 1)
    box = ((col > corner) & (col <= corner + STRIDE) & (corner < STRIDE)).astype(F32)
    square = jnp.dot(near, box, preferred_element_type=F32, precision=lax.Precision.HIGHEST)
    at = lax.broadcasted_iota(jnp.int32, near.shape, 1)
    contact = jnp.where((at >= 1) & (at <= STRIDE), jnp.exp(near), 0.0)
    down = jnp.sum(contact, axis=1, keepdims=True)
    here = lax.broadcasted_iota(jnp.int32, (height, wide), 0)
    there = lax.broadcasted_iota(jnp.int32, (height, wide), 1)

    def by_row(values, back):
        rows = []
        for t in range(back * targets, (back + 1) * targets):
            own = pltpu.roll(
                values[t * height : (t + 1) * height], 0, 1, stride=1, stride_axis=0
            )
            rows.append(jnp.sum(own, axis=0, keepdims=True))
        return rows

    down_rows = []
    for t in range(targets):
        own = jnp.where(here == there, down[t * height : (t + 1) * height], 0.0)
        down_rows.append(jnp.sum(own, axis=0, keepdims=True))
    rows = by_row(square, 0) + by_row(contact, 0)
    rows_before = by_row(square, 1) + by_row(contact, 1)
    keep_ref[...] = jnp.concatenate(rows + down_rows, axis=0)
    per_row = LANES // height
    first = lax.broadcasted_iota(jnp.int32, (per_row, LANES), 1) < height
    def packs_of(rows):
        return [
            jnp.concatenate(
                rows[p : p + per_row]
                + [jnp.zeros((1, LANES), F32)] * (per_row - len(rows[p : p + per_row])),
                axis=0,
            )
            for p in range(0, len(rows), per_row)
        ]

    packs = list(zip(packs_of(rows), packs_of(rows_before)))
    for k in range(1, STRIDE // height + 1):
        same = place_ref[0] + k < STRIDE // height
        packed = []
        for own, previous in packs:
            turned = pltpu.roll(jnp.where(same, own, previous), LANES - k * height, 1)
            turned = pltpu.roll(
                jnp.where(first, turned, 0.0), 0, 1, stride=height, stride_axis=0
            )
            packed.append(jnp.sum(turned, axis=0, keepdims=True))
        send_ref[lax.rem(place_ref[0] + k, STRIDE // height)] = jnp.concatenate(packed, axis=0)


def finish_kernel(height, keep_ref, got_ref, out_ref):
    targets = out_ref.shape[0]
    per_row = LANES // height
    keep = keep_ref[...][:, :height]
    got = jnp.sum(got_ref[...], axis=0)
    rows = []
    for q in range(2 * targets):
        at = (q % per_row) * height
        rows.append(got[q // per_row : q // per_row + 1, at : at + height])
    sums = keep[: 2 * targets] + jnp.concatenate(rows, axis=0)
    upstream = sums[targets:]
    downstream = keep[2 * targets :]
    insulation = sums[:targets] / (STRIDE * STRIDE)
    direction = (downstream - upstream) / (downstream + upstream)
    for t in range(targets):
        out_ref[t] = jnp.concatenate([insulation[t : t + 1], direction[t : t + 1]], axis=0)


def per_device(
    genome_bases,
    stitch_weight,
    stem_weight,
    trunk_in,
    trunk_out,
    pair_weight,
    distance_rate,
    tower_conv,
    tower_mix,
    head_weight,
):
    towers = lax.axis_size("tower")
    height = STRIDE // towers
    tower_index = lax.axis_index("tower")
    genome_index = lax.axis_index("genome")
    own = stem(genome_bases, stem_weight, lax.axis_size("genome"))
    features = lax.all_to_all(own, "genome", 0, 0, tiled=True)
    groups = 3
    channels = distance_rate.shape[0]
    targets = head_weight.shape[0]
    place = jnp.stack([tower_index, genome_index]).astype(jnp.int32)
    lanes = segments(2, height)[2]
    packs = -(-2 * targets * height // LANES)
    vmem = pl.BlockSpec(memory_space=pltpu.VMEM)
    smem = pl.BlockSpec(memory_space=pltpu.SMEM)
    layers, mid, width = trunk_in.shape
    rows = height + 4
    shapes = [
        jax.ShapeDtypeStruct((layers, 3 * mid, width // 3), BF16),
        jax.ShapeDtypeStruct((channels, LANES), F32),
        jax.ShapeDtypeStruct((rows, lanes), F32),
        jax.ShapeDtypeStruct((rows, lanes), F32),
        jax.ShapeDtypeStruct((targets * height, height * channels), BF16),
        jax.ShapeDtypeStruct((2 * BLOCKS, height, BINS), F32),
    ]
    for count in (height + 2, height):
        for span in spans_of(count, groups):
            tall = span * channels
            shapes.append(jax.ShapeDtypeStruct((tall, (span + 2) * 3 * channels), BF16))
            shapes.append(jax.ShapeDtypeStruct((tall, tall), BF16))
    prepared = pl.pallas_call(
        functools.partial(prepare_kernel, height, groups),
        out_shape=shapes,
        in_specs=[smem, pl.BlockSpec(memory_space=pltpu.HBM)] + [vmem] * 6,
        out_specs=[vmem] * len(shapes),
        compiler_params=pltpu.CompilerParams(vmem_limit_bytes=8 * 1024 * 1024),
        cost_estimate=pl.CostEstimate(flops=10**9, bytes_accessed=1 << 22, transcendentals=0),
        name="prepare",
    )(
        place,
        own,
        trunk_in,
        distance_rate.reshape(1, channels),
        tower_conv,
        tower_mix,
        head_weight,
        stitch_weight.reshape(1, BINS),
    )
    stitched, keep, send = pl.pallas_call(
        functools.partial(main_kernel, height, groups),
        out_shape=[
            jax.ShapeDtypeStruct((targets, height, BINS), F32),
            jax.ShapeDtypeStruct((3 * targets, LANES), F32),
            jax.ShapeDtypeStruct((towers, packs, LANES), F32),
        ],
        in_specs=[smem] + [vmem] * (3 + len(shapes)),
        out_specs=[vmem] * 3,
        scratch_shapes=[
            pltpu.VMEM((rows * 3 * channels, lanes), BF16),
            pltpu.VMEM(((height + 2) * 3 * channels, lanes), BF16),
            pltpu.VMEM((height * channels, lanes), F32),
            pltpu.VMEM((height * channels, lanes), BF16),
            pltpu.VMEM(((height + 2) * channels, lanes), BF16),
        ],
        compiler_params=pltpu.CompilerParams(vmem_limit_bytes=VMEM_BYTES),
        name="windows",
    )(place, features, jnp.transpose(trunk_out, (0, 2, 1)), pair_weight, *prepared)
    got = lax.all_to_all(send, "tower", 0, 0, tiled=True)
    scores = pl.pallas_call(
        functools.partial(finish_kernel, height),
        out_shape=jax.ShapeDtypeStruct((targets, 2, height), F32),
        in_specs=[vmem, vmem],
        out_specs=vmem,
        compiler_params=pltpu.CompilerParams(vmem_limit_bytes=2 * 1024 * 1024),
        name="finish",
    )(keep, got)
    return (stitched, jnp.transpose(scores, (1, 0, 2)))


def solution(mesh):
    placed = (P("genome"), P(), P(), P(), P(), P(), P(), P(), P(), P())
    return jax.shard_map(
        per_device,
        mesh=mesh,
        in_specs=placed,
        out_specs=(P(None, ("genome", "tower"), None), P(None, None, ("genome", "tower"))),
        check_vma=False,
    )
```

```python
import functools

import jax
import jax.numpy as jnp
from jax import lax
from jax.experimental import pallas as pl
from jax.experimental.pallas import tpu as pltpu
from jax.sharding import PartitionSpec as P

BP = 2048
STRIDE = 64
BINS = 256
BLOCKS = BINS // STRIDE
LANES = 128
F32 = jnp.float32
BF16 = jnp.bfloat16
VMEM_BYTES = 40 * 1024 * 1024


def dot(a, b):
    return jnp.dot(a, b, preferred_element_type=F32)


def stem_kernel(bins, bases_hbm, weight_hbm, out_ref, bases, weight, base_sem, weight_sem):
    groups = BP // LANES
    chunks = weight.shape[0]
    span = weight.shape[2]
    base_copy = pltpu.make_async_copy(bases_hbm, bases, base_sem)
    base_copy.start()
    copies = []
    for k in range(chunks):
        copy = pltpu.make_async_copy(
            weight_hbm.at[:, pl.ds(k * span, span)], weight.at[k], weight_sem.at[k]
        )
        copy.start()
        copies.append(copy)
    row = lax.broadcasted_iota(jnp.int32, (LANES, 4 * LANES), 0)
    col = lax.broadcasted_iota(jnp.int32, (LANES, 4 * LANES), 1)
    repeat = (row == col // 4).astype(F32).astype(BF16)
    letter = (lax.broadcasted_iota(jnp.int32, (bins, 4 * LANES), 1) % 4).astype(F32)
    base_copy.wait()
    total = None
    per_chunk = groups // chunks
    for k in range(chunks):
        hot = []
        for q in range(per_chunk):
            rows = bases[pl.ds(k * per_chunk + q, bins, stride=groups), :]
            spread = dot(rows.astype(F32).astype(BF16), repeat)
            hot.append(jnp.where(spread == letter, 1.0, 0.0).astype(BF16))
        hot = jnp.concatenate(hot, axis=1)
        copies[k].wait()
        part = lax.dot_general(
            weight[k], hot, (((1,), (1,)), ((), ())), preferred_element_type=F32
        )
        total = part if total is None else total + part
    total = total.astype(BF16)
    half = out_ref.shape[1]
    packed = jnp.concatenate([total[:half], total[half:]], axis=1)
    for slot in range(out_ref.shape[0]):
        out_ref[slot] = packed


def stem(genome_bases, stem_weight, slots):
    bins = genome_bases.shape[0] // BP
    channels, depth = stem_weight.shape
    chunks = 4
    return pl.pallas_call(
        functools.partial(stem_kernel, bins),
        out_shape=jax.ShapeDtypeStruct((slots, channels // 2, 2 * bins), BF16),
        in_specs=[pl.BlockSpec(memory_space=pltpu.HBM)] * 2,
        out_specs=pl.BlockSpec(memory_space=pltpu.VMEM),
        scratch_shapes=[
            pltpu.VMEM((genome_bases.shape[0] // LANES, LANES), jnp.int32),
            pltpu.VMEM((chunks, channels, depth // chunks), BF16),
            pltpu.SemaphoreType.DMA,
            pltpu.SemaphoreType.DMA((chunks,)),
        ],
        compiler_params=pltpu.CompilerParams(vmem_limit_bytes=63 * 1024 * 1024),
        name="stem",
    )(genome_bases.reshape(-1, LANES), stem_weight)


def banded(kernel, rows):
    taps, out_channels, depth = kernel.shape
    flat = jnp.concatenate([kernel[u] for u in range(taps)], axis=1)
    bands = []
    for r in range(rows):
        parts = [flat]
        if r:
            parts.insert(0, jnp.zeros((out_channels, r * depth), BF16))
        if rows - 1 - r:
            parts.append(jnp.zeros((out_channels, (rows - 1 - r) * depth), BF16))
        bands.append(jnp.concatenate(parts, axis=1) if len(parts) > 1 else flat)
    return jnp.concatenate(bands, axis=0)


def block_diagonal(matrix, count):
    height, width = matrix.shape
    tiled = jnp.concatenate([jnp.concatenate([matrix] * count, axis=1)] * count, axis=0)
    row = lax.broadcasted_iota(jnp.int32, tiled.shape, 0) // height
    col = lax.broadcasted_iota(jnp.int32, tiled.shape, 1) // width
    return jnp.where(row == col, tiled, jnp.zeros((), BF16))


def head_by_row(head, count):
    targets, width = head.shape
    wide = jnp.concatenate([head] * count, axis=1)
    tall = jnp.broadcast_to(wide[:, None, :], (targets, count, count * width))
    row = lax.broadcasted_iota(jnp.int32, tall.shape, 1)
    col = lax.broadcasted_iota(jnp.int32, tall.shape, 2) // width
    return jnp.where(row == col, tall, jnp.zeros((), BF16)).reshape(targets * count, count * width)


def segments(margin, height):
    whole = [BINS - STRIDE * b + margin + 1 for b in range(BLOCKS)]
    near = 2 * STRIDE + height - 1 + 2 * margin
    parts = [(b, b, whole[b]) for b in range(BLOCKS)]
    parts += [(b + 1, b, min(whole[b], near)) for b in range(BLOCKS)]
    sizes = [part[2] for part in parts]
    offsets = [sum(sizes[:k]) for k in range(len(sizes))]
    lanes = -(-sum(sizes) // LANES) * LANES
    return parts, offsets, lanes


def shifted(values, offset):
    if offset == 0:
        return values
    channels, extent = values.shape
    edge = jnp.zeros((channels, abs(offset)), values.dtype)
    if offset >= 0:
        return jnp.concatenate([values[:, offset:], edge], axis=1)
    return jnp.concatenate([edge, values[:, : extent + offset]], axis=1)


def spans_of(rows, groups):
    return sorted({groups, rows % groups} - {0})


def prepare_kernel(
    height,
    groups,
    place_ref,
    _,
    trunk_in,
    rate_in,
    conv_in,
    mix_in,
    head_in,
    stitch_in,
    trunk_ref,
    rate_ref,
    decay_ref,
    inside_ref,
    head_ref,
    stitch_ref,
    *conv_refs,
):
    margin = 2
    parts, offsets, lanes = segments(margin, height)
    tower_row = place_ref[0] * height
    for layer in range(trunk_in.shape[0]):
        flat = trunk_in[layer]
        width = flat.shape[1] // 3
        trunk_ref[layer] = jnp.concatenate(
            [flat[:, q * width : (q + 1) * width] for q in range(3)], axis=0
        )
    at = 0
    for block, rows in enumerate((height + 2, height)):
        for span in spans_of(rows, groups):
            conv_refs[at][...] = banded(conv_in[block], span)
            conv_refs[at + 1][...] = block_diagonal(mix_in[block], span)
            at += 2
    head_ref[...] = head_by_row(head_in[...], height)
    channels = rate_in.shape[1]
    row = lax.broadcasted_iota(jnp.int32, (channels, channels), 0)
    col = lax.broadcasted_iota(jnp.int32, (channels, channels), 1)
    rate = jnp.sum(jnp.where(row == col, rate_in[...], 0.0), axis=1, keepdims=True)
    rate_ref[...] = jnp.broadcast_to(rate, rate_ref.shape)

    lane = lax.broadcasted_iota(jnp.int32, (height + 2 * margin, lanes), 1)
    block_of = jnp.zeros((height + 2 * margin, lanes), jnp.int32)
    start_of = jnp.zeros((height + 2 * margin, lanes), jnp.int32)
    for (_, b, _), offset in zip(parts, offsets):
        block_of = jnp.where(lane >= offset, b, block_of)
        start_of = jnp.where(lane >= offset, offset, start_of)
    step = lane - start_of
    first_row = STRIDE * block_of + tower_row - margin
    column = first_row + step
    in_column = (column < BINS) & (column >= 0)

    row = lax.broadcasted_iota(jnp.int32, (height + 2 * margin, lanes), 0)
    decay_ref[...] = jnp.log1p(jnp.abs(step - row).astype(F32))
    at = first_row + row
    inside_ref[...] = jnp.where(in_column & (at >= 0) & (at < BINS), 1.0, 0.0)

    local = lax.broadcasted_iota(jnp.int32, (height, BINS), 0)
    ahead = lax.broadcasted_iota(jnp.int32, (height, BINS), 1)
    for back in range(2):
        weight_sum = jnp.zeros((height, BINS), F32)
        weights = []
        for b in range(BLOCKS):
            weight = jnp.where(ahead == STRIDE * b + tower_row + local, stitch_in[...], 0)
            weight = jnp.sum(weight.astype(F32), axis=1, keepdims=True)
            weight = jnp.where(place_ref[1] - back >= b, weight, 0.0)
            reach = STRIDE * b + tower_row + local + ahead < BINS
            weight = jnp.where(reach, weight, 0.0)
            weights.append(weight)
            weight_sum = weight_sum + weight
        scale = 1.0 / jnp.maximum(weight_sum, 1.0)
        for b in range(BLOCKS):
            stitch_ref[back * BLOCKS + b] = weights[b] * scale


def main_kernel(
    height,
    groups,
    place_ref,
    features,
    trunk_out,
    pair_weight,
    trunk_in,
    rate_ref,
    decay_ref,
    inside_ref,
    head_ref,
    stitch_ref,
    *rest,
):
    margin = 2
    parts, offsets, lanes = segments(margin, height)
    tower_row = place_ref[0] * height
    channels = rate_ref.shape[0]
    depth = 3 * channels
    rest = list(rest)
    conv_a, conv_b, mix_a, mix_b = {}, {}, {}, {}
    for span in spans_of(height + 2, groups):
        conv_a[span], mix_a[span] = rest.pop(0), rest.pop(0)
    for span in spans_of(height, groups):
        conv_b[span], mix_b[span] = rest.pop(0), rest.pop(0)
    stitched_ref, keep_ref, send_ref, taps_a, taps_b, grid_ref, final_ref = rest

    starts = features.shape[0]
    blocks = []
    for d in range(-BLOCKS, BLOCKS):
        at = place_ref[1] + d
        block = features[jnp.clip(at, 0, starts - 1)]
        blocks.append(jnp.where((at >= 0) & (at < starts), block, jnp.zeros_like(block)))
    blocks = jnp.concatenate(
        [
            jnp.concatenate([half[:, :STRIDE] for half in blocks], axis=1),
            jnp.concatenate([half[:, STRIDE:] for half in blocks], axis=1),
        ],
        axis=0,
    )
    extent = BINS
    windows = []
    for b in range(BLOCKS + 1):
        first = (BLOCKS - b) * STRIDE
        windows.append(blocks[:, first : first + BINS].astype(F32))
    stream = jnp.concatenate(windows, axis=1)
    layers = trunk_in.shape[0]
    for layer in range(layers):
        dilation = max(1, extent // 2 ** (layers - layer))
        active = jnp.maximum(stream, 0.0).astype(BF16)
        mid = trunk_in.shape[1] // 3
        taps = dot(trunk_in[layer], active)
        inner = taps[mid : 2 * mid] + jnp.concatenate(
            [
                shifted(taps[:mid, b * BINS : (b + 1) * BINS], -dilation)
                + shifted(taps[2 * mid :, b * BINS : (b + 1) * BINS], dilation)
                for b in range(BLOCKS + 1)
            ],
            axis=1,
        )
        squeezed = jax.nn.relu(inner).astype(BF16)
        stream = stream + lax.dot_general(
            trunk_out[layer], squeezed, (((0,), (0,)), ((), ())), preferred_element_type=F32
        )
    projected = dot(pair_weight[...], jax.nn.relu(stream).astype(BF16))

    right = []
    left = []
    for window, b, size in parts:
        begin = STRIDE * b + tower_row - margin
        turn = jnp.where(begin > 0, BINS - begin, -begin)
        terms = projected[:, window * BINS : (window + 1) * BINS]
        turned = pltpu.roll(terms, turn, 1)
        left.append(turned[:channels, :LANES])
        own = turned[channels:]
        if size > BINS:
            own = jnp.concatenate([own, own[:, : size - BINS]], axis=1)
        right.append(own[:, :size])
    used = sum(part[2] for part in parts)
    if lanes > used:
        right.append(jnp.zeros((channels, lanes - used), F32))
    right = jnp.concatenate(right, axis=1)
    rate = jnp.concatenate([rate_ref[...]] * (lanes // LANES), axis=1)
    lane = lax.broadcasted_iota(jnp.int32, (1, lanes), 1)

    def place_sides(ref, slot, act):
        ref[pl.ds(slot * depth, channels), :] = pltpu.roll(act, 1, 1)
        ref[pl.ds(slot * depth + 2 * channels, channels), :] = pltpu.roll(act, lanes - 1, 1)

    for row in range(height + 2 * margin):
        tiles = []
        for tile in range(lanes // LANES):
            piece = None
            here = lane[:, tile * LANES : (tile + 1) * LANES]
            for b in range(len(parts)):
                low, high = offsets[b], offsets[b] + parts[b][2]
                if high <= tile * LANES or low >= (tile + 1) * LANES:
                    continue
                spread = jnp.broadcast_to(left[b][:, row : row + 1], (channels, LANES))
                piece = spread if piece is None else jnp.where(here >= low, spread, piece)
            tiles.append(piece)
        mixed = jnp.concatenate(tiles, axis=1) + right - rate * decay_ref[pl.ds(row, 1), :]
        act = (jnp.maximum(mixed, 0.0) * inside_ref[pl.ds(row, 1), :]).astype(BF16)
        taps_a[pl.ds(row * depth + channels, channels), :] = act
        place_sides(taps_a, row, act)

    chunks = [pl.ds(at, min(2 * LANES, lanes - at)) for at in range(0, lanes, 2 * LANES)]

    def update(kernels, mixes, taps, first, span, chunk):
        conv = dot(kernels[span][...], taps[pl.ds(first * depth, (span + 2) * depth), chunk])
        return dot(mixes[span][...], jnp.maximum(conv, 0.0).astype(BF16))

    for first in range(0, height + 2, groups):
        span = min(groups, height + 2 - first)
        for chunk in chunks:
            added = update(conv_a, mix_a, taps_a, first, span, chunk)
            for r in range(span):
                row = first + r
                kept = taps_a[pl.ds((row + 1) * depth + channels, channels), chunk]
                grid = kept.astype(F32) + added[r * channels : (r + 1) * channels]
                if 1 <= row <= height:
                    grid_ref[pl.ds((row - 1) * channels, channels), chunk] = grid
                act = jnp.maximum(grid, 0.0) * inside_ref[pl.ds(row + 1, 1), chunk]
                taps_b[pl.ds(row * depth + channels, channels), chunk] = act.astype(BF16)
        for row in range(first, first + span):
            place_sides(taps_b, row, taps_b[pl.ds(row * depth + channels, channels), :])
    for first in range(0, height, groups):
        span = min(groups, height - first)
        rows = pl.ds(first * channels, span * channels)
        for chunk in chunks:
            added = update(conv_b, mix_b, taps_b, first, span, chunk)
            final_ref[rows, chunk] = jnp.maximum(grid_ref[rows, chunk] + added, 0.0).astype(BF16)
    targets = head_ref.shape[0] // height
    contact = dot(head_ref[...], final_ref[...]).reshape(targets, height, lanes)

    wide = 2 * STRIDE
    stitched, before = [], []
    map_row = lax.broadcasted_iota(jnp.int32, (height, lanes), 0)
    for t in range(targets):
        skewed = contact[t]
        for bit in range((height - 1).bit_length()):
            turned = pltpu.roll(skewed, lanes - (1 << bit), 1)
            skewed = jnp.where((map_row >> bit) & 1 == 1, turned, skewed)
        for back, width, bands in ((0, BINS, stitched), (1, wide, before)):
            band = None
            for b in range(BLOCKS):
                k = back * BLOCKS + b
                first, reach = offsets[k] + margin, min(width, BINS - STRIDE * b)
                piece = skewed[:, first : first + reach]
                if reach < width:
                    piece = jnp.concatenate(
                        [piece, jnp.zeros((height, width - reach), F32)], axis=1
                    )
                piece = piece * stitch_ref[k][:, :width]
                band = piece if band is None else band + piece
            bands.append(band)
        stitched_ref[t] = stitched[t]

    near = jnp.concatenate([band[:, :wide] for band in stitched] + before, axis=0)
    col = lax.broadcasted_iota(jnp.int32, (wide, wide), 0)
    corner = lax.broadcasted_iota(jnp.int32, (wide, wide), 1)
    box = ((col > corner) & (col <= corner + STRIDE) & (corner < STRIDE)).astype(F32)
    square = jnp.dot(near, box, preferred_element_type=F32, precision=lax.Precision.HIGHEST)
    at = lax.broadcasted_iota(jnp.int32, near.shape, 1)
    contact = jnp.where((at >= 1) & (at <= STRIDE), jnp.exp(near), 0.0)
    down = jnp.sum(contact, axis=1, keepdims=True)
    here = lax.broadcasted_iota(jnp.int32, (height, wide), 0)
    there = lax.broadcasted_iota(jnp.int32, (height, wide), 1)

    def by_row(values, back):
        rows = []
        for t in range(back * targets, (back + 1) * targets):
            own = pltpu.roll(
                values[t * height : (t + 1) * height], 0, 1, stride=1, stride_axis=0
            )
            rows.append(jnp.sum(own, axis=0, keepdims=True))
        return rows

    down_rows = []
    for t in range(targets):
        own = jnp.where(here == there, down[t * height : (t + 1) * height], 0.0)
        down_rows.append(jnp.sum(own, axis=0, keepdims=True))
    rows = by_row(square, 0) + by_row(contact, 0)
    rows_before = by_row(square, 1) + by_row(contact, 1)
    keep_ref[...] = jnp.concatenate(rows + down_rows, axis=0)
    per_row = LANES // height
    first = lax.broadcasted_iota(jnp.int32, (per_row, LANES), 1) < height
    def packs_of(rows):
        return [
            jnp.concatenate(
                rows[p : p + per_row]
                + [jnp.zeros((1, LANES), F32)] * (per_row - len(rows[p : p + per_row])),
                axis=0,
            )
            for p in range(0, len(rows), per_row)
        ]

    packs = list(zip(packs_of(rows), packs_of(rows_before)))
    for k in range(1, STRIDE // height + 1):
        same = place_ref[0] + k < STRIDE // height
        packed = []
        for own, previous in packs:
            turned = pltpu.roll(jnp.where(same, own, previous), LANES - k * height, 1)
            turned = pltpu.roll(
                jnp.where(first, turned, 0.0), 0, 1, stride=height, stride_axis=0
            )
            packed.append(jnp.sum(turned, axis=0, keepdims=True))
        send_ref[lax.rem(place_ref[0] + k, STRIDE // height)] = jnp.concatenate(packed, axis=0)


def finish_kernel(height, keep_ref, got_ref, out_ref):
    targets = out_ref.shape[0]
    per_row = LANES // height
    keep = keep_ref[...][:, :height]
    got = jnp.sum(got_ref[...], axis=0)
    rows = []
    for q in range(2 * targets):
        at = (q % per_row) * height
        rows.append(got[q // per_row : q // per_row + 1, at : at + height])
    sums = keep[: 2 * targets] + jnp.concatenate(rows, axis=0)
    upstream = sums[targets:]
    downstream = keep[2 * targets :]
    insulation = sums[:targets] / (STRIDE * STRIDE)
    direction = (downstream - upstream) / (downstream + upstream)
    for t in range(targets):
        out_ref[t] = jnp.concatenate([insulation[t : t + 1], direction[t : t + 1]], axis=0)


def per_device(
    genome_bases,
    stitch_weight,
    stem_weight,
    trunk_in,
    trunk_out,
    pair_weight,
    distance_rate,
    tower_conv,
    tower_mix,
    head_weight,
):
    towers = lax.axis_size("tower")
    height = STRIDE // towers
    tower_index = lax.axis_index("tower")
    genome_index = lax.axis_index("genome")
    own = stem(genome_bases, stem_weight, lax.axis_size("genome"))
    features = lax.all_to_all(own, "genome", 0, 0, tiled=True)
    groups = 3
    channels = distance_rate.shape[0]
    targets = head_weight.shape[0]
    place = jnp.stack([tower_index, genome_index]).astype(jnp.int32)
    lanes = segments(2, height)[2]
    packs = -(-2 * targets * height // LANES)
    vmem = pl.BlockSpec(memory_space=pltpu.VMEM)
    smem = pl.BlockSpec(memory_space=pltpu.SMEM)
    layers, mid, width = trunk_in.shape
    rows = height + 4
    shapes = [
        jax.ShapeDtypeStruct((layers, 3 * mid, width // 3), BF16),
        jax.ShapeDtypeStruct((channels, LANES), F32),
        jax.ShapeDtypeStruct((rows, lanes), F32),
        jax.ShapeDtypeStruct((rows, lanes), F32),
        jax.ShapeDtypeStruct((targets * height, height * channels), BF16),
        jax.ShapeDtypeStruct((2 * BLOCKS, height, BINS), F32),
    ]
    for count in (height + 2, height):
        for span in spans_of(count, groups):
            tall = span * channels
            shapes.append(jax.ShapeDtypeStruct((tall, (span + 2) * 3 * channels), BF16))
            shapes.append(jax.ShapeDtypeStruct((tall, tall), BF16))
    prepared = pl.pallas_call(
        functools.partial(prepare_kernel, height, groups),
        out_shape=shapes,
        in_specs=[smem, pl.BlockSpec(memory_space=pltpu.HBM)] + [vmem] * 6,
        out_specs=[vmem] * len(shapes),
        compiler_params=pltpu.CompilerParams(vmem_limit_bytes=8 * 1024 * 1024),
        cost_estimate=pl.CostEstimate(flops=10**9, bytes_accessed=1 << 22, transcendentals=0),
        name="prepare",
    )(
        place,
        own,
        trunk_in,
        distance_rate.reshape(1, channels),
        tower_conv,
        tower_mix,
        head_weight,
        stitch_weight.reshape(1, BINS),
    )
    stitched, keep, send = pl.pallas_call(
        functools.partial(main_kernel, height, groups),
        out_shape=[
            jax.ShapeDtypeStruct((targets, height, BINS), F32),
            jax.ShapeDtypeStruct((3 * targets, LANES), F32),
            jax.ShapeDtypeStruct((towers, packs, LANES), F32),
        ],
        in_specs=[smem] + [vmem] * (3 + len(shapes)),
        out_specs=[vmem] * 3,
        scratch_shapes=[
            pltpu.VMEM((rows * 3 * channels, lanes), BF16),
            pltpu.VMEM(((height + 2) * 3 * channels, lanes), BF16),
            pltpu.VMEM((height * channels, lanes), F32),
            pltpu.VMEM((height * channels, lanes), BF16),
        ],
        compiler_params=pltpu.CompilerParams(vmem_limit_bytes=VMEM_BYTES),
        name="windows",
    )(place, features, jnp.transpose(trunk_out, (0, 2, 1)), pair_weight, *prepared)
    got = lax.all_to_all(send, "tower", 0, 0, tiled=True)
    scores = pl.pallas_call(
        functools.partial(finish_kernel, height),
        out_shape=jax.ShapeDtypeStruct((targets, 2, height), F32),
        in_specs=[vmem, vmem],
        out_specs=vmem,
        compiler_params=pltpu.CompilerParams(vmem_limit_bytes=2 * 1024 * 1024),
        name="finish",
    )(keep, got)
    return (stitched, jnp.transpose(scores, (1, 0, 2)))


def solution(mesh):
    placed = (P("genome"), P(), P(), P(), P(), P(), P(), P(), P(), P())
    return jax.shard_map(
        per_device,
        mesh=mesh,
        in_specs=placed,
        out_specs=(P(None, ("genome", "tower"), None), P(None, None, ("genome", "tower"))),
        check_vma=False,
    )
```

```python
import functools

import jax
import jax.numpy as jnp
from jax import lax
from jax.experimental import pallas as pl
from jax.experimental.pallas import tpu as pltpu
from jax.sharding import PartitionSpec as P

BP = 2048
STRIDE = 64
BINS = 256
BLOCKS = BINS // STRIDE
LANES = 128
F32 = jnp.float32
BF16 = jnp.bfloat16
VMEM_BYTES = 40 * 1024 * 1024


def dot(a, b):
    return jnp.dot(a, b, preferred_element_type=F32)


def stem_kernel(bins, bases_hbm, weight_hbm, out_ref, bases, weight, base_sem, weight_sem):
    groups = BP // LANES
    chunks = weight.shape[0]
    span = weight.shape[2]
    base_copy = pltpu.make_async_copy(bases_hbm, bases, base_sem)
    base_copy.start()
    copies = []
    for k in range(chunks):
        copy = pltpu.make_async_copy(
            weight_hbm.at[:, pl.ds(k * span, span)], weight.at[k], weight_sem.at[k]
        )
        copy.start()
        copies.append(copy)
    row = lax.broadcasted_iota(jnp.int32, (LANES, 4 * LANES), 0)
    col = lax.broadcasted_iota(jnp.int32, (LANES, 4 * LANES), 1)
    repeat = (row == col // 4).astype(F32).astype(BF16)
    letter = (lax.broadcasted_iota(jnp.int32, (bins, 4 * LANES), 1) % 4).astype(F32)
    base_copy.wait()
    total = None
    per_chunk = groups // chunks
    for k in range(chunks):
        hot = []
        for q in range(per_chunk):
            rows = bases[pl.ds(k * per_chunk + q, bins, stride=groups), :]
            spread = dot(rows.astype(F32).astype(BF16), repeat)
            hot.append(jnp.where(spread == letter, 1.0, 0.0).astype(BF16))
        hot = jnp.concatenate(hot, axis=1)
        copies[k].wait()
        part = lax.dot_general(
            weight[k], hot, (((1,), (1,)), ((), ())), preferred_element_type=F32
        )
        total = part if total is None else total + part
    total = total.astype(BF16)
    half = out_ref.shape[1]
    packed = jnp.concatenate([total[:half], total[half:]], axis=1)
    for slot in range(out_ref.shape[0]):
        out_ref[slot] = packed


def stem(genome_bases, stem_weight, slots):
    bins = genome_bases.shape[0] // BP
    channels, depth = stem_weight.shape
    chunks = 4
    return pl.pallas_call(
        functools.partial(stem_kernel, bins),
        out_shape=jax.ShapeDtypeStruct((slots, channels // 2, 2 * bins), BF16),
        in_specs=[pl.BlockSpec(memory_space=pltpu.HBM)] * 2,
        out_specs=pl.BlockSpec(memory_space=pltpu.VMEM),
        scratch_shapes=[
            pltpu.VMEM((genome_bases.shape[0] // LANES, LANES), jnp.int32),
            pltpu.VMEM((chunks, channels, depth // chunks), BF16),
            pltpu.SemaphoreType.DMA,
            pltpu.SemaphoreType.DMA((chunks,)),
        ],
        compiler_params=pltpu.CompilerParams(vmem_limit_bytes=63 * 1024 * 1024),
        name="stem",
    )(genome_bases.reshape(-1, LANES), stem_weight)


def banded(kernel, rows):
    taps, out_channels, depth = kernel.shape
    flat = jnp.concatenate([kernel[u] for u in range(taps)], axis=1)
    bands = []
    for r in range(rows):
        parts = [flat]
        if r:
            parts.insert(0, jnp.zeros((out_channels, r * depth), BF16))
        if rows - 1 - r:
            parts.append(jnp.zeros((out_channels, (rows - 1 - r) * depth), BF16))
        bands.append(jnp.concatenate(parts, axis=1) if len(parts) > 1 else flat)
    return jnp.concatenate(bands, axis=0)


def block_diagonal(matrix, count):
    height, width = matrix.shape
    tiled = jnp.concatenate([jnp.concatenate([matrix] * count, axis=1)] * count, axis=0)
    row = lax.broadcasted_iota(jnp.int32, tiled.shape, 0) // height
    col = lax.broadcasted_iota(jnp.int32, tiled.shape, 1) // width
    return jnp.where(row == col, tiled, jnp.zeros((), BF16))


def head_by_row(head, count):
    targets, width = head.shape
    wide = jnp.concatenate([head] * count, axis=1)
    tall = jnp.broadcast_to(wide[:, None, :], (targets, count, count * width))
    row = lax.broadcasted_iota(jnp.int32, tall.shape, 1)
    col = lax.broadcasted_iota(jnp.int32, tall.shape, 2) // width
    return jnp.where(row == col, tall, jnp.zeros((), BF16)).reshape(targets * count, count * width)


def segments(margin, height):
    whole = [BINS - STRIDE * b + margin + 1 for b in range(BLOCKS)]
    near = 2 * STRIDE + height - 1 + 2 * margin
    parts = [(b, b, whole[b]) for b in range(BLOCKS)]
    parts += [(b + 1, b, min(whole[b], near)) for b in range(BLOCKS)]
    sizes = [part[2] for part in parts]
    offsets = [sum(sizes[:k]) for k in range(len(sizes))]
    lanes = -(-sum(sizes) // LANES) * LANES
    return parts, offsets, lanes


def shifted(values, offset):
    if offset == 0:
        return values
    channels, extent = values.shape
    edge = jnp.zeros((channels, abs(offset)), values.dtype)
    if offset >= 0:
        return jnp.concatenate([values[:, offset:], edge], axis=1)
    return jnp.concatenate([edge, values[:, : extent + offset]], axis=1)


def spans_of(rows, groups):
    return sorted({groups, rows % groups} - {0})


def prepare_kernel(
    height,
    groups,
    place_ref,
    _,
    trunk_in,
    rate_in,
    conv_in,
    mix_in,
    head_in,
    stitch_in,
    trunk_ref,
    rate_ref,
    decay_ref,
    inside_ref,
    head_ref,
    stitch_ref,
    *conv_refs,
):
    margin = 2
    parts, offsets, lanes = segments(margin, height)
    tower_row = place_ref[0] * height
    for layer in range(trunk_in.shape[0]):
        flat = trunk_in[layer]
        width = flat.shape[1] // 3
        trunk_ref[layer] = jnp.concatenate(
            [flat[:, q * width : (q + 1) * width] for q in range(3)], axis=0
        )
    at = 0
    for block, rows in enumerate((height + 2, height)):
        for span in spans_of(rows, groups):
            conv_refs[at][...] = banded(conv_in[block], span)
            conv_refs[at + 1][...] = block_diagonal(mix_in[block], span)
            at += 2
    head_ref[...] = head_by_row(head_in[...], height)
    channels = rate_in.shape[1]
    row = lax.broadcasted_iota(jnp.int32, (channels, channels), 0)
    col = lax.broadcasted_iota(jnp.int32, (channels, channels), 1)
    rate = jnp.sum(jnp.where(row == col, rate_in[...], 0.0), axis=1, keepdims=True)
    rate_ref[...] = jnp.broadcast_to(rate, rate_ref.shape)

    lane = lax.broadcasted_iota(jnp.int32, (height + 2 * margin, lanes), 1)
    block_of = jnp.zeros((height + 2 * margin, lanes), jnp.int32)
    start_of = jnp.zeros((height + 2 * margin, lanes), jnp.int32)
    for (_, b, _), offset in zip(parts, offsets):
        block_of = jnp.where(lane >= offset, b, block_of)
        start_of = jnp.where(lane >= offset, offset, start_of)
    step = lane - start_of
    first_row = STRIDE * block_of + tower_row - margin
    column = first_row + step
    in_column = (column < BINS) & (column >= 0)

    row = lax.broadcasted_iota(jnp.int32, (height + 2 * margin, lanes), 0)
    decay_ref[...] = jnp.log1p(jnp.abs(step - row).astype(F32))
    at = first_row + row
    inside_ref[...] = jnp.where(in_column & (at >= 0) & (at < BINS), 1.0, 0.0)

    local = lax.broadcasted_iota(jnp.int32, (height, BINS), 0)
    ahead = lax.broadcasted_iota(jnp.int32, (height, BINS), 1)
    for back in range(2):
        weight_sum = jnp.zeros((height, BINS), F32)
        weights = []
        for b in range(BLOCKS):
            weight = jnp.where(ahead == STRIDE * b + tower_row + local, stitch_in[...], 0)
            weight = jnp.sum(weight.astype(F32), axis=1, keepdims=True)
            weight = jnp.where(place_ref[1] - back >= b, weight, 0.0)
            reach = STRIDE * b + tower_row + local + ahead < BINS
            weight = jnp.where(reach, weight, 0.0)
            weights.append(weight)
            weight_sum = weight_sum + weight
        scale = 1.0 / jnp.maximum(weight_sum, 1.0)
        for b in range(BLOCKS):
            stitch_ref[back * BLOCKS + b] = weights[b] * scale


def main_kernel(
    height,
    groups,
    place_ref,
    features,
    trunk_out,
    pair_weight,
    trunk_in,
    rate_ref,
    decay_ref,
    inside_ref,
    head_ref,
    stitch_ref,
    *rest,
):
    margin = 2
    parts, offsets, lanes = segments(margin, height)
    tower_row = place_ref[0] * height
    channels = rate_ref.shape[0]
    depth = 3 * channels
    rest = list(rest)
    conv_a, conv_b, mix_a, mix_b = {}, {}, {}, {}
    for span in spans_of(height + 2, groups):
        conv_a[span], mix_a[span] = rest.pop(0), rest.pop(0)
    for span in spans_of(height, groups):
        conv_b[span], mix_b[span] = rest.pop(0), rest.pop(0)
    stitched_ref, keep_ref, send_ref, taps_a, taps_b, grid_ref, final_ref, squeezed_ref = rest

    starts = features.shape[0]
    blocks = []
    for d in range(-BLOCKS, BLOCKS):
        at = place_ref[1] + d
        block = features[jnp.clip(at, 0, starts - 1)]
        blocks.append(jnp.where((at >= 0) & (at < starts), block, jnp.zeros_like(block)))
    blocks = jnp.concatenate(
        [
            jnp.concatenate([half[:, :STRIDE] for half in blocks], axis=1),
            jnp.concatenate([half[:, STRIDE:] for half in blocks], axis=1),
        ],
        axis=0,
    )
    extent = BINS
    windows = []
    for b in range(BLOCKS + 1):
        first = (BLOCKS - b) * STRIDE
        windows.append(blocks[:, first : first + BINS].astype(F32))
    stream = jnp.concatenate(windows, axis=1)
    layers = trunk_in.shape[0]
    for layer in range(layers):
        dilation = max(1, extent // 2 ** (layers - layer))
        active = jnp.maximum(stream, 0.0).astype(BF16)
        mid = trunk_in.shape[1] // 3
        taps = dot(trunk_in[layer], active)
        inner = taps[mid : 2 * mid] + jnp.concatenate(
            [
                shifted(taps[:mid, b * BINS : (b + 1) * BINS], -dilation)
                + shifted(taps[2 * mid :, b * BINS : (b + 1) * BINS], dilation)
                for b in range(BLOCKS + 1)
            ],
            axis=1,
        )
        squeezed = jax.nn.relu(inner).astype(BF16)
        stream = stream + lax.dot_general(
            trunk_out[layer], squeezed, (((0,), (0,)), ((), ())), preferred_element_type=F32
        )
    projected = dot(pair_weight[...], jax.nn.relu(stream).astype(BF16))

    right = []
    left = []
    for window, b, size in parts:
        begin = STRIDE * b + tower_row - margin
        turn = jnp.where(begin > 0, BINS - begin, -begin)
        terms = projected[:, window * BINS : (window + 1) * BINS]
        turned = pltpu.roll(terms, turn, 1)
        left.append(turned[:channels, :LANES])
        own = turned[channels:]
        if size > BINS:
            own = jnp.concatenate([own, own[:, : size - BINS]], axis=1)
        right.append(own[:, :size])
    used = sum(part[2] for part in parts)
    if lanes > used:
        right.append(jnp.zeros((channels, lanes - used), F32))
    right = jnp.concatenate(right, axis=1)
    rate = jnp.concatenate([rate_ref[...]] * (lanes // LANES), axis=1)
    lane = lax.broadcasted_iota(jnp.int32, (1, lanes), 1)

    def place_taps(ref, slot, act):
        act = act.astype(BF16)
        ref[pl.ds(slot * depth, channels), :] = pltpu.roll(act, 1, 1)
        ref[pl.ds(slot * depth + channels, channels), :] = act
        ref[pl.ds(slot * depth + 2 * channels, channels), :] = pltpu.roll(act, lanes - 1, 1)

    for row in range(height + 2 * margin):
        tiles = []
        for tile in range(lanes // LANES):
            piece = None
            here = lane[:, tile * LANES : (tile + 1) * LANES]
            for b in range(len(parts)):
                low, high = offsets[b], offsets[b] + parts[b][2]
                if high <= tile * LANES or low >= (tile + 1) * LANES:
                    continue
                spread = jnp.broadcast_to(left[b][:, row : row + 1], (channels, LANES))
                piece = spread if piece is None else jnp.where(here >= low, spread, piece)
            tiles.append(piece)
        mixed = jnp.concatenate(tiles, axis=1) + right - rate * decay_ref[pl.ds(row, 1), :]
        place_taps(taps_a, row, jnp.maximum(mixed, 0.0) * inside_ref[pl.ds(row, 1), :])

    def tower_block(kernels, mixes, taps, rows):
        for group, first in enumerate(range(0, rows, groups)):
            span = min(groups, rows - first)
            conv = dot(kernels[span][...], taps[pl.ds(first * depth, (span + 2) * depth), :])
            squeezed_ref[pl.ds(0, span * channels), pl.ds(group * lanes, lanes)] = jnp.maximum(
                conv, 0.0
            ).astype(BF16)
        full, left_over = rows // groups, rows % groups
        wide = dot(mixes[groups][...], squeezed_ref[:, pl.ds(0, full * lanes)])
        added = [
            wide[(row % groups) * channels :][:channels, (row // groups) * lanes :][:, :lanes]
            for row in range(full * groups)
        ]
        if left_over:
            rest = squeezed_ref[pl.ds(0, left_over * channels), pl.ds(full * lanes, lanes)]
            last = dot(mixes[left_over][...], rest)
            added += [last[r * channels : (r + 1) * channels] for r in range(left_over)]
        return added

    for row, added in enumerate(tower_block(conv_a, mix_a, taps_a, height + 2)):
        kept = taps_a[pl.ds((row + 1) * depth + channels, channels), :].astype(F32)
        grid = kept + added
        if 1 <= row <= height:
            grid_ref[pl.ds((row - 1) * channels, channels), :] = grid
        place_taps(taps_b, row, jnp.maximum(grid, 0.0) * inside_ref[pl.ds(row + 1, 1), :])
    for row, added in enumerate(tower_block(conv_b, mix_b, taps_b, height)):
        rows = pl.ds(row * channels, channels)
        final_ref[rows, :] = jnp.maximum(grid_ref[rows, :] + added, 0.0).astype(BF16)
    targets = head_ref.shape[0] // height
    contact = dot(head_ref[...], final_ref[...]).reshape(targets, height, lanes)

    wide = 2 * STRIDE
    stitched, before = [], []
    map_row = lax.broadcasted_iota(jnp.int32, (height, lanes), 0)
    for t in range(targets):
        skewed = contact[t]
        for bit in range((height - 1).bit_length()):
            turned = pltpu.roll(skewed, lanes - (1 << bit), 1)
            skewed = jnp.where((map_row >> bit) & 1 == 1, turned, skewed)
        for back, width, bands in ((0, BINS, stitched), (1, wide, before)):
            band = None
            for b in range(BLOCKS):
                k = back * BLOCKS + b
                first, reach = offsets[k] + margin, min(width, BINS - STRIDE * b)
                piece = skewed[:, first : first + reach]
                if reach < width:
                    piece = jnp.concatenate(
                        [piece, jnp.zeros((height, width - reach), F32)], axis=1
                    )
                piece = piece * stitch_ref[k][:, :width]
                band = piece if band is None else band + piece
            bands.append(band)
        stitched_ref[t] = stitched[t]

    near = jnp.concatenate([band[:, :wide] for band in stitched] + before, axis=0)
    col = lax.broadcasted_iota(jnp.int32, (wide, wide), 0)
    corner = lax.broadcasted_iota(jnp.int32, (wide, wide), 1)
    box = ((col > corner) & (col <= corner + STRIDE) & (corner < STRIDE)).astype(F32)
    square = jnp.dot(near, box, preferred_element_type=F32, precision=lax.Precision.HIGHEST)
    at = lax.broadcasted_iota(jnp.int32, near.shape, 1)
    contact = jnp.where((at >= 1) & (at <= STRIDE), jnp.exp(near), 0.0)
    down = jnp.sum(contact, axis=1, keepdims=True)
    here = lax.broadcasted_iota(jnp.int32, (height, wide), 0)
    there = lax.broadcasted_iota(jnp.int32, (height, wide), 1)

    def by_row(values, back):
        rows = []
        for t in range(back * targets, (back + 1) * targets):
            own = pltpu.roll(
                values[t * height : (t + 1) * height], 0, 1, stride=1, stride_axis=0
            )
            rows.append(jnp.sum(own, axis=0, keepdims=True))
        return rows

    down_rows = []
    for t in range(targets):
        own = jnp.where(here == there, down[t * height : (t + 1) * height], 0.0)
        down_rows.append(jnp.sum(own, axis=0, keepdims=True))
    rows = by_row(square, 0) + by_row(contact, 0)
    rows_before = by_row(square, 1) + by_row(contact, 1)
    keep_ref[...] = jnp.concatenate(rows + down_rows, axis=0)
    per_row = LANES // height
    first = lax.broadcasted_iota(jnp.int32, (per_row, LANES), 1) < height
    def packs_of(rows):
        return [
            jnp.concatenate(
                rows[p : p + per_row]
                + [jnp.zeros((1, LANES), F32)] * (per_row - len(rows[p : p + per_row])),
                axis=0,
            )
            for p in range(0, len(rows), per_row)
        ]

    packs = list(zip(packs_of(rows), packs_of(rows_before)))
    for k in range(1, STRIDE // height + 1):
        same = place_ref[0] + k < STRIDE // height
        packed = []
        for own, previous in packs:
            turned = pltpu.roll(jnp.where(same, own, previous), LANES - k * height, 1)
            turned = pltpu.roll(
                jnp.where(first, turned, 0.0), 0, 1, stride=height, stride_axis=0
            )
            packed.append(jnp.sum(turned, axis=0, keepdims=True))
        send_ref[lax.rem(place_ref[0] + k, STRIDE // height)] = jnp.concatenate(packed, axis=0)


def finish_kernel(height, keep_ref, got_ref, out_ref):
    targets = out_ref.shape[0]
    per_row = LANES // height
    keep = keep_ref[...][:, :height]
    got = jnp.sum(got_ref[...], axis=0)
    rows = []
    for q in range(2 * targets):
        at = (q % per_row) * height
        rows.append(got[q // per_row : q // per_row + 1, at : at + height])
    sums = keep[: 2 * targets] + jnp.concatenate(rows, axis=0)
    upstream = sums[targets:]
    downstream = keep[2 * targets :]
    insulation = sums[:targets] / (STRIDE * STRIDE)
    direction = (downstream - upstream) / (downstream + upstream)
    for t in range(targets):
        out_ref[t] = jnp.concatenate([insulation[t : t + 1], direction[t : t + 1]], axis=0)


def per_device(
    genome_bases,
    stitch_weight,
    stem_weight,
    trunk_in,
    trunk_out,
    pair_weight,
    distance_rate,
    tower_conv,
    tower_mix,
    head_weight,
):
    towers = lax.axis_size("tower")
    height = STRIDE // towers
    tower_index = lax.axis_index("tower")
    genome_index = lax.axis_index("genome")
    own = stem(genome_bases, stem_weight, lax.axis_size("genome"))
    features = lax.all_to_all(own, "genome", 0, 0, tiled=True)
    groups = 3
    channels = distance_rate.shape[0]
    targets = head_weight.shape[0]
    place = jnp.stack([tower_index, genome_index]).astype(jnp.int32)
    lanes = segments(2, height)[2]
    packs = -(-2 * targets * height // LANES)
    vmem = pl.BlockSpec(memory_space=pltpu.VMEM)
    smem = pl.BlockSpec(memory_space=pltpu.SMEM)
    layers, mid, width = trunk_in.shape
    rows = height + 4
    shapes = [
        jax.ShapeDtypeStruct((layers, 3 * mid, width // 3), BF16),
        jax.ShapeDtypeStruct((channels, LANES), F32),
        jax.ShapeDtypeStruct((rows, lanes), F32),
        jax.ShapeDtypeStruct((rows, lanes), F32),
        jax.ShapeDtypeStruct((targets * height, height * channels), BF16),
        jax.ShapeDtypeStruct((2 * BLOCKS, height, BINS), F32),
    ]
    for count in (height + 2, height):
        for span in spans_of(count, groups):
            tall = span * channels
            shapes.append(jax.ShapeDtypeStruct((tall, (span + 2) * 3 * channels), BF16))
            shapes.append(jax.ShapeDtypeStruct((tall, tall), BF16))
    prepared = pl.pallas_call(
        functools.partial(prepare_kernel, height, groups),
        out_shape=shapes,
        in_specs=[smem, pl.BlockSpec(memory_space=pltpu.HBM)] + [vmem] * 6,
        out_specs=[vmem] * len(shapes),
        compiler_params=pltpu.CompilerParams(vmem_limit_bytes=8 * 1024 * 1024),
        cost_estimate=pl.CostEstimate(flops=10**9, bytes_accessed=1 << 22, transcendentals=0),
        name="prepare",
    )(
        place,
        own,
        trunk_in,
        distance_rate.reshape(1, channels),
        tower_conv,
        tower_mix,
        head_weight,
        stitch_weight.reshape(1, BINS),
    )
    stitched, keep, send = pl.pallas_call(
        functools.partial(main_kernel, height, groups),
        out_shape=[
            jax.ShapeDtypeStruct((targets, height, BINS), F32),
            jax.ShapeDtypeStruct((3 * targets, LANES), F32),
            jax.ShapeDtypeStruct((towers, packs, LANES), F32),
        ],
        in_specs=[smem] + [vmem] * (3 + len(shapes)),
        out_specs=[vmem] * 3,
        scratch_shapes=[
            pltpu.VMEM((rows * 3 * channels, lanes), BF16),
            pltpu.VMEM(((height + 2) * 3 * channels, lanes), BF16),
            pltpu.VMEM((height * channels, lanes), F32),
            pltpu.VMEM((height * channels, lanes), BF16),
            pltpu.VMEM((groups * channels, -(-(height + 2) // groups) * lanes), BF16),
        ],
        compiler_params=pltpu.CompilerParams(vmem_limit_bytes=VMEM_BYTES),
        name="windows",
    )(place, features, jnp.transpose(trunk_out, (0, 2, 1)), pair_weight, *prepared)
    got = lax.all_to_all(send, "tower", 0, 0, tiled=True)
    scores = pl.pallas_call(
        functools.partial(finish_kernel, height),
        out_shape=jax.ShapeDtypeStruct((targets, 2, height), F32),
        in_specs=[vmem, vmem],
        out_specs=vmem,
        compiler_params=pltpu.CompilerParams(vmem_limit_bytes=2 * 1024 * 1024),
        name="finish",
    )(keep, got)
    return (stitched, jnp.transpose(scores, (1, 0, 2)))


def solution(mesh):
    placed = (P("genome"), P(), P(), P(), P(), P(), P(), P(), P(), P())
    return jax.shard_map(
        per_device,
        mesh=mesh,
        in_specs=placed,
        out_specs=(P(None, ("genome", "tower"), None), P(None, None, ("genome", "tower"))),
        check_vma=False,
    )
```

```python
import functools

import jax
import jax.numpy as jnp
from jax import lax
from jax.experimental import pallas as pl
from jax.experimental.pallas import tpu as pltpu
from jax.sharding import PartitionSpec as P

BP = 2048
STRIDE = 64
BINS = 256
BLOCKS = BINS // STRIDE
LANES = 128
F32 = jnp.float32
BF16 = jnp.bfloat16
VMEM_BYTES = 40 * 1024 * 1024


def dot(a, b):
    return jnp.dot(a, b, preferred_element_type=F32)


def stem_kernel(bins, bases_hbm, weight_hbm, out_ref, bases, weight, base_sem, weight_sem):
    groups = BP // LANES
    chunks = weight.shape[0]
    span = weight.shape[2]
    base_copy = pltpu.make_async_copy(bases_hbm, bases, base_sem)
    base_copy.start()
    copies = []
    for k in range(chunks):
        copy = pltpu.make_async_copy(
            weight_hbm.at[:, pl.ds(k * span, span)], weight.at[k], weight_sem.at[k]
        )
        copy.start()
        copies.append(copy)
    row = lax.broadcasted_iota(jnp.int32, (LANES, 4 * LANES), 0)
    col = lax.broadcasted_iota(jnp.int32, (LANES, 4 * LANES), 1)
    repeat = (row == col // 4).astype(F32).astype(BF16)
    letter = (lax.broadcasted_iota(jnp.int32, (1, 4 * LANES), 1) % 4).astype(F32)
    base_copy.wait()
    total = None
    per_chunk = groups // chunks
    for k in range(chunks):
        rows = jnp.concatenate(
            [
                bases[pl.ds(k * per_chunk + q, bins, stride=groups), :]
                for q in range(per_chunk)
            ],
            axis=0,
        )
        spread = dot(rows.astype(F32).astype(BF16), repeat)
        hot = jnp.where(spread == letter, 1.0, 0.0).astype(BF16)
        hot = jnp.concatenate(
            [hot[q * bins : (q + 1) * bins] for q in range(per_chunk)], axis=1
        )
        copies[k].wait()
        part = lax.dot_general(
            weight[k], hot, (((1,), (1,)), ((), ())), preferred_element_type=F32
        )
        total = part if total is None else total + part
    total = total.astype(BF16)
    half = out_ref.shape[1]
    packed = jnp.concatenate([total[:half], total[half:]], axis=1)
    for slot in range(out_ref.shape[0]):
        out_ref[slot] = packed


def stem(genome_bases, stem_weight, slots):
    bins = genome_bases.shape[0] // BP
    channels, depth = stem_weight.shape
    chunks = 2
    return pl.pallas_call(
        functools.partial(stem_kernel, bins),
        out_shape=jax.ShapeDtypeStruct((slots, channels // 2, 2 * bins), BF16),
        in_specs=[pl.BlockSpec(memory_space=pltpu.HBM)] * 2,
        out_specs=pl.BlockSpec(memory_space=pltpu.VMEM),
        scratch_shapes=[
            pltpu.VMEM((genome_bases.shape[0] // LANES, LANES), jnp.int32),
            pltpu.VMEM((chunks, channels, depth // chunks), BF16),
            pltpu.SemaphoreType.DMA,
            pltpu.SemaphoreType.DMA((chunks,)),
        ],
        compiler_params=pltpu.CompilerParams(vmem_limit_bytes=63 * 1024 * 1024),
        name="stem",
    )(genome_bases.reshape(-1, LANES), stem_weight)


def banded(kernel, rows):
    taps, out_channels, depth = kernel.shape
    flat = jnp.concatenate([kernel[u] for u in range(taps)], axis=1)
    bands = []
    for r in range(rows):
        parts = [flat]
        if r:
            parts.insert(0, jnp.zeros((out_channels, r * depth), BF16))
        if rows - 1 - r:
            parts.append(jnp.zeros((out_channels, (rows - 1 - r) * depth), BF16))
        bands.append(jnp.concatenate(parts, axis=1) if len(parts) > 1 else flat)
    return jnp.concatenate(bands, axis=0)


def block_diagonal(matrix, count):
    height, width = matrix.shape
    tiled = jnp.concatenate([jnp.concatenate([matrix] * count, axis=1)] * count, axis=0)
    row = lax.broadcasted_iota(jnp.int32, tiled.shape, 0) // height
    col = lax.broadcasted_iota(jnp.int32, tiled.shape, 1) // width
    return jnp.where(row == col, tiled, jnp.zeros((), BF16))


def head_by_row(head, count):
    targets, width = head.shape
    wide = jnp.concatenate([head] * count, axis=1)
    tall = jnp.broadcast_to(wide[:, None, :], (targets, count, count * width))
    row = lax.broadcasted_iota(jnp.int32, tall.shape, 1)
    col = lax.broadcasted_iota(jnp.int32, tall.shape, 2) // width
    return jnp.where(row == col, tall, jnp.zeros((), BF16)).reshape(targets * count, count * width)


def segments(margin, height):
    whole = [BINS - STRIDE * b + margin + 1 for b in range(BLOCKS)]
    near = 2 * STRIDE + height - 1 + 2 * margin
    parts = [(b, b, whole[b]) for b in range(BLOCKS)]
    parts += [(b + 1, b, min(whole[b], near)) for b in range(BLOCKS)]
    sizes = [part[2] for part in parts]
    offsets = [sum(sizes[:k]) for k in range(len(sizes))]
    lanes = -(-sum(sizes) // LANES) * LANES
    return parts, offsets, lanes


def shifted(values, offset):
    if offset == 0:
        return values
    channels, extent = values.shape
    edge = jnp.zeros((channels, abs(offset)), values.dtype)
    if offset >= 0:
        return jnp.concatenate([values[:, offset:], edge], axis=1)
    return jnp.concatenate([edge, values[:, : extent + offset]], axis=1)


def spans_of(rows, groups):
    return sorted({groups, rows % groups} - {0})


def prepare_kernel(
    height,
    groups,
    place_ref,
    _,
    trunk_in,
    rate_in,
    conv_in,
    mix_in,
    head_in,
    stitch_in,
    trunk_ref,
    rate_ref,
    decay_ref,
    inside_ref,
    head_ref,
    stitch_ref,
    *conv_refs,
):
    margin = 2
    parts, offsets, lanes = segments(margin, height)
    tower_row = place_ref[0] * height
    for layer in range(trunk_in.shape[0]):
        flat = trunk_in[layer]
        width = flat.shape[1] // 3
        trunk_ref[layer] = jnp.concatenate(
            [flat[:, q * width : (q + 1) * width] for q in range(3)], axis=0
        )
    at = 0
    for block, rows in enumerate((height + 2, height)):
        for span in spans_of(rows, groups):
            conv_refs[at][...] = banded(conv_in[block], span)
            conv_refs[at + 1][...] = block_diagonal(mix_in[block], span)
            at += 2
    head_ref[...] = head_by_row(head_in[...], height)
    channels = rate_in.shape[1]
    row = lax.broadcasted_iota(jnp.int32, (channels, channels), 0)
    col = lax.broadcasted_iota(jnp.int32, (channels, channels), 1)
    rate = jnp.sum(jnp.where(row == col, rate_in[...], 0.0), axis=1, keepdims=True)
    rate_ref[...] = jnp.broadcast_to(rate, rate_ref.shape)

    lane = lax.broadcasted_iota(jnp.int32, (height + 2 * margin, lanes), 1)
    block_of = jnp.zeros((height + 2 * margin, lanes), jnp.int32)
    start_of = jnp.zeros((height + 2 * margin, lanes), jnp.int32)
    for (_, b, _), offset in zip(parts, offsets):
        block_of = jnp.where(lane >= offset, b, block_of)
        start_of = jnp.where(lane >= offset, offset, start_of)
    step = lane - start_of
    first_row = STRIDE * block_of + tower_row - margin
    column = first_row + step
    in_column = (column < BINS) & (column >= 0)

    row = lax.broadcasted_iota(jnp.int32, (height + 2 * margin, lanes), 0)
    decay_ref[...] = jnp.log1p(jnp.abs(step - row).astype(F32))
    at = first_row + row
    inside_ref[...] = jnp.where(in_column & (at >= 0) & (at < BINS), 1.0, 0.0)

    local = lax.broadcasted_iota(jnp.int32, (height, BINS), 0)
    ahead = lax.broadcasted_iota(jnp.int32, (height, BINS), 1)
    for back in range(2):
        weight_sum = jnp.zeros((height, BINS), F32)
        weights = []
        for b in range(BLOCKS):
            weight = jnp.where(ahead == STRIDE * b + tower_row + local, stitch_in[...], 0)
            weight = jnp.sum(weight.astype(F32), axis=1, keepdims=True)
            weight = jnp.where(place_ref[1] - back >= b, weight, 0.0)
            reach = STRIDE * b + tower_row + local + ahead < BINS
            weight = jnp.where(reach, weight, 0.0)
            weights.append(weight)
            weight_sum = weight_sum + weight
        scale = 1.0 / jnp.maximum(weight_sum, 1.0)
        for b in range(BLOCKS):
            stitch_ref[back * BLOCKS + b] = weights[b] * scale


def main_kernel(
    height,
    groups,
    place_ref,
    features,
    trunk_out,
    pair_weight,
    trunk_in,
    rate_ref,
    decay_ref,
    inside_ref,
    head_ref,
    stitch_ref,
    *rest,
):
    margin = 2
    parts, offsets, lanes = segments(margin, height)
    tower_row = place_ref[0] * height
    channels = rate_ref.shape[0]
    depth = 3 * channels
    rest = list(rest)
    conv_a, conv_b, mix_a, mix_b = {}, {}, {}, {}
    for span in spans_of(height + 2, groups):
        conv_a[span], mix_a[span] = rest.pop(0), rest.pop(0)
    for span in spans_of(height, groups):
        conv_b[span], mix_b[span] = rest.pop(0), rest.pop(0)
    stitched_ref, keep_ref, send_ref, taps_a, taps_b, grid_ref, final_ref, squeezed_ref = rest

    starts = features.shape[0]
    blocks = []
    for d in range(-BLOCKS, BLOCKS):
        at = place_ref[1] + d
        block = features[jnp.clip(at, 0, starts - 1)]
        blocks.append(jnp.where((at >= 0) & (at < starts), block, jnp.zeros_like(block)))
    blocks = jnp.concatenate(
        [
            jnp.concatenate([half[:, :STRIDE] for half in blocks], axis=1),
            jnp.concatenate([half[:, STRIDE:] for half in blocks], axis=1),
        ],
        axis=0,
    )
    extent = BINS
    windows = []
    for b in range(BLOCKS + 1):
        first = (BLOCKS - b) * STRIDE
        windows.append(blocks[:, first : first + BINS].astype(F32))
    stream = jnp.concatenate(windows, axis=1)
    layers = trunk_in.shape[0]
    for layer in range(layers):
        dilation = max(1, extent // 2 ** (layers - layer))
        active = jnp.maximum(stream, 0.0).astype(BF16)
        mid = trunk_in.shape[1] // 3
        taps = dot(trunk_in[layer], active)
        inner = taps[mid : 2 * mid] + jnp.concatenate(
            [
                shifted(taps[:mid, b * BINS : (b + 1) * BINS], -dilation)
                + shifted(taps[2 * mid :, b * BINS : (b + 1) * BINS], dilation)
                for b in range(BLOCKS + 1)
            ],
            axis=1,
        )
        squeezed = jax.nn.relu(inner).astype(BF16)
        stream = stream + lax.dot_general(
            trunk_out[layer], squeezed, (((0,), (0,)), ((), ())), preferred_element_type=F32
        )
    projected = dot(pair_weight[...], jax.nn.relu(stream).astype(BF16))

    right = []
    left = []
    for window, b, size in parts:
        begin = STRIDE * b + tower_row - margin
        turn = jnp.where(begin > 0, BINS - begin, -begin)
        terms = projected[:, window * BINS : (window + 1) * BINS]
        turned = pltpu.roll(terms, turn, 1)
        left.append(turned[:channels, :LANES])
        own = turned[channels:]
        if size > BINS:
            own = jnp.concatenate([own, own[:, : size - BINS]], axis=1)
        right.append(own[:, :size])
    used = sum(part[2] for part in parts)
    if lanes > used:
        right.append(jnp.zeros((channels, lanes - used), F32))
    right = jnp.concatenate(right, axis=1)
    rate = jnp.concatenate([rate_ref[...]] * (lanes // LANES), axis=1)
    lane = lax.broadcasted_iota(jnp.int32, (1, lanes), 1)

    def place_taps(ref, slot, act):
        act = act.astype(BF16)
        ref[pl.ds(slot * depth, channels), :] = pltpu.roll(act, 1, 1)
        ref[pl.ds(slot * depth + channels, channels), :] = act
        ref[pl.ds(slot * depth + 2 * channels, channels), :] = pltpu.roll(act, lanes - 1, 1)

    for row in range(height + 2 * margin):
        tiles = []
        for tile in range(lanes // LANES):
            piece = None
            here = lane[:, tile * LANES : (tile + 1) * LANES]
            for b in range(len(parts)):
                low, high = offsets[b], offsets[b] + parts[b][2]
                if high <= tile * LANES or low >= (tile + 1) * LANES:
                    continue
                spread = jnp.broadcast_to(left[b][:, row : row + 1], (channels, LANES))
                piece = spread if piece is None else jnp.where(here >= low, spread, piece)
            tiles.append(piece)
        mixed = jnp.concatenate(tiles, axis=1) + right - rate * decay_ref[pl.ds(row, 1), :]
        place_taps(taps_a, row, jnp.maximum(mixed, 0.0) * inside_ref[pl.ds(row, 1), :])

    def tower_block(kernels, mixes, taps, rows):
        for group, first in enumerate(range(0, rows, groups)):
            span = min(groups, rows - first)
            conv = dot(kernels[span][...], taps[pl.ds(first * depth, (span + 2) * depth), :])
            squeezed_ref[pl.ds(0, span * channels), pl.ds(group * lanes, lanes)] = jnp.maximum(
                conv, 0.0
            ).astype(BF16)
        full, left_over = rows // groups, rows % groups
        wide = dot(mixes[groups][...], squeezed_ref[:, pl.ds(0, full * lanes)])
        added = [
            wide[(row % groups) * channels :][:channels, (row // groups) * lanes :][:, :lanes]
            for row in range(full * groups)
        ]
        if left_over:
            rest = squeezed_ref[pl.ds(0, left_over * channels), pl.ds(full * lanes, lanes)]
            last = dot(mixes[left_over][...], rest)
            added += [last[r * channels : (r + 1) * channels] for r in range(left_over)]
        return added

    for row, added in enumerate(tower_block(conv_a, mix_a, taps_a, height + 2)):
        kept = taps_a[pl.ds((row + 1) * depth + channels, channels), :].astype(F32)
        grid = kept + added
        if 1 <= row <= height:
            grid_ref[pl.ds((row - 1) * channels, channels), :] = grid
        place_taps(taps_b, row, jnp.maximum(grid, 0.0) * inside_ref[pl.ds(row + 1, 1), :])
    for row, added in enumerate(tower_block(conv_b, mix_b, taps_b, height)):
        rows = pl.ds(row * channels, channels)
        final_ref[rows, :] = jnp.maximum(grid_ref[rows, :] + added, 0.0).astype(BF16)
    targets = head_ref.shape[0] // height
    contact = dot(head_ref[...], final_ref[...]).reshape(targets, height, lanes)

    wide = 2 * STRIDE
    stitched, before = [], []
    map_row = lax.broadcasted_iota(jnp.int32, (height, lanes), 0)
    for t in range(targets):
        skewed = contact[t]
        for bit in range((height - 1).bit_length()):
            turned = pltpu.roll(skewed, lanes - (1 << bit), 1)
            skewed = jnp.where((map_row >> bit) & 1 == 1, turned, skewed)
        for back, width, bands in ((0, BINS, stitched), (1, wide, before)):
            band = None
            for b in range(BLOCKS):
                k = back * BLOCKS + b
                first, reach = offsets[k] + margin, min(width, BINS - STRIDE * b)
                piece = skewed[:, first : first + reach]
                if reach < width:
                    piece = jnp.concatenate(
                        [piece, jnp.zeros((height, width - reach), F32)], axis=1
                    )
                piece = piece * stitch_ref[k][:, :width]
                band = piece if band is None else band + piece
            bands.append(band)
        stitched_ref[t] = stitched[t]

    near = jnp.concatenate([band[:, :wide] for band in stitched] + before, axis=0)
    col = lax.broadcasted_iota(jnp.int32, (wide, wide), 0)
    corner = lax.broadcasted_iota(jnp.int32, (wide, wide), 1)
    box = ((col > corner) & (col <= corner + STRIDE) & (corner < STRIDE)).astype(F32)
    square = jnp.dot(near, box, preferred_element_type=F32, precision=lax.Precision.HIGHEST)
    at = lax.broadcasted_iota(jnp.int32, near.shape, 1)
    contact = jnp.where((at >= 1) & (at <= STRIDE), jnp.exp(near), 0.0)
    down = jnp.sum(contact, axis=1, keepdims=True)
    here = lax.broadcasted_iota(jnp.int32, (height, wide), 0)
    there = lax.broadcasted_iota(jnp.int32, (height, wide), 1)

    def by_row(values, back):
        rows = []
        for t in range(back * targets, (back + 1) * targets):
            own = pltpu.roll(
                values[t * height : (t + 1) * height], 0, 1, stride=1, stride_axis=0
            )
            rows.append(jnp.sum(own, axis=0, keepdims=True))
        return rows

    down_rows = []
    for t in range(targets):
        own = jnp.where(here == there, down[t * height : (t + 1) * height], 0.0)
        down_rows.append(jnp.sum(own, axis=0, keepdims=True))
    rows = by_row(square, 0) + by_row(contact, 0)
    rows_before = by_row(square, 1) + by_row(contact, 1)
    keep_ref[...] = jnp.concatenate(rows + down_rows, axis=0)
    per_row = LANES // height
    first = lax.broadcasted_iota(jnp.int32, (per_row, LANES), 1) < height
    def packs_of(rows):
        return [
            jnp.concatenate(
                rows[p : p + per_row]
                + [jnp.zeros((1, LANES), F32)] * (per_row - len(rows[p : p + per_row])),
                axis=0,
            )
            for p in range(0, len(rows), per_row)
        ]

    packs = list(zip(packs_of(rows), packs_of(rows_before)))
    for k in range(1, STRIDE // height + 1):
        same = place_ref[0] + k < STRIDE // height
        packed = []
        for own, previous in packs:
            turned = pltpu.roll(jnp.where(same, own, previous), LANES - k * height, 1)
            turned = pltpu.roll(
                jnp.where(first, turned, 0.0), 0, 1, stride=height, stride_axis=0
            )
            packed.append(jnp.sum(turned, axis=0, keepdims=True))
        send_ref[lax.rem(place_ref[0] + k, STRIDE // height)] = jnp.concatenate(packed, axis=0)


def finish_kernel(height, keep_ref, got_ref, out_ref):
    targets = out_ref.shape[0]
    per_row = LANES // height
    keep = keep_ref[...][:, :height]
    got = jnp.sum(got_ref[...], axis=0)
    rows = []
    for q in range(2 * targets):
        at = (q % per_row) * height
        rows.append(got[q // per_row : q // per_row + 1, at : at + height])
    sums = keep[: 2 * targets] + jnp.concatenate(rows, axis=0)
    upstream = sums[targets:]
    downstream = keep[2 * targets :]
    insulation = sums[:targets] / (STRIDE * STRIDE)
    direction = (downstream - upstream) / (downstream + upstream)
    for t in range(targets):
        out_ref[t] = jnp.concatenate([insulation[t : t + 1], direction[t : t + 1]], axis=0)


def per_device(
    genome_bases,
    stitch_weight,
    stem_weight,
    trunk_in,
    trunk_out,
    pair_weight,
    distance_rate,
    tower_conv,
    tower_mix,
    head_weight,
):
    towers = lax.axis_size("tower")
    height = STRIDE // towers
    tower_index = lax.axis_index("tower")
    genome_index = lax.axis_index("genome")
    own = stem(genome_bases, stem_weight, lax.axis_size("genome"))
    features = lax.all_to_all(own, "genome", 0, 0, tiled=True)
    groups = 3
    channels = distance_rate.shape[0]
    targets = head_weight.shape[0]
    place = jnp.stack([tower_index, genome_index]).astype(jnp.int32)
    lanes = segments(2, height)[2]
    packs = -(-2 * targets * height // LANES)
    vmem = pl.BlockSpec(memory_space=pltpu.VMEM)
    smem = pl.BlockSpec(memory_space=pltpu.SMEM)
    layers, mid, width = trunk_in.shape
    rows = height + 4
    shapes = [
        jax.ShapeDtypeStruct((layers, 3 * mid, width // 3), BF16),
        jax.ShapeDtypeStruct((channels, LANES), F32),
        jax.ShapeDtypeStruct((rows, lanes), F32),
        jax.ShapeDtypeStruct((rows, lanes), F32),
        jax.ShapeDtypeStruct((targets * height, height * channels), BF16),
        jax.ShapeDtypeStruct((2 * BLOCKS, height, BINS), F32),
    ]
    for count in (height + 2, height):
        for span in spans_of(count, groups):
            tall = span * channels
            shapes.append(jax.ShapeDtypeStruct((tall, (span + 2) * 3 * channels), BF16))
            shapes.append(jax.ShapeDtypeStruct((tall, tall), BF16))
    prepared = pl.pallas_call(
        functools.partial(prepare_kernel, height, groups),
        out_shape=shapes,
        in_specs=[smem, pl.BlockSpec(memory_space=pltpu.HBM)] + [vmem] * 6,
        out_specs=[vmem] * len(shapes),
        compiler_params=pltpu.CompilerParams(vmem_limit_bytes=8 * 1024 * 1024),
        cost_estimate=pl.CostEstimate(flops=10**9, bytes_accessed=1 << 22, transcendentals=0),
        name="prepare",
    )(
        place,
        own,
        trunk_in,
        distance_rate.reshape(1, channels),
        tower_conv,
        tower_mix,
        head_weight,
        stitch_weight.reshape(1, BINS),
    )
    stitched, keep, send = pl.pallas_call(
        functools.partial(main_kernel, height, groups),
        out_shape=[
            jax.ShapeDtypeStruct((targets, height, BINS), F32),
            jax.ShapeDtypeStruct((3 * targets, LANES), F32),
            jax.ShapeDtypeStruct((towers, packs, LANES), F32),
        ],
        in_specs=[smem] + [vmem] * (3 + len(shapes)),
        out_specs=[vmem] * 3,
        scratch_shapes=[
            pltpu.VMEM((rows * 3 * channels, lanes), BF16),
            pltpu.VMEM(((height + 2) * 3 * channels, lanes), BF16),
            pltpu.VMEM((height * channels, lanes), F32),
            pltpu.VMEM((height * channels, lanes), BF16),
            pltpu.VMEM((groups * channels, -(-(height + 2) // groups) * lanes), BF16),
        ],
        compiler_params=pltpu.CompilerParams(vmem_limit_bytes=VMEM_BYTES),
        name="windows",
    )(place, features, jnp.transpose(trunk_out, (0, 2, 1)), pair_weight, *prepared)
    got = lax.all_to_all(send, "tower", 0, 0, tiled=True)
    scores = pl.pallas_call(
        functools.partial(finish_kernel, height),
        out_shape=jax.ShapeDtypeStruct((targets, 2, height), F32),
        in_specs=[vmem, vmem],
        out_specs=vmem,
        compiler_params=pltpu.CompilerParams(vmem_limit_bytes=2 * 1024 * 1024),
        name="finish",
    )(keep, got)
    return (stitched, jnp.transpose(scores, (1, 0, 2)))


def solution(mesh):
    placed = (P("genome"), P(), P(), P(), P(), P(), P(), P(), P(), P())
    return jax.shard_map(
        per_device,
        mesh=mesh,
        in_specs=placed,
        out_specs=(P(None, ("genome", "tower"), None), P(None, None, ("genome", "tower"))),
        check_vma=False,
    )
```

```python
import functools

import jax
import jax.numpy as jnp
from jax import lax
from jax.experimental import pallas as pl
from jax.experimental.pallas import tpu as pltpu
from jax.sharding import PartitionSpec as P

BP = 2048
STRIDE = 64
BINS = 256
BLOCKS = BINS // STRIDE
LANES = 128
F32 = jnp.float32
BF16 = jnp.bfloat16
VMEM_BYTES = 40 * 1024 * 1024


def dot(a, b):
    return jnp.dot(a, b, preferred_element_type=F32)


def stem_kernel(bins, bases_hbm, weight_hbm, out_ref, bases, weight, base_sem, weight_sem):
    groups = BP // LANES
    chunks = weight.shape[0]
    span = weight.shape[2]
    base_copy = pltpu.make_async_copy(bases_hbm, bases, base_sem)
    base_copy.start()
    copies = []
    for k in range(chunks):
        copy = pltpu.make_async_copy(
            weight_hbm.at[:, pl.ds(k * span, span)], weight.at[k], weight_sem.at[k]
        )
        copy.start()
        copies.append(copy)
    row = lax.broadcasted_iota(jnp.int32, (LANES, 4 * LANES), 0)
    col = lax.broadcasted_iota(jnp.int32, (LANES, 4 * LANES), 1)
    repeat = (row == col // 4).astype(F32).astype(BF16)
    letter = (lax.broadcasted_iota(jnp.int32, (1, 4 * LANES), 1) % 4).astype(F32)
    base_copy.wait()
    total = None
    per_chunk = groups // chunks
    for k in range(chunks):
        rows = jnp.concatenate(
            [
                bases[pl.ds(k * per_chunk + q, bins, stride=groups), :]
                for q in range(per_chunk)
            ],
            axis=0,
        )
        spread = dot(rows.astype(F32).astype(BF16), repeat)
        hot = jnp.where(spread == letter, 1.0, 0.0).astype(BF16)
        hot = jnp.concatenate(
            [hot[q * bins : (q + 1) * bins] for q in range(per_chunk)], axis=1
        )
        copies[k].wait()
        part = lax.dot_general(
            weight[k], hot, (((1,), (1,)), ((), ())), preferred_element_type=F32
        )
        total = part if total is None else total + part
    total = total.astype(BF16)
    half = out_ref.shape[1]
    packed = jnp.concatenate([total[:half], total[half:]], axis=1)
    for slot in range(out_ref.shape[0]):
        out_ref[slot] = packed


def stem(genome_bases, stem_weight, slots):
    bins = genome_bases.shape[0] // BP
    channels, depth = stem_weight.shape
    chunks = 2
    return pl.pallas_call(
        functools.partial(stem_kernel, bins),
        out_shape=jax.ShapeDtypeStruct((slots, channels // 2, 2 * bins), BF16),
        in_specs=[pl.BlockSpec(memory_space=pltpu.HBM)] * 2,
        out_specs=pl.BlockSpec(memory_space=pltpu.VMEM),
        scratch_shapes=[
            pltpu.VMEM((genome_bases.shape[0] // LANES, LANES), jnp.int32),
            pltpu.VMEM((chunks, channels, depth // chunks), BF16),
            pltpu.SemaphoreType.DMA,
            pltpu.SemaphoreType.DMA((chunks,)),
        ],
        compiler_params=pltpu.CompilerParams(vmem_limit_bytes=63 * 1024 * 1024),
        name="stem",
    )(genome_bases.reshape(-1, LANES), stem_weight)


def banded(kernel, rows):
    taps, out_channels, depth = kernel.shape
    flat = jnp.concatenate([kernel[u] for u in range(taps)], axis=1)
    bands = []
    for r in range(rows):
        parts = [flat]
        if r:
            parts.insert(0, jnp.zeros((out_channels, r * depth), BF16))
        if rows - 1 - r:
            parts.append(jnp.zeros((out_channels, (rows - 1 - r) * depth), BF16))
        bands.append(jnp.concatenate(parts, axis=1) if len(parts) > 1 else flat)
    return jnp.concatenate(bands, axis=0)


def block_diagonal(matrix, count):
    height, width = matrix.shape
    tiled = jnp.concatenate([jnp.concatenate([matrix] * count, axis=1)] * count, axis=0)
    row = lax.broadcasted_iota(jnp.int32, tiled.shape, 0) // height
    col = lax.broadcasted_iota(jnp.int32, tiled.shape, 1) // width
    return jnp.where(row == col, tiled, jnp.zeros((), BF16))


def head_by_row(head, count):
    targets, width = head.shape
    wide = jnp.concatenate([head] * count, axis=1)
    tall = jnp.broadcast_to(wide[:, None, :], (targets, count, count * width))
    row = lax.broadcasted_iota(jnp.int32, tall.shape, 1)
    col = lax.broadcasted_iota(jnp.int32, tall.shape, 2) // width
    return jnp.where(row == col, tall, jnp.zeros((), BF16)).reshape(targets * count, count * width)


def segments(margin, height):
    whole = [BINS - STRIDE * b + margin + 1 for b in range(BLOCKS)]
    near = 2 * STRIDE + height - 1 + 2 * margin
    parts = [(b, b, whole[b]) for b in range(BLOCKS)]
    parts += [(b + 1, b, min(whole[b], near)) for b in range(BLOCKS)]
    sizes = [part[2] for part in parts]
    offsets = [sum(sizes[:k]) for k in range(len(sizes))]
    lanes = -(-sum(sizes) // LANES) * LANES
    return parts, offsets, lanes


def shifted(values, offset):
    if offset == 0:
        return values
    channels, extent = values.shape
    edge = jnp.zeros((channels, abs(offset)), values.dtype)
    if offset >= 0:
        return jnp.concatenate([values[:, offset:], edge], axis=1)
    return jnp.concatenate([edge, values[:, : extent + offset]], axis=1)


def spans_of(rows, groups):
    return sorted({groups, rows % groups} - {0})


def prepare_kernel(
    height,
    groups,
    place_ref,
    _,
    trunk_in,
    rate_in,
    conv_in,
    mix_in,
    head_in,
    stitch_in,
    trunk_ref,
    rate_ref,
    decay_ref,
    inside_ref,
    head_ref,
    stitch_ref,
    *conv_refs,
):
    margin = 2
    parts, offsets, lanes = segments(margin, height)
    tower_row = place_ref[0] * height
    for layer in range(trunk_in.shape[0]):
        flat = trunk_in[layer]
        width = flat.shape[1] // 3
        trunk_ref[layer] = jnp.concatenate(
            [flat[:, q * width : (q + 1) * width] for q in range(3)], axis=0
        )
    at = 0
    for block, rows in enumerate((height + 2, height)):
        for span in spans_of(rows, groups):
            conv_refs[at][...] = banded(conv_in[block], span)
            conv_refs[at + 1][...] = block_diagonal(mix_in[block], span)
            at += 2
    head_ref[...] = head_by_row(head_in[...], height)
    channels = rate_in.shape[1]
    row = lax.broadcasted_iota(jnp.int32, (channels, channels), 0)
    col = lax.broadcasted_iota(jnp.int32, (channels, channels), 1)
    rate = jnp.sum(jnp.where(row == col, rate_in[...], 0.0), axis=1, keepdims=True)
    rate_ref[...] = jnp.broadcast_to(rate, rate_ref.shape)

    lane = lax.broadcasted_iota(jnp.int32, (height + 2 * margin, lanes), 1)
    block_of = jnp.zeros((height + 2 * margin, lanes), jnp.int32)
    start_of = jnp.zeros((height + 2 * margin, lanes), jnp.int32)
    for (_, b, _), offset in zip(parts, offsets):
        block_of = jnp.where(lane >= offset, b, block_of)
        start_of = jnp.where(lane >= offset, offset, start_of)
    step = lane - start_of
    first_row = STRIDE * block_of + tower_row - margin
    column = first_row + step
    in_column = (column < BINS) & (column >= 0)

    row = lax.broadcasted_iota(jnp.int32, (height + 2 * margin, lanes), 0)
    decay_ref[...] = jnp.log1p(jnp.abs(step - row).astype(F32))
    at = first_row + row
    inside_ref[...] = jnp.where(in_column & (at >= 0) & (at < BINS), 1.0, 0.0)

    local = lax.broadcasted_iota(jnp.int32, (height, BINS), 0)
    ahead = lax.broadcasted_iota(jnp.int32, (height, BINS), 1)
    for back in range(2):
        weight_sum = jnp.zeros((height, BINS), F32)
        weights = []
        for b in range(BLOCKS):
            weight = jnp.where(ahead == STRIDE * b + tower_row + local, stitch_in[...], 0)
            weight = jnp.sum(weight.astype(F32), axis=1, keepdims=True)
            weight = jnp.where(place_ref[1] - back >= b, weight, 0.0)
            reach = STRIDE * b + tower_row + local + ahead < BINS
            weight = jnp.where(reach, weight, 0.0)
            weights.append(weight)
            weight_sum = weight_sum + weight
        scale = 1.0 / jnp.maximum(weight_sum, 1.0)
        for b in range(BLOCKS):
            stitch_ref[back * BLOCKS + b] = weights[b] * scale


def main_kernel(
    height,
    groups,
    place_ref,
    features,
    trunk_out,
    pair_weight,
    trunk_in,
    rate_ref,
    decay_ref,
    inside_ref,
    head_ref,
    stitch_ref,
    *rest,
):
    margin = 2
    parts, offsets, lanes = segments(margin, height)
    tower_row = place_ref[0] * height
    channels = rate_ref.shape[0]
    depth = 3 * channels
    rest = list(rest)
    conv_a, conv_b, mix_a, mix_b = {}, {}, {}, {}
    for span in spans_of(height + 2, groups):
        conv_a[span], mix_a[span] = rest.pop(0), rest.pop(0)
    for span in spans_of(height, groups):
        conv_b[span], mix_b[span] = rest.pop(0), rest.pop(0)
    stitched_ref, keep_ref, send_ref, taps_a, taps_b, grid_ref, final_ref, squeezed_ref = rest

    starts = features.shape[0]
    blocks = []
    for d in range(-BLOCKS, BLOCKS):
        at = place_ref[1] + d
        block = features[jnp.clip(at, 0, starts - 1)]
        blocks.append(jnp.where((at >= 0) & (at < starts), block, jnp.zeros_like(block)))
    blocks = jnp.concatenate(
        [
            jnp.concatenate([half[:, :STRIDE] for half in blocks], axis=1),
            jnp.concatenate([half[:, STRIDE:] for half in blocks], axis=1),
        ],
        axis=0,
    )
    extent = BINS
    windows = []
    for b in range(BLOCKS + 1):
        first = (BLOCKS - b) * STRIDE
        windows.append(blocks[:, first : first + BINS].astype(F32))
    stream = jnp.concatenate(windows, axis=1)
    layers = trunk_in.shape[0]
    for layer in range(layers):
        dilation = max(1, extent // 2 ** (layers - layer))
        active = jnp.maximum(stream, 0.0).astype(BF16)
        mid = trunk_in.shape[1] // 3
        taps = dot(trunk_in[layer], active)
        inner = taps[mid : 2 * mid] + jnp.concatenate(
            [
                shifted(taps[:mid, b * BINS : (b + 1) * BINS], -dilation)
                + shifted(taps[2 * mid :, b * BINS : (b + 1) * BINS], dilation)
                for b in range(BLOCKS + 1)
            ],
            axis=1,
        )
        squeezed = jax.nn.relu(inner).astype(BF16)
        stream = stream + lax.dot_general(
            trunk_out[layer], squeezed, (((0,), (0,)), ((), ())), preferred_element_type=F32
        )
    projected = dot(pair_weight[...], jax.nn.relu(stream).astype(BF16))

    right = []
    left = []
    for window, b, size in parts:
        begin = STRIDE * b + tower_row - margin
        turn = jnp.where(begin > 0, BINS - begin, -begin)
        terms = projected[:, window * BINS : (window + 1) * BINS]
        turned = pltpu.roll(terms, turn, 1)
        left.append(turned[:channels, :LANES])
        own = turned[channels:]
        if size > BINS:
            own = jnp.concatenate([own, own[:, : size - BINS]], axis=1)
        right.append(own[:, :size])
    used = sum(part[2] for part in parts)
    if lanes > used:
        right.append(jnp.zeros((channels, lanes - used), F32))
    right = jnp.concatenate(right, axis=1)
    rate = jnp.concatenate([rate_ref[...]] * (lanes // LANES), axis=1)
    lane = lax.broadcasted_iota(jnp.int32, (1, lanes), 1)

    def place_taps(ref, slot, act):
        act = act.astype(BF16)
        ref[pl.ds(slot * depth, channels), :] = pltpu.roll(act, 1, 1)
        ref[pl.ds(slot * depth + channels, channels), :] = act
        ref[pl.ds(slot * depth + 2 * channels, channels), :] = pltpu.roll(act, lanes - 1, 1)

    for row in range(height + 2 * margin):
        tiles = []
        for tile in range(lanes // LANES):
            piece = None
            here = lane[:, tile * LANES : (tile + 1) * LANES]
            for b in range(len(parts)):
                low, high = offsets[b], offsets[b] + parts[b][2]
                if high <= tile * LANES or low >= (tile + 1) * LANES:
                    continue
                spread = jnp.broadcast_to(left[b][:, row : row + 1], (channels, LANES))
                piece = spread if piece is None else jnp.where(here >= low, spread, piece)
            tiles.append(piece)
        mixed = jnp.concatenate(tiles, axis=1) + right - rate * decay_ref[pl.ds(row, 1), :]
        place_taps(taps_a, row, jnp.maximum(mixed, 0.0) * inside_ref[pl.ds(row, 1), :])

    def tower_block(kernels, mixes, taps, rows):
        for group, first in enumerate(range(0, rows, groups)):
            span = min(groups, rows - first)
            conv = dot(kernels[span][...], taps[pl.ds(first * depth, (span + 2) * depth), :])
            squeezed_ref[pl.ds(0, span * channels), pl.ds(group * lanes, lanes)] = jnp.maximum(
                conv, 0.0
            ).astype(BF16)
        full, left_over = rows // groups, rows % groups
        wide = dot(mixes[groups][...], squeezed_ref[:, pl.ds(0, full * lanes)])
        added = [
            wide[(row % groups) * channels :][:channels, (row // groups) * lanes :][:, :lanes]
            for row in range(full * groups)
        ]
        if left_over:
            rest = squeezed_ref[pl.ds(0, left_over * channels), pl.ds(full * lanes, lanes)]
            last = dot(mixes[left_over][...], rest)
            added += [last[r * channels : (r + 1) * channels] for r in range(left_over)]
        return added

    for row, added in enumerate(tower_block(conv_a, mix_a, taps_a, height + 2)):
        kept = taps_a[pl.ds((row + 1) * depth + channels, channels), :].astype(F32)
        grid = kept + added
        if 1 <= row <= height:
            grid_ref[pl.ds((row - 1) * channels, channels), :] = grid
        place_taps(taps_b, row, jnp.maximum(grid, 0.0) * inside_ref[pl.ds(row + 1, 1), :])
    for row, added in enumerate(tower_block(conv_b, mix_b, taps_b, height)):
        rows = pl.ds(row * channels, channels)
        final_ref[rows, :] = jnp.maximum(grid_ref[rows, :] + added, 0.0).astype(BF16)
    targets = head_ref.shape[0] // height
    contact = dot(head_ref[...], final_ref[...]).reshape(targets, height, lanes)

    wide = 2 * STRIDE
    stitched, before = [], []
    map_row = lax.broadcasted_iota(jnp.int32, (height, lanes), 0)
    for t in range(targets):
        skewed = contact[t]
        for bit in range((height - 1).bit_length()):
            turned = pltpu.roll(skewed, lanes - (1 << bit), 1)
            skewed = jnp.where((map_row >> bit) & 1 == 1, turned, skewed)
        for back, width, bands in ((0, BINS, stitched), (1, wide, before)):
            band = None
            for b in range(BLOCKS):
                k = back * BLOCKS + b
                first, reach = offsets[k] + margin, min(width, BINS - STRIDE * b)
                piece = skewed[:, first : first + reach]
                if reach < width:
                    piece = jnp.concatenate(
                        [piece, jnp.zeros((height, width - reach), F32)], axis=1
                    )
                piece = piece * stitch_ref[k][:, :width]
                band = piece if band is None else band + piece
            bands.append(band)
        stitched_ref[t] = stitched[t]

    near = jnp.concatenate([band[:, :wide] for band in stitched] + before, axis=0)
    col = lax.broadcasted_iota(jnp.int32, (wide, wide), 0)
    corner = lax.broadcasted_iota(jnp.int32, (wide, wide), 1)
    box = ((col > corner) & (col <= corner + STRIDE) & (corner < STRIDE)).astype(F32)
    square = jnp.dot(near, box, preferred_element_type=F32, precision=lax.Precision.HIGHEST)
    at = lax.broadcasted_iota(jnp.int32, near.shape, 1)
    contact = jnp.where((at >= 1) & (at <= STRIDE), jnp.exp(near), 0.0)
    down = jnp.sum(contact, axis=1, keepdims=True)
    here = lax.broadcasted_iota(jnp.int32, (height, wide), 0)
    there = lax.broadcasted_iota(jnp.int32, (height, wide), 1)

    def by_row(values, back):
        rows = []
        for t in range(back * targets, (back + 1) * targets):
            own = pltpu.roll(
                values[t * height : (t + 1) * height], 0, 1, stride=1, stride_axis=0
            )
            rows.append(jnp.sum(own, axis=0, keepdims=True))
        return rows

    down_rows = []
    for t in range(targets):
        own = jnp.where(here == there, down[t * height : (t + 1) * height], 0.0)
        down_rows.append(jnp.sum(own, axis=0, keepdims=True))
    rows = by_row(square, 0) + by_row(contact, 0)
    rows_before = by_row(square, 1) + by_row(contact, 1)
    keep_ref[...] = jnp.concatenate(rows + down_rows, axis=0)
    per_row = LANES // height
    first = lax.broadcasted_iota(jnp.int32, (per_row, LANES), 1) < height
    def packs_of(rows):
        return [
            jnp.concatenate(
                rows[p : p + per_row]
                + [jnp.zeros((1, LANES), F32)] * (per_row - len(rows[p : p + per_row])),
                axis=0,
            )
            for p in range(0, len(rows), per_row)
        ]

    packs = list(zip(packs_of(rows), packs_of(rows_before)))
    for k in range(1, STRIDE // height + 1):
        same = place_ref[0] + k < STRIDE // height
        packed = []
        for own, previous in packs:
            turned = pltpu.roll(jnp.where(same, own, previous), LANES - k * height, 1)
            turned = pltpu.roll(
                jnp.where(first, turned, 0.0), 0, 1, stride=height, stride_axis=0
            )
            packed.append(jnp.sum(turned, axis=0, keepdims=True))
        send_ref[lax.rem(place_ref[0] + k, STRIDE // height)] = jnp.concatenate(packed, axis=0)


def finish_kernel(height, keep_ref, got_ref, out_ref):
    targets = out_ref.shape[0]
    per_row = LANES // height
    keep = keep_ref[...][:, :height]
    got = got_ref[...]
    rows = []
    for q in range(2 * targets):
        at = (q % per_row) * height
        rows.append(got[q // per_row : q // per_row + 1, at : at + height])
    sums = keep[: 2 * targets] + jnp.concatenate(rows, axis=0)
    upstream = sums[targets:]
    downstream = keep[2 * targets :]
    insulation = sums[:targets] / (STRIDE * STRIDE)
    direction = (downstream - upstream) / (downstream + upstream)
    for t in range(targets):
        out_ref[t] = jnp.concatenate([insulation[t : t + 1], direction[t : t + 1]], axis=0)


def per_device(
    genome_bases,
    stitch_weight,
    stem_weight,
    trunk_in,
    trunk_out,
    pair_weight,
    distance_rate,
    tower_conv,
    tower_mix,
    head_weight,
):
    towers = lax.axis_size("tower")
    height = STRIDE // towers
    tower_index = lax.axis_index("tower")
    genome_index = lax.axis_index("genome")
    own = stem(genome_bases, stem_weight, lax.axis_size("genome"))
    features = lax.all_to_all(own, "genome", 0, 0, tiled=True)
    groups = 3
    channels = distance_rate.shape[0]
    targets = head_weight.shape[0]
    place = jnp.stack([tower_index, genome_index]).astype(jnp.int32)
    lanes = segments(2, height)[2]
    packs = -(-2 * targets * height // LANES)
    vmem = pl.BlockSpec(memory_space=pltpu.VMEM)
    smem = pl.BlockSpec(memory_space=pltpu.SMEM)
    layers, mid, width = trunk_in.shape
    rows = height + 4
    shapes = [
        jax.ShapeDtypeStruct((layers, 3 * mid, width // 3), BF16),
        jax.ShapeDtypeStruct((channels, LANES), F32),
        jax.ShapeDtypeStruct((rows, lanes), F32),
        jax.ShapeDtypeStruct((rows, lanes), F32),
        jax.ShapeDtypeStruct((targets * height, height * channels), BF16),
        jax.ShapeDtypeStruct((2 * BLOCKS, height, BINS), F32),
    ]
    for count in (height + 2, height):
        for span in spans_of(count, groups):
            tall = span * channels
            shapes.append(jax.ShapeDtypeStruct((tall, (span + 2) * 3 * channels), BF16))
            shapes.append(jax.ShapeDtypeStruct((tall, tall), BF16))
    prepared = pl.pallas_call(
        functools.partial(prepare_kernel, height, groups),
        out_shape=shapes,
        in_specs=[smem, pl.BlockSpec(memory_space=pltpu.HBM)] + [vmem] * 6,
        out_specs=[vmem] * len(shapes),
        compiler_params=pltpu.CompilerParams(vmem_limit_bytes=8 * 1024 * 1024),
        cost_estimate=pl.CostEstimate(flops=10**9, bytes_accessed=1 << 22, transcendentals=0),
        name="prepare",
    )(
        place,
        own,
        trunk_in,
        distance_rate.reshape(1, channels),
        tower_conv,
        tower_mix,
        head_weight,
        stitch_weight.reshape(1, BINS),
    )
    stitched, keep, send = pl.pallas_call(
        functools.partial(main_kernel, height, groups),
        out_shape=[
            jax.ShapeDtypeStruct((targets, height, BINS), F32),
            jax.ShapeDtypeStruct((3 * targets, LANES), F32),
            jax.ShapeDtypeStruct((towers, packs, LANES), F32),
        ],
        in_specs=[smem] + [vmem] * (3 + len(shapes)),
        out_specs=[vmem] * 3,
        scratch_shapes=[
            pltpu.VMEM((rows * 3 * channels, lanes), BF16),
            pltpu.VMEM(((height + 2) * 3 * channels, lanes), BF16),
            pltpu.VMEM((height * channels, lanes), F32),
            pltpu.VMEM((height * channels, lanes), BF16),
            pltpu.VMEM((groups * channels, -(-(height + 2) // groups) * lanes), BF16),
        ],
        compiler_params=pltpu.CompilerParams(vmem_limit_bytes=VMEM_BYTES),
        name="windows",
    )(place, features, jnp.transpose(trunk_out, (0, 2, 1)), pair_weight, *prepared)
    got = lax.psum_scatter(send, "tower", scatter_dimension=0)
    scores = pl.pallas_call(
        functools.partial(finish_kernel, height),
        out_shape=jax.ShapeDtypeStruct((targets, 2, height), F32),
        in_specs=[vmem, vmem],
        out_specs=vmem,
        compiler_params=pltpu.CompilerParams(vmem_limit_bytes=2 * 1024 * 1024),
        name="finish",
    )(keep, got)
    return (stitched, jnp.transpose(scores, (1, 0, 2)))


def solution(mesh):
    placed = (P("genome"), P(), P(), P(), P(), P(), P(), P(), P(), P())
    return jax.shard_map(
        per_device,
        mesh=mesh,
        in_specs=placed,
        out_specs=(P(None, ("genome", "tower"), None), P(None, None, ("genome", "tower"))),
        check_vma=False,
    )
```

```python
import functools

import jax
import jax.numpy as jnp
from jax import lax
from jax.experimental import pallas as pl
from jax.experimental.pallas import tpu as pltpu
from jax.sharding import PartitionSpec as P

BP = 2048
STRIDE = 64
BINS = 256
BLOCKS = BINS // STRIDE
LANES = 128
F32 = jnp.float32
BF16 = jnp.bfloat16
VMEM_BYTES = 40 * 1024 * 1024


def dot(a, b):
    return jnp.dot(a, b, preferred_element_type=F32)


def stem_kernel(bins, bases_hbm, weight_hbm, out_ref, bases, weight, base_sem, weight_sem):
    groups = BP // LANES
    chunks = weight.shape[0]
    span = weight.shape[2]
    base_copy = pltpu.make_async_copy(bases_hbm, bases, base_sem)
    base_copy.start()
    copies = []
    for k in range(chunks):
        copy = pltpu.make_async_copy(
            weight_hbm.at[:, pl.ds(k * span, span)], weight.at[k], weight_sem.at[k]
        )
        copy.start()
        copies.append(copy)
    row = lax.broadcasted_iota(jnp.int32, (LANES, 4 * LANES), 0)
    col = lax.broadcasted_iota(jnp.int32, (LANES, 4 * LANES), 1)
    repeat = (row == col // 4).astype(F32).astype(BF16)
    letter = (lax.broadcasted_iota(jnp.int32, (1, 4 * LANES), 1) % 4).astype(F32)
    base_copy.wait()
    total = None
    per_chunk = groups // chunks
    for k in range(chunks):
        rows = jnp.concatenate(
            [
                bases[pl.ds(k * per_chunk + q, bins, stride=groups), :]
                for q in range(per_chunk)
            ],
            axis=0,
        )
        spread = dot(rows.astype(F32).astype(BF16), repeat)
        hot = jnp.where(spread == letter, 1.0, 0.0).astype(BF16)
        hot = jnp.concatenate(
            [hot[q * bins : (q + 1) * bins] for q in range(per_chunk)], axis=1
        )
        copies[k].wait()
        part = lax.dot_general(
            weight[k], hot, (((1,), (1,)), ((), ())), preferred_element_type=F32
        )
        total = part if total is None else total + part
    total = total.astype(BF16)
    half = out_ref.shape[1]
    packed = jnp.concatenate([total[:half], total[half:]], axis=1)
    for slot in range(out_ref.shape[0]):
        out_ref[slot] = packed


def stem(genome_bases, stem_weight, slots):
    bins = genome_bases.shape[0] // BP
    channels, depth = stem_weight.shape
    chunks = 2
    return pl.pallas_call(
        functools.partial(stem_kernel, bins),
        out_shape=jax.ShapeDtypeStruct((slots, channels // 2, 2 * bins), BF16),
        in_specs=[pl.BlockSpec(memory_space=pltpu.HBM)] * 2,
        out_specs=pl.BlockSpec(memory_space=pltpu.VMEM),
        scratch_shapes=[
            pltpu.VMEM((genome_bases.shape[0] // LANES, LANES), jnp.int32),
            pltpu.VMEM((chunks, channels, depth // chunks), BF16),
            pltpu.SemaphoreType.DMA,
            pltpu.SemaphoreType.DMA((chunks,)),
        ],
        compiler_params=pltpu.CompilerParams(vmem_limit_bytes=63 * 1024 * 1024),
        name="stem",
    )(genome_bases.reshape(-1, LANES), stem_weight)


def banded(kernel, rows):
    taps, out_channels, depth = kernel.shape
    flat = jnp.concatenate([kernel[u] for u in range(taps)], axis=1)
    bands = []
    for r in range(rows):
        parts = [flat]
        if r:
            parts.insert(0, jnp.zeros((out_channels, r * depth), BF16))
        if rows - 1 - r:
            parts.append(jnp.zeros((out_channels, (rows - 1 - r) * depth), BF16))
        bands.append(jnp.concatenate(parts, axis=1) if len(parts) > 1 else flat)
    return jnp.concatenate(bands, axis=0)


def block_diagonal(matrix, count):
    height, width = matrix.shape
    tiled = jnp.concatenate([jnp.concatenate([matrix] * count, axis=1)] * count, axis=0)
    row = lax.broadcasted_iota(jnp.int32, tiled.shape, 0) // height
    col = lax.broadcasted_iota(jnp.int32, tiled.shape, 1) // width
    return jnp.where(row == col, tiled, jnp.zeros((), BF16))


def head_by_row(head, count):
    targets, width = head.shape
    wide = jnp.concatenate([head] * count, axis=1)
    tall = jnp.broadcast_to(wide[:, None, :], (targets, count, count * width))
    row = lax.broadcasted_iota(jnp.int32, tall.shape, 1)
    col = lax.broadcasted_iota(jnp.int32, tall.shape, 2) // width
    return jnp.where(row == col, tall, jnp.zeros((), BF16)).reshape(targets * count, count * width)


def segments(margin, height):
    whole = [BINS - STRIDE * b + margin + 1 for b in range(BLOCKS)]
    near = 2 * STRIDE + height - 1 + 2 * margin
    parts = [(b, b, whole[b]) for b in range(BLOCKS)]
    parts += [(b + 1, b, min(whole[b], near)) for b in range(BLOCKS)]
    sizes = [part[2] for part in parts]
    offsets = [sum(sizes[:k]) for k in range(len(sizes))]
    lanes = -(-sum(sizes) // LANES) * LANES
    return parts, offsets, lanes


def shifted(values, offset):
    if offset == 0:
        return values
    channels, extent = values.shape
    edge = jnp.zeros((channels, abs(offset)), values.dtype)
    if offset >= 0:
        return jnp.concatenate([values[:, offset:], edge], axis=1)
    return jnp.concatenate([edge, values[:, : extent + offset]], axis=1)


def spans_of(rows, groups):
    return sorted({groups, rows % groups} - {0})


def prepare_kernel(
    height,
    groups,
    place_ref,
    _,
    trunk_in,
    rate_in,
    conv_in,
    mix_in,
    head_in,
    stitch_in,
    trunk_ref,
    rate_ref,
    decay_ref,
    inside_ref,
    head_ref,
    stitch_ref,
    *conv_refs,
):
    margin = 2
    parts, offsets, lanes = segments(margin, height)
    tower_row = place_ref[0] * height
    for layer in range(trunk_in.shape[0]):
        flat = trunk_in[layer]
        width = flat.shape[1] // 3
        trunk_ref[layer] = jnp.concatenate(
            [flat[:, q * width : (q + 1) * width] for q in range(3)], axis=0
        )
    at = 0
    for block, rows in enumerate((height + 2, height)):
        for span in spans_of(rows, groups):
            conv_refs[at][...] = banded(conv_in[block], span)
            conv_refs[at + 1][...] = block_diagonal(mix_in[block], span)
            at += 2
    head_ref[...] = head_by_row(head_in[...], height)
    channels = rate_in.shape[1]
    row = lax.broadcasted_iota(jnp.int32, (channels, channels), 0)
    col = lax.broadcasted_iota(jnp.int32, (channels, channels), 1)
    rate = jnp.sum(jnp.where(row == col, rate_in[...], 0.0), axis=1, keepdims=True)
    rate_ref[...] = jnp.broadcast_to(rate, rate_ref.shape)

    lane = lax.broadcasted_iota(jnp.int32, (height + 2 * margin, lanes), 1)
    block_of = jnp.zeros((height + 2 * margin, lanes), jnp.int32)
    start_of = jnp.zeros((height + 2 * margin, lanes), jnp.int32)
    for (_, b, _), offset in zip(parts, offsets):
        block_of = jnp.where(lane >= offset, b, block_of)
        start_of = jnp.where(lane >= offset, offset, start_of)
    step = lane - start_of
    first_row = STRIDE * block_of + tower_row - margin
    column = first_row + step
    in_column = (column < BINS) & (column >= 0)

    row = lax.broadcasted_iota(jnp.int32, (height + 2 * margin, lanes), 0)
    decay_ref[...] = jnp.log1p(jnp.abs(step - row).astype(F32))
    at = first_row + row
    inside_ref[...] = jnp.where(in_column & (at >= 0) & (at < BINS), 1.0, 0.0)

    local = lax.broadcasted_iota(jnp.int32, (height, BINS), 0)
    ahead = lax.broadcasted_iota(jnp.int32, (height, BINS), 1)
    for back in range(2):
        weight_sum = jnp.zeros((height, BINS), F32)
        weights = []
        for b in range(BLOCKS):
            weight = jnp.where(ahead == STRIDE * b + tower_row + local, stitch_in[...], 0)
            weight = jnp.sum(weight.astype(F32), axis=1, keepdims=True)
            weight = jnp.where(place_ref[1] - back >= b, weight, 0.0)
            reach = STRIDE * b + tower_row + local + ahead < BINS
            weight = jnp.where(reach, weight, 0.0)
            weights.append(weight)
            weight_sum = weight_sum + weight
        scale = 1.0 / jnp.maximum(weight_sum, 1.0)
        for b in range(BLOCKS):
            stitch_ref[back * BLOCKS + b] = weights[b] * scale


def main_kernel(
    height,
    groups,
    place_ref,
    features,
    trunk_out,
    pair_weight,
    trunk_in,
    rate_ref,
    decay_ref,
    inside_ref,
    head_ref,
    stitch_ref,
    *rest,
):
    margin = 2
    parts, offsets, lanes = segments(margin, height)
    tower_row = place_ref[0] * height
    channels = rate_ref.shape[0]
    depth = 3 * channels
    rest = list(rest)
    conv_a, conv_b, mix_a, mix_b = {}, {}, {}, {}
    for span in spans_of(height + 2, groups):
        conv_a[span], mix_a[span] = rest.pop(0), rest.pop(0)
    for span in spans_of(height, groups):
        conv_b[span], mix_b[span] = rest.pop(0), rest.pop(0)
    stitched_ref, keep_ref, send_ref, taps_a, taps_b, grid_ref, final_ref, squeezed_ref = rest

    starts = features.shape[0]
    blocks = []
    for d in range(-BLOCKS, BLOCKS):
        at = place_ref[1] + d
        block = features[jnp.clip(at, 0, starts - 1)]
        blocks.append(jnp.where((at >= 0) & (at < starts), block, jnp.zeros_like(block)))
    blocks = jnp.concatenate(
        [
            jnp.concatenate([half[:, :STRIDE] for half in blocks], axis=1),
            jnp.concatenate([half[:, STRIDE:] for half in blocks], axis=1),
        ],
        axis=0,
    )
    extent = BINS
    windows = []
    for b in range(BLOCKS + 1):
        first = (BLOCKS - b) * STRIDE
        windows.append(blocks[:, first : first + BINS].astype(F32))
    stream = jnp.concatenate(windows, axis=1)
    layers = trunk_in.shape[0]
    for layer in range(layers):
        dilation = max(1, extent // 2 ** (layers - layer))
        active = jnp.maximum(stream, 0.0).astype(BF16)
        mid = trunk_in.shape[1] // 3
        taps = dot(trunk_in[layer], active)
        inner = taps[mid : 2 * mid] + jnp.concatenate(
            [
                shifted(taps[:mid, b * BINS : (b + 1) * BINS], -dilation)
                + shifted(taps[2 * mid :, b * BINS : (b + 1) * BINS], dilation)
                for b in range(BLOCKS + 1)
            ],
            axis=1,
        )
        squeezed = jax.nn.relu(inner).astype(BF16)
        stream = stream + lax.dot_general(
            trunk_out[layer], squeezed, (((0,), (0,)), ((), ())), preferred_element_type=F32
        )
    projected = dot(pair_weight[...], jax.nn.relu(stream).astype(BF16))

    right = []
    left = []
    for window, b, size in parts:
        begin = STRIDE * b + tower_row - margin
        turn = jnp.where(begin > 0, BINS - begin, -begin)
        terms = projected[:, window * BINS : (window + 1) * BINS]
        turned = pltpu.roll(terms, turn, 1)
        left.append(turned[:channels, :LANES])
        own = turned[channels:]
        if size > BINS:
            own = jnp.concatenate([own, own[:, : size - BINS]], axis=1)
        right.append(own[:, :size])
    used = sum(part[2] for part in parts)
    if lanes > used:
        right.append(jnp.zeros((channels, lanes - used), F32))
    right = jnp.concatenate(right, axis=1)
    rate = jnp.concatenate([rate_ref[...]] * (lanes // LANES), axis=1)
    lane = lax.broadcasted_iota(jnp.int32, (1, lanes), 1)

    def place_taps(ref, slot, act):
        act = act.astype(BF16)
        ref[pl.ds(slot * depth, channels), :] = pltpu.roll(act, 1, 1)
        ref[pl.ds(slot * depth + channels, channels), :] = act
        ref[pl.ds(slot * depth + 2 * channels, channels), :] = pltpu.roll(act, lanes - 1, 1)

    for row in range(height + 2 * margin):
        tiles = []
        for tile in range(lanes // LANES):
            piece = None
            here = lane[:, tile * LANES : (tile + 1) * LANES]
            for b in range(len(parts)):
                low, high = offsets[b], offsets[b] + parts[b][2]
                if high <= tile * LANES or low >= (tile + 1) * LANES:
                    continue
                spread = jnp.broadcast_to(left[b][:, row : row + 1], (channels, LANES))
                piece = spread if piece is None else jnp.where(here >= low, spread, piece)
            tiles.append(piece)
        mixed = jnp.concatenate(tiles, axis=1) + right - rate * decay_ref[pl.ds(row, 1), :]
        place_taps(taps_a, row, jnp.maximum(mixed, 0.0) * inside_ref[pl.ds(row, 1), :])

    def tower_block(kernels, mixes, taps, rows):
        for group, first in enumerate(range(0, rows, groups)):
            span = min(groups, rows - first)
            conv = dot(kernels[span][...], taps[pl.ds(first * depth, (span + 2) * depth), :])
            squeezed_ref[pl.ds(0, span * channels), pl.ds(group * lanes, lanes)] = jnp.maximum(
                conv, 0.0
            ).astype(BF16)
        full, left_over = rows // groups, rows % groups
        wide = dot(mixes[groups][...], squeezed_ref[:, pl.ds(0, full * lanes)])
        added = [
            wide[(row % groups) * channels :][:channels, (row // groups) * lanes :][:, :lanes]
            for row in range(full * groups)
        ]
        if left_over:
            rest = squeezed_ref[pl.ds(0, left_over * channels), pl.ds(full * lanes, lanes)]
            last = dot(mixes[left_over][...], rest)
            added += [last[r * channels : (r + 1) * channels] for r in range(left_over)]
        return added

    for row, added in enumerate(tower_block(conv_a, mix_a, taps_a, height + 2)):
        kept = taps_a[pl.ds((row + 1) * depth + channels, channels), :].astype(F32)
        grid = kept + added
        if 1 <= row <= height:
            grid_ref[pl.ds((row - 1) * channels, channels), :] = grid
        place_taps(taps_b, row, jnp.maximum(grid, 0.0) * inside_ref[pl.ds(row + 1, 1), :])
    for row, added in enumerate(tower_block(conv_b, mix_b, taps_b, height)):
        rows = pl.ds(row * channels, channels)
        final_ref[rows, :] = jnp.maximum(grid_ref[rows, :] + added, 0.0).astype(BF16)
    targets = head_ref.shape[0] // height
    contact = dot(head_ref[...], final_ref[...]).reshape(targets, height, lanes)

    wide = 2 * STRIDE
    stitched, before = [], []
    map_row = lax.broadcasted_iota(jnp.int32, (height, lanes), 0)
    for t in range(targets):
        skewed = contact[t]
        for bit in range((height - 1).bit_length()):
            turned = pltpu.roll(skewed, lanes - (1 << bit), 1)
            skewed = jnp.where((map_row >> bit) & 1 == 1, turned, skewed)
        for back, width, bands in ((0, BINS, stitched), (1, wide, before)):
            band = None
            for b in range(BLOCKS):
                k = back * BLOCKS + b
                first, reach = offsets[k] + margin, min(width, BINS - STRIDE * b)
                piece = skewed[:, first : first + reach]
                if reach < width:
                    piece = jnp.concatenate(
                        [piece, jnp.zeros((height, width - reach), F32)], axis=1
                    )
                piece = piece * stitch_ref[k][:, :width]
                band = piece if band is None else band + piece
            bands.append(band)
        stitched_ref[t] = stitched[t]

    near = jnp.concatenate([band[:, :wide] for band in stitched] + before, axis=0)
    col = lax.broadcasted_iota(jnp.int32, (wide, wide), 0)
    corner = lax.broadcasted_iota(jnp.int32, (wide, wide), 1)
    box = ((col > corner) & (col <= corner + STRIDE) & (corner < STRIDE)).astype(F32)
    square = jnp.dot(near, box, preferred_element_type=F32, precision=lax.Precision.HIGHEST)
    at = lax.broadcasted_iota(jnp.int32, near.shape, 1)
    contact = jnp.where((at >= 1) & (at <= STRIDE), jnp.exp(near), 0.0)
    down = jnp.sum(contact, axis=1, keepdims=True)
    here = lax.broadcasted_iota(jnp.int32, (height, wide), 0)
    there = lax.broadcasted_iota(jnp.int32, (height, wide), 1)

    def by_row(values, back):
        rows = []
        for t in range(back * targets, (back + 1) * targets):
            own = pltpu.roll(
                values[t * height : (t + 1) * height], 0, 1, stride=1, stride_axis=0
            )
            rows.append(jnp.sum(own, axis=0, keepdims=True))
        return rows

    down_rows = []
    for t in range(targets):
        own = jnp.where(here == there, down[t * height : (t + 1) * height], 0.0)
        down_rows.append(jnp.sum(own, axis=0, keepdims=True))
    rows = by_row(square, 0) + by_row(contact, 0)
    rows_before = by_row(square, 1) + by_row(contact, 1)
    keep_ref[...] = jnp.concatenate(rows + down_rows, axis=0)
    per_row = LANES // height
    first = lax.broadcasted_iota(jnp.int32, (per_row, LANES), 1) < height
    def packs_of(rows):
        return [
            jnp.concatenate(
                rows[p : p + per_row]
                + [jnp.zeros((1, LANES), F32)] * (per_row - len(rows[p : p + per_row])),
                axis=0,
            )
            for p in range(0, len(rows), per_row)
        ]

    packs = list(zip(packs_of(rows), packs_of(rows_before)))
    for k in range(1, STRIDE // height + 1):
        same = place_ref[0] + k < STRIDE // height
        packed = []
        for own, previous in packs:
            turned = pltpu.roll(jnp.where(same, own, previous), LANES - k * height, 1)
            turned = pltpu.roll(
                jnp.where(first, turned, 0.0), 0, 1, stride=height, stride_axis=0
            )
            packed.append(jnp.sum(turned, axis=0, keepdims=True))
        send_ref[lax.rem(place_ref[0] + k, STRIDE // height)] = jnp.concatenate(packed, axis=0)


def finish_kernel(height, place_ref, keep_ref, got_ref, out_ref):
    targets = out_ref.shape[0]
    per_row = LANES // height
    keep = keep_ref[...][:, :height]
    got = got_ref[place_ref[0]]
    rows = []
    for q in range(2 * targets):
        at = (q % per_row) * height
        rows.append(got[q // per_row : q // per_row + 1, at : at + height])
    sums = keep[: 2 * targets] + jnp.concatenate(rows, axis=0)
    upstream = sums[targets:]
    downstream = keep[2 * targets :]
    insulation = sums[:targets] / (STRIDE * STRIDE)
    direction = (downstream - upstream) / (downstream + upstream)
    for t in range(targets):
        out_ref[t] = jnp.concatenate([insulation[t : t + 1], direction[t : t + 1]], axis=0)


def per_device(
    genome_bases,
    stitch_weight,
    stem_weight,
    trunk_in,
    trunk_out,
    pair_weight,
    distance_rate,
    tower_conv,
    tower_mix,
    head_weight,
):
    towers = lax.axis_size("tower")
    height = STRIDE // towers
    tower_index = lax.axis_index("tower")
    genome_index = lax.axis_index("genome")
    own = stem(genome_bases, stem_weight, lax.axis_size("genome"))
    features = lax.all_to_all(own, "genome", 0, 0, tiled=True)
    groups = 3
    channels = distance_rate.shape[0]
    targets = head_weight.shape[0]
    place = jnp.stack([tower_index, genome_index]).astype(jnp.int32)
    lanes = segments(2, height)[2]
    packs = -(-2 * targets * height // LANES)
    vmem = pl.BlockSpec(memory_space=pltpu.VMEM)
    smem = pl.BlockSpec(memory_space=pltpu.SMEM)
    layers, mid, width = trunk_in.shape
    rows = height + 4
    shapes = [
        jax.ShapeDtypeStruct((layers, 3 * mid, width // 3), BF16),
        jax.ShapeDtypeStruct((channels, LANES), F32),
        jax.ShapeDtypeStruct((rows, lanes), F32),
        jax.ShapeDtypeStruct((rows, lanes), F32),
        jax.ShapeDtypeStruct((targets * height, height * channels), BF16),
        jax.ShapeDtypeStruct((2 * BLOCKS, height, BINS), F32),
    ]
    for count in (height + 2, height):
        for span in spans_of(count, groups):
            tall = span * channels
            shapes.append(jax.ShapeDtypeStruct((tall, (span + 2) * 3 * channels), BF16))
            shapes.append(jax.ShapeDtypeStruct((tall, tall), BF16))
    prepared = pl.pallas_call(
        functools.partial(prepare_kernel, height, groups),
        out_shape=shapes,
        in_specs=[smem, pl.BlockSpec(memory_space=pltpu.HBM)] + [vmem] * 6,
        out_specs=[vmem] * len(shapes),
        compiler_params=pltpu.CompilerParams(vmem_limit_bytes=8 * 1024 * 1024),
        cost_estimate=pl.CostEstimate(flops=10**9, bytes_accessed=1 << 22, transcendentals=0),
        name="prepare",
    )(
        place,
        own,
        trunk_in,
        distance_rate.reshape(1, channels),
        tower_conv,
        tower_mix,
        head_weight,
        stitch_weight.reshape(1, BINS),
    )
    stitched, keep, send = pl.pallas_call(
        functools.partial(main_kernel, height, groups),
        out_shape=[
            jax.ShapeDtypeStruct((targets, height, BINS), F32),
            jax.ShapeDtypeStruct((3 * targets, LANES), F32),
            jax.ShapeDtypeStruct((towers, packs, LANES), F32),
        ],
        in_specs=[smem] + [vmem] * (3 + len(shapes)),
        out_specs=[vmem] * 3,
        scratch_shapes=[
            pltpu.VMEM((rows * 3 * channels, lanes), BF16),
            pltpu.VMEM(((height + 2) * 3 * channels, lanes), BF16),
            pltpu.VMEM((height * channels, lanes), F32),
            pltpu.VMEM((height * channels, lanes), BF16),
            pltpu.VMEM((groups * channels, -(-(height + 2) // groups) * lanes), BF16),
        ],
        compiler_params=pltpu.CompilerParams(vmem_limit_bytes=VMEM_BYTES),
        name="windows",
    )(place, features, jnp.transpose(trunk_out, (0, 2, 1)), pair_weight, *prepared)
    got = lax.psum(send, "tower")
    scores = pl.pallas_call(
        functools.partial(finish_kernel, height),
        out_shape=jax.ShapeDtypeStruct((targets, 2, height), F32),
        in_specs=[smem, vmem, vmem],
        out_specs=vmem,
        compiler_params=pltpu.CompilerParams(vmem_limit_bytes=2 * 1024 * 1024),
        name="finish",
    )(place, keep, got)
    return (stitched, jnp.transpose(scores, (1, 0, 2)))


def solution(mesh):
    placed = (P("genome"), P(), P(), P(), P(), P(), P(), P(), P(), P())
    return jax.shard_map(
        per_device,
        mesh=mesh,
        in_specs=placed,
        out_specs=(P(None, ("genome", "tower"), None), P(None, None, ("genome", "tower"))),
        check_vma=False,
    )
```
